32 devices in a mesh: group: 2 (over x), reader: 16 (over z, y, core).
Axes of the slice: x: 2, y: 2, z: 4, core: 2. Of those that a mesh axis runs over, the one named last changes fastest.
Arguments:
- answer_lengths: int32 [64], P('group'), parts along dimension 0, may hold values from 1 to 256, 4096 in all
- mixer_input: bfloat16 [8192, 4096], P(('group', 'reader')), parts along dimension 0, may hold values from -6 to 6
- gate_input: bfloat16 [8192, 4096], P(('group', 'reader')), parts along dimension 0, may hold values from -6 to 6
- state_write: bfloat16 [8192, 512], P(('group', 'reader')), parts along dimension 0, may hold values from -6 to 6
- state_read: bfloat16 [8192, 512], P(('group', 'reader')), parts along dimension 0, may hold values from -0.5 to 0.5
- step_raw: float32 [8192, 64], P(('group', 'reader')), parts along dimension 0, may hold values from -4 to 50
- decay_rate: float32 [64], replicated, may hold values from 0.006 to 0.15
- skip_gain: float32 [64], replicated, may hold values from 0.5 to 2
- norm_gain: float32 [4096], replicated, may hold values from 0.1 to 1.9
- prompt_state: float32 [8192, 128], P(('group', 'reader')), parts along dimension 0, may hold values from -24 to 24
- queries: bfloat16 [8192, 2048], P(('group', 'reader')), parts along dimension 0, may hold values from -160 to 160
- answer_keys: bfloat16 [8192, 512], P(('group', 'reader')), parts along dimension 0, may hold values from -6 to 6
- answer_values: bfloat16 [8192, 512], P(('group', 'reader')), parts along dimension 0, may hold values from -48 to 48
- prompt_keys: bfloat16 [256, 512], P(('group', 'reader')), parts along dimension 0, may hold values from -4 to 4
- prompt_values: bfloat16 [256, 512], P(('group', 'reader')), parts along dimension 0, may hold values from -48 to 48
Outputs:
- mixer_out: bfloat16 [8192, 4096], P(('group', 'reader')), parts along dimension 0
- attention_out: bfloat16 [8192, 2048], P(('group', 'reader')), parts along dimension 0
The draws below stay inside these ranges and needn't reach their ends.
There are 2 independent parts, one for each index of `group`. The reference program is written for one: setup_inputs(seed, part) draws one part's arguments, and reference() takes and returns one part's arrays. A program takes and returns all parts, laid end to end along the dimension named above; an argument that names none is the same for every part. Nothing has to cross between parts.
Inputs may be any that keep to these rules, and one draw needn't show every extreme that they name: `answer_lengths`: the answers fill the 4096 tokens in order, back to back; the longest has exactly 256 tokens.
All inputs are finite; a program needn't handle non-finite values.
Results may differ from the reference program's by a relative error of at most 0.0047.
Values may be sent and summed in bfloat16 or wider, within the bound.
No kernel may reach another device: no remote copies, remote signals or barrier semaphores. Data moves between devices by JAX's collectives and lax.ppermute only.
A program may use at most 128 MiB of HBM per device.

```python
import math
import jax
import jax.numpy as jnp
import numpy as np
from jax import lax

H = 64
P_SIZE = 64
N = 128
G = 4
QH = 16
KVH = 4
HD = 128
SPAN = 64
TOK_DEV = 256
PACKED_TOKENS = 4096
PROMPT = 128
ANSWERS = 32


def draw_step_raw(key, part):
    root_random_key, spike_random_key, level_random_key = jax.random.split(jax.random.fold_in(key, 1), 3)
    root_value_entry = jnp.clip(-1.2 + 0.5 * jax.random.normal(root_random_key, (PACKED_TOKENS, H), jnp.float32), -3.5, 0.5)
    spike_mask_rows = jax.random.bernoulli(spike_random_key, 1.0 / 256.0, (PACKED_TOKENS, 1))
    spike_level_value = jax.random.uniform(level_random_key, (PACKED_TOKENS, 1), jnp.float32, 30.0, 50.0)
    return jnp.where(spike_mask_rows, spike_level_value, root_value_entry).astype(jnp.float32)


def draw_decay_rate(key, part):
    spread_key = jax.random.fold_in(jax.random.fold_in(key, 2), 0)
    fraction = jax.random.uniform(spread_key, (H,), jnp.float32)
    return jnp.exp(math.log(0.006) + fraction * math.log(0.15 / 0.006)).astype(jnp.float32)


def prompt_table(key):
    return jnp.clip(jax.random.normal(jax.random.fold_in(key, 3), (PROMPT, KVH, HD), jnp.float32), -4.0, 4.0)


def draw_prompt_keys(key, part):
    key_table = prompt_table(key)
    return key_table.reshape(PROMPT, KVH * HD).astype(jnp.bfloat16)


def draw_queries(key, part):
    query_table = jnp.clip(jax.random.normal(jax.random.fold_in(key, 5), (PACKED_TOKENS, QH, HD), jnp.float32), -4.0, 4.0)
    return query_table.reshape(PACKED_TOKENS, QH * HD).astype(jnp.bfloat16)


def steps_of(rng, shape, cuts, least, high):
    def one(axis_at, parts):
        draws = jax.random.uniform(jax.random.fold_in(jax.random.fold_in(rng, 6), axis_at), (parts,), jnp.float32, least / len(cuts), high / len(cuts))
        return jnp.repeat(jnp.exp(draws), shape[axis_at] // parts).reshape((-1,) + (1,) * (len(shape) - axis_at - 1))

    level = one(*cuts[0])
    for cut in cuts[1:]:
        level = level * one(*cut)
    return level


def split_up(amount, total, limit, lean):
    loads = [(1 << 20) // math.isqrt(standing ** lean) + 1 for standing in range(2, amount + 1)]
    surplus, given = total - limit - (amount - 1), [1] * (amount - 1)
    while surplus > 0:
        movable = [i for i in range(amount - 1) if given[i] < limit]
        pool, left = sum([loads[i] for i in movable]), surplus
        for i in movable:
            extra = min(limit - given[i], max(1, left * loads[i] // pool), surplus)
            given[i] = given[i] + extra
            surplus = surplus - extra
    return np.array([limit] + given)


def ragged(rng, amount, total, most, lean):
    if amount == 2:
        one = jax.random.randint(rng, (), max(1, total - most), min(most, total - 1) + 1)
        return jnp.stack([one, total - one])
    sizes = jnp.asarray(split_up(amount, total, most, lean), jnp.int32)
    pairs = (amount - 1) // 2
    source_of, sink = sizes[1:1 + 2 * pairs:2], sizes[2:2 + 2 * pairs:2]
    slack = jnp.minimum(source_of - 1, most - sink)
    moved = jax.random.randint(jax.random.fold_in(rng, 1), (pairs,), 0, 1 << 20) % (slack + 1)
    sizes = sizes.at[1:1 + 2 * pairs:2].set(source_of - moved).at[2:2 + 2 * pairs:2].set(sink + moved)
    return sizes[jax.random.permutation(jax.random.fold_in(rng, 2), amount)]


def centred(stream_key, dims, scale, bound, shards=(), held_as=jnp.bfloat16):
    array = scale * jax.random.normal(stream_key, dims, jnp.float32)
    if shards:
        array = array * steps_of(stream_key, dims, shards, -0.22, 0.18)
    return jnp.clip(array, -bound, bound).astype(held_as)


def setup_inputs(seed: int = 0, part: int = 0) -> dict:
    streams_of = jax.random.split(jax.random.key(seed), 16)
    own_keys = jax.random.split(jax.random.fold_in(streams_of[15], part), 16)
    answer_lengths = ragged(own_keys[0], ANSWERS, PACKED_TOKENS, TOK_DEV, 1).astype(jnp.int32)
    mixer_input = centred(own_keys[1], (PACKED_TOKENS, H * P_SIZE), 1.0, 6.0, ((0, 16),))
    gate_input = centred(own_keys[2], (PACKED_TOKENS, H * P_SIZE), 1.0, 6.0, ((0, 16),))
    state_write = centred(own_keys[3], (PACKED_TOKENS, G * N), 1.0, 6.0, ((0, 16),))
    state_read = centred(own_keys[4], (PACKED_TOKENS, G * N), N ** -0.5, 0.5, ((0, 16),))
    step_raw = draw_step_raw(jax.random.fold_in(jax.random.fold_in(streams_of[15], part), 71), part)
    decay_rate = draw_decay_rate(jax.random.fold_in(streams_of[15], 71), part)
    skip_gain = jnp.clip(jax.random.uniform(streams_of[7], (H,), jnp.float32, 0.5, 2.0), 0.5, 2.0)
    norm_gain = jnp.clip(1.0 + 0.18 * jax.random.normal(streams_of[8], (H * P_SIZE,), jnp.float32), 0.1, 1.9)
    prompt_state = centred(own_keys[9], (H * P_SIZE, N), 4.0, 24.0, ((0, 16),), jnp.float32)
    queries = draw_queries(jax.random.fold_in(jax.random.fold_in(streams_of[15], part), 71), part)
    answer_keys = centred(own_keys[11], (PACKED_TOKENS, KVH * HD), 1.0, 6.0, ((0, 16),))
    answer_values = centred(own_keys[12], (PACKED_TOKENS, KVH * HD), 8.0, 48.0, ((0, 16),))
    prompt_keys = draw_prompt_keys(jax.random.fold_in(jax.random.fold_in(streams_of[15], part), 71), part)
    prompt_values = centred(own_keys[14], (PROMPT, KVH * HD), 8.0, 48.0, ((0, 16),))
    return {"answer_lengths": answer_lengths, "mixer_input": mixer_input, "gate_input": gate_input, "state_write": state_write, "state_read": state_read, "step_raw": step_raw, "decay_rate": decay_rate, "skip_gain": skip_gain, "norm_gain": norm_gain, "prompt_state": prompt_state, "queries": queries, "answer_keys": answer_keys, "answer_values": answer_values, "prompt_keys": prompt_keys, "prompt_values": prompt_values}


def segments_at(answer_lengths, places):
    answer_ends = jnp.cumsum(answer_lengths).astype(jnp.int32)
    answer_starts = (answer_ends - answer_lengths).astype(jnp.int32)
    segment = lax.optimization_barrier(jnp.sum((answer_ends[None, :] <= places[:, None]).astype(jnp.int32), axis=1)).astype(jnp.int32)
    numbers = jnp.arange(answer_lengths.shape[0], dtype=jnp.int32)
    start_of = lax.optimization_barrier(jnp.sum(jnp.where(segment[:, None] == numbers[None, :], answer_starts[None, :], 0), axis=1)).astype(jnp.int32)
    return (segment, (start_of == places).astype(jnp.int32))

def span_local(inputs_block, write_block, read_block, raw_block, segment, opening, decay_rate):
    length, groups, per_group, channels = inputs_block.shape
    step_size = jax.nn.softplus(raw_block)
    falling = -decay_rate[None, :] * step_size
    running = jnp.cumsum(falling, axis=0)
    before = running - falling
    places = jnp.arange(length, dtype=jnp.int32)
    same_answer = segment[:, None] == segment[None, :]
    leading = jnp.concatenate([jnp.ones((1,), dtype=bool), segment[1:] != segment[:-1]])
    entry_level = lax.optimization_barrier(jnp.sum(jnp.where((same_answer & leading[None, :])[:, :, None], before[None, :, :], 0.0), axis=1))
    decay_in = jnp.exp(running - entry_level)
    carried = same_answer[:, 0] & (opening[0] == 0)
    causal = same_answer & (places[None, :] <= places[:, None])
    spread = jnp.where(causal[:, :, None], running[:, None, :] - running[None, :, :], -jnp.inf)
    intersection = jnp.einsum('tgn,sgn->tsg', read_block.astype(jnp.float32), write_block.astype(jnp.float32))
    mixing = intersection[:, :, :, None] * jnp.exp(spread).reshape(length, length, groups, per_group) * step_size.reshape(1, length, groups, per_group)
    mixing = lax.optimization_barrier(mixing.astype(jnp.bfloat16)).astype(jnp.float32)
    inner_part = jnp.einsum('tsgk,sgkp->tgkp', mixing, inputs_block.astype(jnp.float32))
    closing = same_answer[length - 1].astype(jnp.float32)
    weight = jnp.exp(running[length - 1][None, :] - running) * step_size * closing[:, None]
    weighted = (inputs_block.astype(jnp.float32) * weight.reshape(length, groups, per_group, 1)).astype(jnp.bfloat16)
    weighted = lax.optimization_barrier(weighted).astype(jnp.float32)
    gathered_state = jnp.einsum('sgkp,sgn->gkpn', weighted, write_block.astype(jnp.float32))
    decay_end = jnp.exp(running[length - 1] - entry_level[length - 1]).reshape(groups, per_group)
    return (inner_part, decay_in, carried, gathered_state, decay_end, carried[length - 1])

def gated_norm(mixed_value, gate_input, norm_gain, groups):
    token_rows = mixed_value.shape[0]
    gated = mixed_value * jax.nn.silu(gate_input.astype(jnp.float32))
    grouped = gated.reshape(token_rows, groups, -1)
    mean_square = lax.optimization_barrier(jnp.mean(grouped * grouped, axis=2, keepdims=True))
    return (grouped * lax.rsqrt(mean_square + 1e-05)).reshape(token_rows, -1) * norm_gain[None, :]

def reference(answer_lengths, mixer_input, gate_input, state_write, state_read, step_raw, decay_rate, skip_gain, norm_gain, prompt_state, queries, answer_keys, answer_values, prompt_keys, prompt_values):
    per_group = H // G
    block_count = PACKED_TOKENS // SPAN
    places = jnp.arange(PACKED_TOKENS, dtype=jnp.int32)
    segment, opening = segments_at(answer_lengths, places)
    seed_state = prompt_state.reshape(G, per_group, P_SIZE, N)
    pieces = (mixer_input.reshape(block_count, SPAN, G, per_group, P_SIZE), state_write.reshape(block_count, SPAN, G, N), state_read.reshape(block_count, SPAN, G, N), step_raw.reshape(block_count, SPAN, H), segment.reshape(block_count, SPAN), opening.reshape(block_count, SPAN))

    def advance(carry_state, piece):
        inputs_block, write_block, read_block, raw_block, segment_block, opening_block = piece
        inner_part, decay_in, carried, gathered_state, decay_end, carried_last = span_local(inputs_block, write_block, read_block, raw_block, segment_block, opening_block, decay_rate)
        read_wide = read_block.astype(jnp.float32)
        from_prompt = jnp.einsum('tgn,gkpn->tgkp', read_wide, seed_state, precision=lax.Precision.HIGHEST)
        from_state = jnp.einsum('tgn,gkpn->tgkp', read_wide, carry_state, precision=lax.Precision.HIGHEST)
        inflow = jnp.where(carried[:, None, None, None], from_state, from_prompt) * decay_in.reshape(SPAN, G, per_group, 1)
        output = inner_part + inflow + skip_gain.reshape(1, G, per_group, 1) * inputs_block.astype(jnp.float32)
        entering = jnp.where(carried_last, carry_state, seed_state)
        return (decay_end[:, :, None, None] * entering + gathered_state, output)
    initial = jnp.zeros((G, per_group, P_SIZE, N), jnp.float32)
    final_state, outputs = lax.scan(advance, initial, pieces)
    mixer_out = gated_norm(outputs.reshape(PACKED_TOKENS, H * P_SIZE), gate_input, norm_gain, G).astype(jnp.bfloat16)
    group_size = QH // KVH
    score_scale = 1.0 / math.sqrt(HD)
    width = 512 + TOK_DEV
    cache_keys = prompt_keys.reshape(PROMPT, KVH, HD).astype(jnp.float32)
    cache_values = prompt_values.reshape(PROMPT, KVH, HD).astype(jnp.float32)

    def attend(block_index):
        row_start = (block_index * 512).astype(jnp.int32)
        key_start = jnp.maximum(row_start - TOK_DEV, 0).astype(jnp.int32)
        query_part = lax.dynamic_slice_in_dim(queries, row_start, 512, 0).reshape(512, KVH, group_size, HD).astype(jnp.float32)
        near_keys = lax.dynamic_slice_in_dim(answer_keys, key_start, width, 0).reshape(width, KVH, HD).astype(jnp.float32)
        near_values = lax.dynamic_slice_in_dim(answer_values, key_start, width, 0).reshape(width, KVH, HD).astype(jnp.float32)
        query_places = row_start + jnp.arange(512, dtype=jnp.int32)
        key_places = key_start + jnp.arange(width, dtype=jnp.int32)
        query_segment = lax.dynamic_slice_in_dim(segment, row_start, 512, 0)
        key_segment = lax.dynamic_slice_in_dim(segment, key_start, width, 0)
        allowed = (query_segment[:, None] == key_segment[None, :]) & (key_places[None, :] <= query_places[:, None])
        cache_scores = jnp.einsum('tkqd,skd->tkqs', query_part, cache_keys) * score_scale
        near_scores = jnp.einsum('tkqd,skd->tkqs', query_part, near_keys) * score_scale
        near_scores = jnp.where(allowed[:, None, None, :], near_scores, -jnp.inf)
        row_top = jnp.maximum(lax.optimization_barrier(jnp.max(cache_scores, axis=3)), lax.optimization_barrier(jnp.max(near_scores, axis=3)))
        cache_weights = jnp.exp(cache_scores - row_top[:, :, :, None])
        near_weights = jnp.exp(near_scores - row_top[:, :, :, None])
        weight_total = lax.optimization_barrier(jnp.sum(cache_weights, axis=3)) + lax.optimization_barrier(jnp.sum(near_weights, axis=3))
        cache_rounded = lax.optimization_barrier(cache_weights.astype(jnp.bfloat16)).astype(jnp.float32)
        near_rounded = lax.optimization_barrier(near_weights.astype(jnp.bfloat16)).astype(jnp.float32)
        summed = jnp.einsum('tkqs,skd->tkqd', cache_rounded, cache_values) + jnp.einsum('tkqs,skd->tkqd', near_rounded, near_values)
        return (summed / weight_total[:, :, :, None]).astype(jnp.bfloat16).reshape(512, QH * HD)
    attention_out = lax.map(attend, jnp.arange(PACKED_TOKENS // 512, dtype=jnp.int32)).reshape(PACKED_TOKENS, QH * HD)
    return (mixer_out, attention_out)
```

```python
import functools
import math

import jax
import jax.numpy as jnp
from jax import lax
from jax.experimental import pallas as pl
from jax.experimental.pallas import tpu as pltpu
from jax.sharding import PartitionSpec as P

HD = 128
LANES = 128
LOG2E = 1.4426950408889634
F32 = jnp.float32
BF16 = jnp.bfloat16
MIB = 1 << 20


def iota(shape, dim):
    return lax.broadcasted_iota(jnp.int32, shape, dim)


def dot(a, b, ca=1, cb=0):
    return lax.dot_general(a, b, (((ca,), (cb,)), ((), ())), preferred_element_type=F32)


def expander(heads, group, per_group, channels):
    shape = (2 * heads, per_group * channels)
    row = iota(shape, 0)
    head = jnp.where(row >= heads, row - heads, row) - group * per_group
    column = iota(shape, 1)
    first = head * channels
    return jnp.where((column >= first) & (column < first + channels), 1.0, 0.0).astype(BF16)


def two_parts(value, heads):
    high = value.astype(BF16).astype(F32)
    return jnp.where(iota(value.shape, 1) < heads, high, value - high).astype(BF16)


def pack_kernel(state_ref, keys_ref, values_ref, near_keys_ref, near_values_ref, out_ref, near_ref):
    rows = state_ref.shape[0]
    out_ref[:rows, :] = state_ref[...].astype(BF16)
    parts = []
    for ref in (keys_ref, values_ref):
        wide = ref[...].astype(F32)
        for head in range(wide.shape[1] // HD):
            parts.append(wide[:, head * HD : (head + 1) * HD])
    out_ref[rows:, :] = jnp.concatenate(parts, axis=0).astype(BF16)
    width = near_keys_ref.shape[1]
    near_ref[:, :width] = near_keys_ref[...]
    near_ref[:, width:] = near_values_ref[...]


def tail_kernel(
    base_ref,
    lengths_ref,
    raw_ref,
    rate_ref,
    x_ref,
    write_ref,
    tail_ref,
    level_ref,
    column_ref,
    start_ref,
    weight_ref,
    *,
    heads,
    per_group,
    channels,
):
    group = pl.program_id(0)
    tokens = x_ref.shape[0]
    columns = heads * channels

    @pl.when(group == 0)
    def _():
        base = base_ref[0, 0].astype(F32)
        lengths = lengths_ref[...].astype(F32)
        answers = lengths.shape[1]
        square = (answers, answers)
        ends = jnp.sum(
            jnp.where(iota(square, 1) <= iota(square, 0), lengths, 0.0), axis=1, keepdims=True
        )
        place = base + iota((1, tokens), 1).astype(F32)
        start = jnp.max(jnp.where(ends <= place, ends, 0.0), axis=0, keepdims=True) - base
        start = jnp.broadcast_to(start, (LANES, tokens)).T
        start_ref[...] = start
        wide = jnp.concatenate([start] * (tokens // LANES), axis=1)
        square = (tokens, tokens)
        source = iota(square, 1)
        mask = (source.astype(F32) >= wide) & (source <= iota(square, 0))
        mask = jnp.where(mask, 1.0, 0.0).astype(BF16)
        raw = jnp.concatenate([raw_ref[...]] * 2, axis=1)
        rate = jnp.concatenate([rate_ref[...]] * 2, axis=1)
        step = jnp.maximum(raw, 0.0) + jnp.log1p(jnp.exp(-jnp.abs(raw)))
        falling = -rate * step
        first = falling.astype(BF16)
        rest = falling - first.astype(F32)
        second = rest.astype(BF16)
        third = (rest - second.astype(F32)).astype(BF16)
        level = dot(mask, first) + (dot(mask, second) + dot(mask, third))
        level_ref[...] = level
        column = level * LOG2E - jnp.log(step) * LOG2E
        column_ref[...] = column.T[:heads, :]
        last = level[tokens - 1 :, :]
        own = iota((tokens, 2 * heads), 0).astype(F32) >= start[tokens - 1 :, : 2 * heads]
        weight = jnp.where(own, jnp.exp(last - level) * step, 0.0)
        weight_ref[...] = two_parts(weight, heads)
        decay = jnp.exp(jnp.broadcast_to(last, (16, 2 * heads)))
        high = decay.astype(BF16).astype(F32)
        row = iota(decay.shape, 0)
        decay = jnp.where(row == 0, high, jnp.where(row == 1, decay - high, 0.0))
        tail_ref[:, columns:] = jnp.zeros((tail_ref.shape[0], 2 * heads), BF16)
        tail_ref[:16, columns:] = decay.astype(BF16)

    spread = expander(heads, group, per_group, channels)
    weight = dot(weight_ref[...], spread)
    weighted = (x_ref[...].astype(F32) * weight).astype(BF16)
    width = per_group * channels
    tail_ref[:, pl.ds(pl.multiple_of(group * width, width), width)] = dot(
        write_ref[...], weighted, 0, 0
    ).astype(BF16)


def inner_kernel(
    start_ref,
    level_ref,
    column_ref,
    skip_ref,
    x_ref,
    write_ref,
    read_ref,
    out_ref,
    *,
    heads,
    per_group,
    channels,
):
    group = pl.program_id(0)
    tokens = x_ref.shape[0]
    both = dot(read_ref[...], write_ref[...], 1, 1)
    square = (tokens, tokens)
    source = iota(square, 1)
    wide = jnp.concatenate([start_ref[...]] * (tokens // LANES), axis=1)
    both = jnp.where((source.astype(F32) >= wide) & (source <= iota(square, 0)), both, 0.0)
    lanes = level_ref.shape[1]
    level = pltpu.roll(level_ref[...] * LOG2E, lanes - group * per_group, 1)
    skip = jnp.concatenate([skip_ref[...]] * 2, axis=1)
    skip = two_parts(jnp.broadcast_to(skip, (16, 2 * heads)), heads)
    skip = dot(skip, expander(heads, group, per_group, channels))[:1, :]
    per_tile = LANES // channels
    lane = iota((LANES, LANES), 1)
    for tile in range(per_group // per_tile):
        at = slice(tile * LANES, (tile + 1) * LANES)
        x = x_ref[:, at]
        for block in range(tokens // LANES):
            rows = slice(block * LANES, (block + 1) * LANES)
            reach = (block + 1) * LANES
            total = None
            for part in range(per_tile):
                head = tile * per_tile + part
                gap = level[rows, head : head + 1] - column_ref[head : head + 1, :reach]
                mixing = (jnp.exp2(jnp.minimum(gap, 64.0)) * both[rows, :reach]).astype(BF16)
                result = dot(mixing, x[:reach, :])
                total = result if total is None else jnp.where(
                    lane < part * channels, total, result
                )
            total = total + skip[:, at] * x[rows, :].astype(F32)
            out_ref[rows, at] = total.astype(BF16)


def attend_kernel(
    start_ref,
    query_ref,
    key_ref,
    value_ref,
    prior_key_ref,
    prior_value_ref,
    gathered_ref,
    out_ref,
    bias_ref,
    *,
    state_rows,
    prompt_rows,
    kv_count,
):
    head = pl.program_id(0)
    tokens = query_ref.shape[0]
    devices = gathered_ref.shape[0]
    scale = LOG2E / math.sqrt(HD)

    @pl.when(head == 0)
    def _():
        shape = (tokens, 2 * tokens)
        place = iota(shape, 1) - tokens
        wide = jnp.concatenate([start_ref[...]] * (2 * tokens // LANES), axis=1)
        allowed = (place.astype(F32) >= wide) & (place <= iota(shape, 0))
        bias_ref[...] = jnp.where(allowed, 0.0, -jnp.inf)

    def prompt(which):
        at = pl.multiple_of(state_rows + (which * kv_count + head) // 2 * 2 * prompt_rows, 16)
        pair = gathered_ref[:, pl.ds(at, 2 * prompt_rows), :].astype(F32)
        odd = lax.rem(head, 2) == 1
        part = jnp.where(odd, pair[:, prompt_rows:, :], pair[:, :prompt_rows, :])
        return part.reshape(devices * prompt_rows, HD).astype(BF16)

    prompt_keys = prompt(0)
    ones = jnp.ones((tokens, LANES), BF16)
    prompt_values = prompt(1)
    prompt_values = jnp.concatenate(
        [prompt_values, jnp.ones((prompt_values.shape[0], LANES), BF16)], axis=1
    )
    near_keys = jnp.concatenate([prior_key_ref[...], key_ref[...]], axis=0)
    near_values = jnp.concatenate(
        [
            jnp.concatenate([prior_value_ref[...], ones], axis=1),
            jnp.concatenate([value_ref[...], ones], axis=1),
        ],
        axis=0,
    )
    for query in range(query_ref.shape[1] // HD):
        at = slice(query * HD, (query + 1) * HD)
        for block in range(tokens // LANES):
            rows = slice(block * LANES, (block + 1) * LANES)
            reach = tokens + (block + 1) * LANES
            q = query_ref[rows, at]
            far = dot(q, prompt_keys, 1, 1)
            near = dot(q, near_keys[:reach, :], 1, 1) + bias_ref[rows, :reach]
            top = jnp.maximum(
                jnp.max(far, axis=1, keepdims=True), jnp.max(near, axis=1, keepdims=True)
            )
            far = jnp.exp2((far - top) * scale).astype(BF16)
            near = jnp.exp2((near - top) * scale).astype(BF16)
            summed = dot(far, prompt_values) + dot(near, near_values[:reach, :])
            out_ref[rows, at] = (summed[:, :HD] / summed[:, HD:]).astype(BF16)


def final_kernel(
    start_ref,
    level_ref,
    tail_ref,
    decay_ref,
    gathered_ref,
    read_ref,
    inner_ref,
    gate_ref,
    gain_ref,
    out_ref,
    *,
    state_rows,
    heads,
    per_group,
    channels,
):
    group = pl.program_id(0)
    tokens = read_ref.shape[0]
    level = jnp.exp(level_ref[...])
    carried = start_ref[:, : 2 * heads] < 0
    decay = decay_ref[...].astype(F32)
    decay = decay[0:1, :] + decay[1:2, :]
    spread = expander(heads, group, per_group, channels)
    from_prompt = dot(two_parts(jnp.where(carried, level * decay, level), heads), spread)
    from_prior = dot(two_parts(jnp.where(carried, level, 0.0), heads), spread)
    seeds = gathered_ref[:, :state_rows, :]
    seeds = seeds.reshape(seeds.shape[0] * state_rows, seeds.shape[2])
    read = read_ref[...]
    mixed = inner_ref[...].astype(F32)
    mixed = mixed + from_prompt * dot(read, seeds, 1, 1)
    mixed = mixed + from_prior * dot(read, tail_ref[...])
    gate = gate_ref[...].astype(F32)
    gated = mixed * (gate * (0.5 + 0.5 * jnp.tanh(0.5 * gate)))
    scale = lax.rsqrt(jnp.mean(gated * gated, axis=1, keepdims=True) + 1e-05)
    out_ref[...] = (gated * scale * gain_ref[...]).astype(BF16)


def shifted(value, axis, by):
    length = lax.axis_size(axis)
    return lax.ppermute(value, axis, [(i, i + by) for i in range(length - by)])


def params(limit=40):
    return pltpu.CompilerParams(vmem_limit_bytes=limit * MIB)


def whole(shape):
    return pl.BlockSpec(shape, lambda g: (0,) * len(shape))


def local(
    answer_lengths,
    mixer_input,
    gate_input,
    state_write,
    state_read,
    step_raw,
    decay_rate,
    skip_gain,
    norm_gain,
    prompt_state,
    queries,
    answer_keys,
    answer_values,
    prompt_keys,
    prompt_values,
):
    tokens, columns = mixer_input.shape
    heads = decay_rate.shape[0]
    state_rows, state = prompt_state.shape
    groups = state_write.shape[1] // state
    per_group = heads // groups
    channels = columns // heads
    width = per_group * channels
    prompt_rows, kv_width = prompt_keys.shape
    kv_count = kv_width // HD
    devices = lax.axis_size("reader")
    base = (lax.axis_index("reader") * tokens).astype(jnp.int32).reshape(1, 1)
    lengths = answer_lengths.reshape(1, -1)
    sizes = dict(heads=heads, per_group=per_group, channels=channels)
    packed_rows = state_rows + 2 * prompt_rows * kv_count

    packed, near = pl.pallas_call(
        pack_kernel,
        out_shape=(
            jax.ShapeDtypeStruct((packed_rows, HD), BF16),
            jax.ShapeDtypeStruct((tokens, 2 * kv_width), BF16),
        ),
        compiler_params=params(16),
        name="pack",
    )(prompt_state, prompt_keys, prompt_values, answer_keys, answer_values)
    gathered = lax.all_gather(packed, "reader", axis=0, tiled=False)
    prior = shifted(near, "reader", 1)

    by_group = lambda rows: pl.BlockSpec((rows, state), lambda g: (0, g))
    wide = pl.BlockSpec((tokens, width), lambda g: (0, g))
    tail, level, column, start = pl.pallas_call(
        functools.partial(tail_kernel, **sizes),
        grid=(groups,),
        in_specs=[
            pl.BlockSpec(memory_space=pltpu.SMEM),
            whole(lengths.shape),
            whole(step_raw.shape),
            whole((1, heads)),
            wide,
            by_group(tokens),
        ],
        out_specs=(
            whole((state, columns + 2 * heads)),
            whole((tokens, 2 * heads)),
            whole((heads, tokens)),
            whole((tokens, LANES)),
        ),
        out_shape=(
            jax.ShapeDtypeStruct((state, columns + 2 * heads), BF16),
            jax.ShapeDtypeStruct((tokens, 2 * heads), F32),
            jax.ShapeDtypeStruct((heads, tokens), F32),
            jax.ShapeDtypeStruct((tokens, LANES), F32),
        ),
        scratch_shapes=[pltpu.VMEM((tokens, 2 * heads), BF16)],
        compiler_params=params(),
        name="tail",
    )(base, lengths, step_raw, decay_rate.reshape(1, -1), mixer_input, state_write)
    tail = shifted(tail, "reader", 1)

    inner = pl.pallas_call(
        functools.partial(inner_kernel, **sizes),
        grid=(groups,),
        in_specs=[
            whole((tokens, LANES)),
            whole((tokens, 2 * heads)),
            pl.BlockSpec((per_group, tokens), lambda g: (g, 0)),
            whole((1, heads)),
            wide,
            by_group(tokens),
            by_group(tokens),
        ],
        out_specs=wide,
        out_shape=jax.ShapeDtypeStruct((tokens, columns), BF16),
        compiler_params=params(),
        cost_estimate=pl.CostEstimate(
            flops=heads * tokens * tokens * channels * 8,
            bytes_accessed=tokens * columns * 4,
            transcendentals=heads * tokens * tokens,
        ),
        name="inner",
    )(start, level, column, skip_gain.reshape(1, -1), mixer_input, state_write, state_read)

    group_size = queries.shape[1] // kv_width
    attention_out = pl.pallas_call(
        functools.partial(
            attend_kernel, state_rows=state_rows, prompt_rows=prompt_rows, kv_count=kv_count
        ),
        grid=(kv_count,),
        in_specs=[
            whole((tokens, LANES)),
            pl.BlockSpec((tokens, group_size * HD), lambda k: (0, k)),
            pl.BlockSpec((tokens, HD), lambda k: (0, k)),
            pl.BlockSpec((tokens, HD), lambda k: (0, k)),
            pl.BlockSpec((tokens, HD), lambda k: (0, k)),
            pl.BlockSpec((tokens, HD), lambda k: (0, kv_count + k)),
            whole((devices, packed_rows, HD)),
        ],
        out_specs=pl.BlockSpec((tokens, group_size * HD), lambda k: (0, k)),
        out_shape=jax.ShapeDtypeStruct(queries.shape, BF16),
        scratch_shapes=[pltpu.VMEM((tokens, 2 * tokens), F32)],
        compiler_params=params(),
        name="attend",
    )(start, queries, answer_keys, answer_values, prior, prior, gathered)

    mixer_out = pl.pallas_call(
        functools.partial(final_kernel, state_rows=state_rows, **sizes),
        grid=(groups,),
        in_specs=[
            whole((tokens, LANES)),
            whole((tokens, 2 * heads)),
            pl.BlockSpec((state, width), lambda g: (0, g)),
            pl.BlockSpec((16, 2 * heads), lambda g: (0, columns // (2 * heads))),
            pl.BlockSpec((devices // groups, packed_rows, HD), lambda g: (g, 0, 0)),
            by_group(tokens),
            wide,
            wide,
            pl.BlockSpec((1, width), lambda g: (0, g)),
        ],
        out_specs=wide,
        out_shape=jax.ShapeDtypeStruct((tokens, columns), BF16),
        compiler_params=params(),
        name="final",
    )(start, level, tail, tail, gathered, state_read, inner, gate_input, norm_gain.reshape(1, -1))
    return (mixer_out, attention_out)


def solution(mesh):
    rows = P(("group", "reader"), None)
    in_specs = (P("group"),) + (rows,) * 5 + (P(),) * 3 + (rows,) * 6
    return jax.shard_map(
        local, mesh=mesh, in_specs=in_specs, out_specs=(rows, rows), check_vma=False
    )
```

```python
import functools
import math

import jax
import jax.numpy as jnp
from jax import lax
from jax.experimental import pallas as pl
from jax.experimental.pallas import tpu as pltpu
from jax.sharding import PartitionSpec as P

HD = 128
LANES = 128
LOG2E = 1.4426950408889634
F32 = jnp.float32
BF16 = jnp.bfloat16
MIB = 1 << 20


def iota(shape, dim):
    return lax.broadcasted_iota(jnp.int32, shape, dim)


def dot(a, b, ca=1, cb=0):
    return lax.dot_general(a, b, (((ca,), (cb,)), ((), ())), preferred_element_type=F32)


def expander(heads, group, per_group, channels):
    shape = (2 * heads, per_group * channels)
    row = iota(shape, 0)
    head = jnp.where(row >= heads, row - heads, row) - group * per_group
    column = iota(shape, 1)
    first = head * channels
    return jnp.where((column >= first) & (column < first + channels), 1.0, 0.0).astype(BF16)


def two_parts(value, heads):
    high = value.astype(BF16).astype(F32)
    return jnp.where(iota(value.shape, 1) < heads, high, value - high).astype(BF16)


def pack_kernel(state_ref, keys_ref, values_ref, out_ref):
    rows = state_ref.shape[0]
    out_ref[:rows, :] = state_ref[...].astype(BF16)
    parts = []
    for ref in (keys_ref, values_ref):
        wide = ref[...].astype(F32)
        for head in range(wide.shape[1] // HD):
            parts.append(wide[:, head * HD : (head + 1) * HD])
    out_ref[rows:, :] = jnp.concatenate(parts, axis=0).astype(BF16)


def tail_kernel(
    lengths_ref,
    raw_ref,
    rate_ref,
    x_ref,
    write_ref,
    keys_ref,
    values_ref,
    tail_ref,
    level_ref,
    column_ref,
    start_ref,
    weight_ref,
    *,
    heads,
    per_group,
    channels,
):
    group = pl.program_id(0)
    tokens = x_ref.shape[0]
    columns = heads * channels

    @pl.when(group == 0)
    def _():
        base = (lax.axis_index("reader") * tokens).astype(F32)
        lengths = lengths_ref[...].astype(F32)
        answers = lengths.shape[1]
        square = (answers, answers)
        ends = jnp.sum(
            jnp.where(iota(square, 1) <= iota(square, 0), lengths, 0.0), axis=1, keepdims=True
        )
        place = base + iota((1, tokens), 1).astype(F32)
        start = jnp.max(jnp.where(ends <= place, ends, 0.0), axis=0, keepdims=True) - base
        start = jnp.broadcast_to(start, (LANES, tokens)).T
        start_ref[...] = start
        wide = jnp.concatenate([start] * (tokens // LANES), axis=1)
        square = (tokens, tokens)
        source = iota(square, 1)
        mask = (source.astype(F32) >= wide) & (source <= iota(square, 0))
        mask = jnp.where(mask, 1.0, 0.0).astype(BF16)
        raw = raw_ref[...]
        rate = jnp.broadcast_to(rate_ref[...], (heads, heads))
        diagonal = iota((heads, heads), 0) == iota((heads, heads), 1)
        rate = jnp.sum(jnp.where(diagonal, rate, 0.0), axis=1, keepdims=True)
        step = jnp.maximum(raw, 0.0) + jnp.log1p(jnp.exp(-jnp.abs(raw)))
        falling = -rate * step
        first = falling.astype(BF16)
        rest = falling - first.astype(F32)
        second = rest.astype(BF16)
        third = (rest - second.astype(F32)).astype(BF16)
        level = dot(first, mask, 1, 1) + (dot(second, mask, 1, 1) + dot(third, mask, 1, 1))
        column_ref[...] = level * LOG2E - jnp.log(step) * LOG2E
        level = jnp.concatenate([level, level], axis=0).T
        step = jnp.concatenate([step, step], axis=0).T
        level_ref[...] = level
        last = level[tokens - 1 :, :]
        own = iota((tokens, 2 * heads), 0).astype(F32) >= start[tokens - 1 :, : 2 * heads]
        weight = jnp.where(own, jnp.exp(last - level) * step, 0.0)
        weight_ref[...] = two_parts(weight, heads)
        decay = jnp.exp(jnp.broadcast_to(last, (16, 2 * heads)))
        high = decay.astype(BF16).astype(F32)
        row = iota(decay.shape, 0)
        decay = jnp.where(row == 0, high, jnp.where(row == 1, decay - high, 0.0))
        at = columns + 2 * heads
        tail_ref[:, columns:at] = jnp.zeros((tail_ref.shape[0], 2 * heads), BF16)
        tail_ref[:16, columns:at] = decay.astype(BF16)
        depth, width = tail_ref.shape[0], keys_ref.shape[1]
        for ref in (keys_ref, values_ref):
            for half in range(tokens // depth):
                tail_ref[:, at : at + width] = ref[half * depth : (half + 1) * depth, :]
                at += width

    spread = expander(heads, group, per_group, channels)
    weight = dot(weight_ref[...], spread)
    weighted = (x_ref[...].astype(F32) * weight).astype(BF16)
    width = per_group * channels
    tail_ref[:, pl.ds(pl.multiple_of(group * width, width), width)] = dot(
        write_ref[...], weighted, 0, 0
    ).astype(BF16)


def inner_kernel(
    start_ref,
    level_ref,
    column_ref,
    skip_ref,
    x_ref,
    write_ref,
    read_ref,
    out_ref,
    *,
    heads,
    per_group,
    channels,
):
    group = pl.program_id(0)
    tokens = x_ref.shape[0]
    both = dot(read_ref[...], write_ref[...], 1, 1)
    square = (tokens, tokens)
    source = iota(square, 1)
    wide = jnp.concatenate([start_ref[...]] * (tokens // LANES), axis=1)
    both = jnp.where((source.astype(F32) >= wide) & (source <= iota(square, 0)), both, 0.0)
    lanes = level_ref.shape[1]
    level = pltpu.roll(level_ref[...] * LOG2E, lanes - group * per_group, 1)
    skip = jnp.concatenate([skip_ref[...]] * 2, axis=1)
    skip = two_parts(jnp.broadcast_to(skip, (16, 2 * heads)), heads)
    skip = dot(skip, expander(heads, group, per_group, channels))[:1, :]
    per_tile = LANES // channels
    lane = iota((LANES, LANES), 1)
    for tile in range(per_group // per_tile):
        at = slice(tile * LANES, (tile + 1) * LANES)
        x = x_ref[:, at]
        for block in range(tokens // LANES):
            rows = slice(block * LANES, (block + 1) * LANES)
            reach = (block + 1) * LANES
            total = None
            for part in range(per_tile):
                head = tile * per_tile + part
                gap = level[rows, head : head + 1] - column_ref[head : head + 1, :reach]
                mixing = (jnp.exp2(jnp.minimum(gap, 64.0)) * both[rows, :reach]).astype(BF16)
                result = dot(mixing, x[:reach, :])
                total = result if total is None else jnp.where(
                    lane < part * channels, total, result
                )
            total = total + skip[:, at] * x[rows, :].astype(F32)
            out_ref[rows, at] = total.astype(BF16)


def attend_kernel(
    start_ref,
    query_ref,
    key_ref,
    value_ref,
    mine_ref,
    other_ref,
    *rest,
    halves,
    state_rows,
    prompt_rows,
    kv_count,
):
    prior_refs, (out_ref, bias_ref) = rest[:-2], rest[-2:]
    head = pl.program_id(0)
    tokens = query_ref.shape[0]
    devices = 2 * mine_ref.shape[0]
    scale = LOG2E / math.sqrt(HD)

    @pl.when(head == 0)
    def _():
        shape = (tokens, 2 * tokens)
        place = iota(shape, 1) - tokens
        wide = jnp.concatenate([start_ref[...]] * (2 * tokens // LANES), axis=1)
        allowed = (place.astype(F32) >= wide) & (place <= iota(shape, 0))
        bias_ref[...] = jnp.where(allowed, 0.0, -jnp.inf)

    def prompt(which):
        at = pl.multiple_of(state_rows + (which * kv_count + head) // 2 * 2 * prompt_rows, 16)
        at = pl.ds(at, 2 * prompt_rows)
        pair = jnp.concatenate([mine_ref[:, at, :], other_ref[:, at, :]], axis=0).astype(F32)
        odd = lax.rem(head, 2) == 1
        part = jnp.where(odd, pair[:, prompt_rows:, :], pair[:, :prompt_rows, :])
        return part.reshape(devices * prompt_rows, HD).astype(BF16)

    prompt_keys = prompt(0)
    ones = jnp.ones((tokens, LANES), BF16)
    prompt_values = prompt(1)
    prompt_values = jnp.concatenate(
        [prompt_values, jnp.ones((prompt_values.shape[0], LANES), BF16)], axis=1
    )
    near_keys = jnp.concatenate([ref[...] for ref in prior_refs[:halves]] + [key_ref[...]], axis=0)
    near_values = [ref[...] for ref in prior_refs[halves:]] + [value_ref[...]]
    near_values = jnp.concatenate(
        [jnp.concatenate(near_values, axis=0), jnp.concatenate([ones, ones], axis=0)], axis=1
    )
    for query in range(query_ref.shape[1] // HD):
        at = slice(query * HD, (query + 1) * HD)
        for block in range(tokens // LANES):
            rows = slice(block * LANES, (block + 1) * LANES)
            reach = tokens + (block + 1) * LANES
            q = query_ref[rows, at]
            far = dot(q, prompt_keys, 1, 1)
            near = dot(q, near_keys[:reach, :], 1, 1) + bias_ref[rows, :reach]
            top = jnp.maximum(
                jnp.max(far, axis=1, keepdims=True), jnp.max(near, axis=1, keepdims=True)
            )
            far = jnp.exp2((far - top) * scale).astype(BF16)
            near = jnp.exp2((near - top) * scale).astype(BF16)
            summed = dot(far, prompt_values) + dot(near, near_values[:reach, :])
            out_ref[rows, at] = (summed[:, :HD] / summed[:, HD:]).astype(BF16)


def final_kernel(
    start_ref,
    level_ref,
    tail_ref,
    decay_ref,
    mine_ref,
    other_ref,
    read_ref,
    inner_ref,
    gate_ref,
    gain_ref,
    out_ref,
    *,
    state_rows,
    heads,
    per_group,
    channels,
):
    group = pl.program_id(0)
    tokens = read_ref.shape[0]
    level = jnp.exp(level_ref[...])
    carried = start_ref[:, : 2 * heads] < 0
    decay = decay_ref[...].astype(F32)
    decay = decay[0:1, :] + decay[1:2, :]
    spread = expander(heads, group, per_group, channels)
    from_prompt = dot(two_parts(jnp.where(carried, level * decay, level), heads), spread)
    from_prior = dot(two_parts(jnp.where(carried, level, 0.0), heads), spread)
    odd = lax.rem(lax.axis_index("reader"), 2) == 1
    seeds = []
    for pair in range(mine_ref.shape[0]):
        mine, other = mine_ref[pair, :state_rows, :], other_ref[pair, :state_rows, :]
        seeds += [jnp.where(odd, other, mine), jnp.where(odd, mine, other)]
    seeds = jnp.concatenate(seeds, axis=0)
    read = read_ref[...]
    mixed = inner_ref[...].astype(F32)
    mixed = mixed + from_prompt * dot(read, seeds, 1, 1)
    mixed = mixed + from_prior * dot(read, tail_ref[...])
    gate = gate_ref[...].astype(F32)
    gated = mixed * (gate * (0.5 + 0.5 * jnp.tanh(0.5 * gate)))
    scale = lax.rsqrt(jnp.mean(gated * gated, axis=1, keepdims=True) + 1e-05)
    out_ref[...] = (gated * scale * gain_ref[...]).astype(BF16)


def shifted(value, axis, by):
    length = lax.axis_size(axis)
    return lax.ppermute(value, axis, [(i, i + by) for i in range(length - by)])


def params(limit=32):
    return pltpu.CompilerParams(vmem_limit_bytes=limit * MIB)


def whole(shape):
    return pl.BlockSpec(shape, lambda g: (0,) * len(shape))


def local(
    answer_lengths,
    mixer_input,
    gate_input,
    state_write,
    state_read,
    step_raw,
    decay_rate,
    skip_gain,
    norm_gain,
    prompt_state,
    queries,
    answer_keys,
    answer_values,
    prompt_keys,
    prompt_values,
):
    tokens, columns = mixer_input.shape
    heads = decay_rate.shape[0]
    state_rows, state = prompt_state.shape
    groups = state_write.shape[1] // state
    per_group = heads // groups
    channels = columns // heads
    width = per_group * channels
    prompt_rows, kv_width = prompt_keys.shape
    kv_count = kv_width // HD
    devices = lax.axis_size("reader")
    in_hbm = lambda value: pltpu.with_memory_space_constraint(value, pltpu.MemorySpace.HBM)
    mixer_input, gate_input, state_write, state_read = map(
        in_hbm, (mixer_input, gate_input, state_write, state_read)
    )
    prompt_state, queries, answer_keys, answer_values, prompt_keys, prompt_values = map(
        in_hbm, (prompt_state, queries, answer_keys, answer_values, prompt_keys, prompt_values)
    )
    lengths, rate, skip, gain = map(
        lambda value: in_hbm(value.reshape(1, -1)),
        (answer_lengths, decay_rate, skip_gain, norm_gain),
    )
    sizes = dict(heads=heads, per_group=per_group, channels=channels)
    packed_rows = state_rows + 2 * prompt_rows * kv_count

    packed = pl.pallas_call(
        pack_kernel,
        out_shape=jax.ShapeDtypeStruct((packed_rows, HD), BF16),
        compiler_params=params(),
        name="pack",
    )(prompt_state, prompt_keys, prompt_values)
    lanes_of = [list(range(first, devices, 2)) for first in range(2)]
    mine = lax.all_gather(packed, "reader", axis=0, tiled=False, axis_index_groups=lanes_of)
    packed, raw = lax.optimization_barrier((packed, step_raw.T))
    raw = in_hbm(raw)

    halves = tokens // state
    tail_width = columns + 2 * heads + 2 * halves * kv_width
    by_group = lambda rows: pl.BlockSpec((rows, state), lambda g: (0, g))
    wide = pl.BlockSpec((tokens, width), lambda g: (0, g))
    tail, level, column, start = pl.pallas_call(
        functools.partial(tail_kernel, **sizes),
        grid=(groups,),
        in_specs=[
            whole(lengths.shape),
            whole(raw.shape),
            whole((1, heads)),
            wide,
            by_group(tokens),
            whole(answer_keys.shape),
            whole(answer_values.shape),
        ],
        out_specs=(
            whole((state, tail_width)),
            whole((tokens, 2 * heads)),
            whole((heads, tokens)),
            whole((tokens, LANES)),
        ),
        out_shape=(
            jax.ShapeDtypeStruct((state, tail_width), BF16),
            jax.ShapeDtypeStruct((tokens, 2 * heads), F32),
            jax.ShapeDtypeStruct((heads, tokens), F32),
            jax.ShapeDtypeStruct((tokens, LANES), F32),
        ),
        scratch_shapes=[pltpu.VMEM((tokens, 2 * heads), BF16)],
        compiler_params=params(),
        name="tail",
    )(lengths, raw, rate, mixer_input, state_write, answer_keys, answer_values)
    tail = shifted(tail, "reader", 1)

    inner = pl.pallas_call(
        functools.partial(inner_kernel, **sizes),
        grid=(groups,),
        in_specs=[
            whole((tokens, LANES)),
            whole((tokens, 2 * heads)),
            pl.BlockSpec((per_group, tokens), lambda g: (g, 0)),
            whole((1, heads)),
            wide,
            by_group(tokens),
            by_group(tokens),
        ],
        out_specs=wide,
        out_shape=jax.ShapeDtypeStruct((tokens, columns), BF16),
        compiler_params=params(),
        cost_estimate=pl.CostEstimate(
            flops=heads * tokens * tokens * channels * 8,
            bytes_accessed=tokens * columns * 4,
            transcendentals=heads * tokens * tokens,
        ),
        name="inner",
    )(start, level, column, skip, mixer_input, state_write, state_read)

    mine, inner = lax.optimization_barrier((mine, inner))
    other = lax.ppermute(mine, "reader", [(i, i ^ 1) for i in range(devices)])
    mine = in_hbm(mine)
    prior_at = (columns + 2 * heads) // HD
    prior_part = lambda part: pl.BlockSpec(
        (state, HD), lambda k: (0, prior_at + part * kv_count + k)
    )
    group_size = queries.shape[1] // kv_width
    attention_out = pl.pallas_call(
        functools.partial(
            attend_kernel,
            halves=halves,
            state_rows=state_rows,
            prompt_rows=prompt_rows,
            kv_count=kv_count,
        ),
        grid=(kv_count,),
        in_specs=[
            whole((tokens, LANES)),
            pl.BlockSpec((tokens, group_size * HD), lambda k: (0, k)),
            pl.BlockSpec((tokens, HD), lambda k: (0, k)),
            pl.BlockSpec((tokens, HD), lambda k: (0, k)),
            whole((devices // 2, packed_rows, HD)),
            whole((devices // 2, packed_rows, HD)),
        ]
        + [prior_part(part) for part in range(2 * halves)],
        out_specs=pl.BlockSpec((tokens, group_size * HD), lambda k: (0, k)),
        out_shape=jax.ShapeDtypeStruct(queries.shape, BF16),
        scratch_shapes=[pltpu.VMEM((tokens, 2 * tokens), F32)],
        compiler_params=params(),
        name="attend",
    )(start, queries, answer_keys, answer_values, mine, other, *[tail] * (2 * halves))

    mixer_out = pl.pallas_call(
        functools.partial(final_kernel, state_rows=state_rows, **sizes),
        grid=(groups,),
        in_specs=[
            whole((tokens, LANES)),
            whole((tokens, 2 * heads)),
            pl.BlockSpec((state, width), lambda g: (0, g)),
            pl.BlockSpec((16, 2 * heads), lambda g: (0, columns // (2 * heads))),
            pl.BlockSpec((devices // groups // 2, packed_rows, HD), lambda g: (g, 0, 0)),
            pl.BlockSpec((devices // groups // 2, packed_rows, HD), lambda g: (g, 0, 0)),
            by_group(tokens),
            wide,
            wide,
            pl.BlockSpec((1, width), lambda g: (0, g)),
        ],
        out_specs=wide,
        out_shape=jax.ShapeDtypeStruct((tokens, columns), BF16),
        compiler_params=params(),
        name="final",
    )(start, level, tail, tail, mine, other, state_read, inner, gate_input, gain)
    return (mixer_out, attention_out)


def solution(mesh):
    rows = P(("group", "reader"), None)
    in_specs = (P("group"),) + (rows,) * 5 + (P(),) * 3 + (rows,) * 6
    return jax.shard_map(
        local, mesh=mesh, in_specs=in_specs, out_specs=(rows, rows), check_vma=False
    )
```

```python
import functools
import math

import jax
import jax.numpy as jnp
from jax import lax
from jax.experimental import pallas as pl
from jax.experimental.pallas import tpu as pltpu
from jax.sharding import PartitionSpec as P

HD = 128
LANES = 128
LOG2E = 1.4426950408889634
F32 = jnp.float32
BF16 = jnp.bfloat16
MIB = 1 << 20


def iota(shape, dim):
    return lax.broadcasted_iota(jnp.int32, shape, dim)


def dot(a, b, ca=1, cb=0):
    return lax.dot_general(a, b, (((ca,), (cb,)), ((), ())), preferred_element_type=F32)


def expander(heads, group, per_group, channels):
    shape = (2 * heads, per_group * channels)
    row = iota(shape, 0)
    head = jnp.where(row >= heads, row - heads, row) - group * per_group
    column = iota(shape, 1)
    first = head * channels
    return jnp.where((column >= first) & (column < first + channels), 1.0, 0.0).astype(BF16)


def two_parts(value, heads):
    high = value.astype(BF16).astype(F32)
    return jnp.where(iota(value.shape, 1) < heads, high, value - high).astype(BF16)


def pack_kernel(state_ref, keys_ref, values_ref, out_ref):
    rows = state_ref.shape[0]
    state = state_ref[...].astype(BF16)
    parts = []
    for ref in (keys_ref, values_ref):
        wide = ref[...].astype(F32)
        for head in range(wide.shape[1] // HD):
            parts.append(wide[:, head * HD : (head + 1) * HD])
    parts = jnp.concatenate(parts, axis=0).astype(BF16)
    for copy in range(out_ref.shape[0]):
        out_ref[copy, :rows, :] = state
        out_ref[copy, rows:, :] = parts


def tail_kernel(
    lengths_ref,
    raw_ref,
    rate_ref,
    x_ref,
    write_ref,
    keys_ref,
    values_ref,
    tail_ref,
    level_ref,
    column_ref,
    start_ref,
    weight_ref,
    *,
    heads,
    per_group,
    channels,
):
    group = pl.program_id(0)
    tokens = x_ref.shape[0]
    columns = heads * channels

    @pl.when(group == 0)
    def _():
        base = (lax.axis_index("reader") * tokens).astype(F32)
        lengths = lengths_ref[...].astype(F32)
        answers = lengths.shape[1]
        square = (answers, answers)
        ends = jnp.sum(
            jnp.where(iota(square, 1) <= iota(square, 0), lengths, 0.0), axis=1, keepdims=True
        )
        place = base + iota((1, tokens), 1).astype(F32)
        start = jnp.max(jnp.where(ends <= place, ends, 0.0), axis=0, keepdims=True) - base
        start = jnp.broadcast_to(start, (LANES, tokens)).T
        start_ref[...] = start
        wide = jnp.concatenate([start] * (tokens // LANES), axis=1)
        square = (tokens, tokens)
        source = iota(square, 1)
        mask = (source.astype(F32) >= wide) & (source <= iota(square, 0))
        mask = jnp.where(mask, 1.0, 0.0).astype(BF16)
        raw = raw_ref[...]
        rate = jnp.broadcast_to(rate_ref[...], (heads, heads))
        diagonal = iota((heads, heads), 0) == iota((heads, heads), 1)
        rate = jnp.sum(jnp.where(diagonal, rate, 0.0), axis=1, keepdims=True)
        step = jnp.maximum(raw, 0.0) + jnp.log1p(jnp.exp(-jnp.abs(raw)))
        falling = -rate * step
        first = falling.astype(BF16)
        rest = falling - first.astype(F32)
        second = rest.astype(BF16)
        third = (rest - second.astype(F32)).astype(BF16)
        level = dot(first, mask, 1, 1) + (dot(second, mask, 1, 1) + dot(third, mask, 1, 1))
        column_ref[...] = level * LOG2E - jnp.log(step) * LOG2E
        level = jnp.concatenate([level, level], axis=0).T
        step = jnp.concatenate([step, step], axis=0).T
        level_ref[...] = level
        last = level[tokens - 1 :, :]
        own = iota((tokens, 2 * heads), 0).astype(F32) >= start[tokens - 1 :, : 2 * heads]
        weight = jnp.where(own, jnp.exp(last - level) * step, 0.0)
        weight_ref[...] = two_parts(weight, heads)
        decay = jnp.exp(jnp.broadcast_to(last, (16, 2 * heads)))
        high = decay.astype(BF16).astype(F32)
        row = iota(decay.shape, 0)
        decay = jnp.where(row == 0, high, jnp.where(row == 1, decay - high, 0.0))
        at = columns + 2 * heads
        tail_ref[:, columns:at] = jnp.zeros((tail_ref.shape[0], 2 * heads), BF16)
        tail_ref[:16, columns:at] = decay.astype(BF16)
        depth, width = tail_ref.shape[0], keys_ref.shape[1]
        for ref in (keys_ref, values_ref):
            for half in range(tokens // depth):
                tail_ref[:, at : at + width] = ref[half * depth : (half + 1) * depth, :]
                at += width

    spread = expander(heads, group, per_group, channels)
    weight = dot(weight_ref[...], spread)
    weighted = (x_ref[...].astype(F32) * weight).astype(BF16)
    width = per_group * channels
    tail_ref[:, pl.ds(pl.multiple_of(group * width, width), width)] = dot(
        write_ref[...], weighted, 0, 0
    ).astype(BF16)


def inner_kernel(
    start_ref,
    level_ref,
    column_ref,
    skip_ref,
    x_ref,
    write_ref,
    read_ref,
    out_ref,
    *,
    heads,
    per_group,
    channels,
):
    group = pl.program_id(0)
    tokens = x_ref.shape[0]
    both = dot(read_ref[...], write_ref[...], 1, 1)
    square = (tokens, tokens)
    source = iota(square, 1)
    wide = jnp.concatenate([start_ref[...]] * (tokens // LANES), axis=1)
    both = jnp.where((source.astype(F32) >= wide) & (source <= iota(square, 0)), both, 0.0)
    lanes = level_ref.shape[1]
    level = pltpu.roll(level_ref[...] * LOG2E, lanes - group * per_group, 1)
    skip = jnp.concatenate([skip_ref[...]] * 2, axis=1)
    skip = two_parts(jnp.broadcast_to(skip, (16, 2 * heads)), heads)
    skip = dot(skip, expander(heads, group, per_group, channels))[:1, :]
    per_tile = LANES // channels
    lane = iota((LANES, LANES), 1)
    for tile in range(per_group // per_tile):
        at = slice(tile * LANES, (tile + 1) * LANES)
        x = x_ref[:, at]
        for block in range(tokens // LANES):
            rows = slice(block * LANES, (block + 1) * LANES)
            reach = (block + 1) * LANES
            total = None
            for part in range(per_tile):
                head = tile * per_tile + part
                gap = level[rows, head : head + 1] - column_ref[head : head + 1, :reach]
                mixing = (jnp.exp2(jnp.minimum(gap, 64.0)) * both[rows, :reach]).astype(BF16)
                result = dot(mixing, x[:reach, :])
                total = result if total is None else jnp.where(
                    lane < part * channels, total, result
                )
            total = total + skip[:, at] * x[rows, :].astype(F32)
            out_ref[rows, at] = total.astype(BF16)


def attend_kernel(
    start_ref,
    query_ref,
    key_ref,
    value_ref,
    mine_ref,
    other_ref,
    *rest,
    halves,
    state_rows,
    prompt_rows,
    kv_count,
):
    prior_refs, (out_ref, bias_ref) = rest[:-2], rest[-2:]
    head = pl.program_id(0)
    tokens = query_ref.shape[0]
    devices = 2 * mine_ref.shape[0]
    scale = LOG2E / math.sqrt(HD)

    @pl.when(head == 0)
    def _():
        shape = (tokens, 2 * tokens)
        place = iota(shape, 1) - tokens
        wide = jnp.concatenate([start_ref[...]] * (2 * tokens // LANES), axis=1)
        allowed = (place.astype(F32) >= wide) & (place <= iota(shape, 0))
        bias_ref[...] = jnp.where(allowed, 0.0, -jnp.inf)

    def prompt(which):
        at = pl.multiple_of(state_rows + (which * kv_count + head) // 2 * 2 * prompt_rows, 16)
        at = pl.ds(at, 2 * prompt_rows)
        pair = jnp.concatenate([mine_ref[:, at, :], other_ref[:, at, :]], axis=0).astype(F32)
        odd = lax.rem(head, 2) == 1
        part = jnp.where(odd, pair[:, prompt_rows:, :], pair[:, :prompt_rows, :])
        return part.reshape(devices * prompt_rows, HD).astype(BF16)

    prompt_keys = prompt(0)
    ones = jnp.ones((tokens, LANES), BF16)
    prompt_values = prompt(1)
    prompt_values = jnp.concatenate(
        [prompt_values, jnp.ones((prompt_values.shape[0], LANES), BF16)], axis=1
    )
    near_keys = jnp.concatenate([ref[...] for ref in prior_refs[:halves]] + [key_ref[...]], axis=0)
    near_values = [ref[...] for ref in prior_refs[halves:]] + [value_ref[...]]
    near_values = jnp.concatenate(
        [jnp.concatenate(near_values, axis=0), jnp.concatenate([ones, ones], axis=0)], axis=1
    )
    for query in range(query_ref.shape[1] // HD):
        at = slice(query * HD, (query + 1) * HD)
        for block in range(tokens // LANES):
            rows = slice(block * LANES, (block + 1) * LANES)
            reach = tokens + (block + 1) * LANES
            q = query_ref[rows, at]
            far = dot(q, prompt_keys, 1, 1)
            near = dot(q, near_keys[:reach, :], 1, 1) + bias_ref[rows, :reach]
            top = jnp.maximum(
                jnp.max(far, axis=1, keepdims=True), jnp.max(near, axis=1, keepdims=True)
            )
            far = jnp.exp2((far - top) * scale).astype(BF16)
            near = jnp.exp2((near - top) * scale).astype(BF16)
            summed = dot(far, prompt_values) + dot(near, near_values[:reach, :])
            out_ref[rows, at] = (summed[:, :HD] / summed[:, HD:]).astype(BF16)


def final_kernel(
    start_ref,
    level_ref,
    tail_ref,
    decay_ref,
    mine_ref,
    other_ref,
    read_ref,
    inner_ref,
    gate_ref,
    gain_ref,
    out_ref,
    *,
    state_rows,
    heads,
    per_group,
    channels,
):
    group = pl.program_id(0)
    tokens = read_ref.shape[0]
    level = jnp.exp(level_ref[...])
    carried = start_ref[:, : 2 * heads] < 0
    decay = decay_ref[...].astype(F32)
    decay = decay[0:1, :] + decay[1:2, :]
    spread = expander(heads, group, per_group, channels)
    from_prompt = dot(two_parts(jnp.where(carried, level * decay, level), heads), spread)
    from_prior = dot(two_parts(jnp.where(carried, level, 0.0), heads), spread)
    odd = lax.rem(lax.axis_index("reader"), 2) == 1
    seeds = []
    for pair in range(mine_ref.shape[0]):
        mine, other = mine_ref[pair, :state_rows, :], other_ref[pair, :state_rows, :]
        seeds += [jnp.where(odd, other, mine), jnp.where(odd, mine, other)]
    seeds = jnp.concatenate(seeds, axis=0)
    read = read_ref[...]
    mixed = inner_ref[...].astype(F32)
    mixed = mixed + from_prompt * dot(read, seeds, 1, 1)
    mixed = mixed + from_prior * dot(read, tail_ref[...])
    gate = gate_ref[...].astype(F32)
    gated = mixed * (gate * (0.5 + 0.5 * jnp.tanh(0.5 * gate)))
    scale = lax.rsqrt(jnp.mean(gated * gated, axis=1, keepdims=True) + 1e-05)
    out_ref[...] = (gated * scale * gain_ref[...]).astype(BF16)


def shifted(value, axis, by):
    length = lax.axis_size(axis)
    return lax.ppermute(value, axis, [(i, i + by) for i in range(length - by)])


def params(limit=32):
    return pltpu.CompilerParams(vmem_limit_bytes=limit * MIB)


def whole(shape):
    return pl.BlockSpec(shape, lambda g: (0,) * len(shape))


def local(
    answer_lengths,
    mixer_input,
    gate_input,
    state_write,
    state_read,
    step_raw,
    decay_rate,
    skip_gain,
    norm_gain,
    prompt_state,
    queries,
    answer_keys,
    answer_values,
    prompt_keys,
    prompt_values,
):
    tokens, columns = mixer_input.shape
    heads = decay_rate.shape[0]
    state_rows, state = prompt_state.shape
    groups = state_write.shape[1] // state
    per_group = heads // groups
    channels = columns // heads
    width = per_group * channels
    prompt_rows, kv_width = prompt_keys.shape
    kv_count = kv_width // HD
    devices = lax.axis_size("reader")
    in_hbm = lambda value: pltpu.with_memory_space_constraint(value, pltpu.MemorySpace.HBM)
    mixer_input, gate_input, state_write, state_read = map(
        in_hbm, (mixer_input, gate_input, state_write, state_read)
    )
    prompt_state, queries, answer_keys, answer_values, prompt_keys, prompt_values = map(
        in_hbm, (prompt_state, queries, answer_keys, answer_values, prompt_keys, prompt_values)
    )
    lengths, rate, skip, gain = map(
        lambda value: in_hbm(value.reshape(1, -1)),
        (answer_lengths, decay_rate, skip_gain, norm_gain),
    )
    sizes = dict(heads=heads, per_group=per_group, channels=channels)
    packed_rows = state_rows + 2 * prompt_rows * kv_count

    packed = pl.pallas_call(
        pack_kernel,
        out_shape=jax.ShapeDtypeStruct((devices // 2, packed_rows, HD), BF16),
        compiler_params=params(),
        name="pack",
    )(prompt_state, prompt_keys, prompt_values)
    lanes_of = [list(range(first, devices, 2)) for first in range(2)]
    packed, raw = lax.optimization_barrier((packed, step_raw.T))
    mine = lax.all_to_all(packed, "reader", 0, 0, axis_index_groups=lanes_of, tiled=True)
    raw = in_hbm(raw)

    halves = tokens // state
    tail_width = columns + 2 * heads + 2 * halves * kv_width
    by_group = lambda rows: pl.BlockSpec((rows, state), lambda g: (0, g))
    wide = pl.BlockSpec((tokens, width), lambda g: (0, g))
    tail, level, column, start = pl.pallas_call(
        functools.partial(tail_kernel, **sizes),
        grid=(groups,),
        in_specs=[
            whole(lengths.shape),
            whole(raw.shape),
            whole((1, heads)),
            wide,
            by_group(tokens),
            whole(answer_keys.shape),
            whole(answer_values.shape),
        ],
        out_specs=(
            whole((state, tail_width)),
            whole((tokens, 2 * heads)),
            whole((heads, tokens)),
            whole((tokens, LANES)),
        ),
        out_shape=(
            jax.ShapeDtypeStruct((state, tail_width), BF16),
            jax.ShapeDtypeStruct((tokens, 2 * heads), F32),
            jax.ShapeDtypeStruct((heads, tokens), F32),
            jax.ShapeDtypeStruct((tokens, LANES), F32),
        ),
        scratch_shapes=[pltpu.VMEM((tokens, 2 * heads), BF16)],
        compiler_params=params(),
        name="tail",
    )(lengths, raw, rate, mixer_input, state_write, answer_keys, answer_values)
    tail = shifted(tail, "reader", 1)

    inner = pl.pallas_call(
        functools.partial(inner_kernel, **sizes),
        grid=(groups,),
        in_specs=[
            whole((tokens, LANES)),
            whole((tokens, 2 * heads)),
            pl.BlockSpec((per_group, tokens), lambda g: (g, 0)),
            whole((1, heads)),
            wide,
            by_group(tokens),
            by_group(tokens),
        ],
        out_specs=wide,
        out_shape=jax.ShapeDtypeStruct((tokens, columns), BF16),
        compiler_params=params(),
        cost_estimate=pl.CostEstimate(
            flops=heads * tokens * tokens * channels * 8,
            bytes_accessed=tokens * columns * 4,
            transcendentals=heads * tokens * tokens,
        ),
        name="inner",
    )(start, level, column, skip, mixer_input, state_write, state_read)

    mine, inner = lax.optimization_barrier((mine, inner))
    other = lax.ppermute(mine, "reader", [(i, i ^ 1) for i in range(devices)])
    prior_at = (columns + 2 * heads) // HD
    prior_part = lambda part: pl.BlockSpec(
        (state, HD), lambda k: (0, prior_at + part * kv_count + k)
    )
    group_size = queries.shape[1] // kv_width
    attention_out = pl.pallas_call(
        functools.partial(
            attend_kernel,
            halves=halves,
            state_rows=state_rows,
            prompt_rows=prompt_rows,
            kv_count=kv_count,
        ),
        grid=(kv_count,),
        in_specs=[
            whole((tokens, LANES)),
            pl.BlockSpec((tokens, group_size * HD), lambda k: (0, k)),
            pl.BlockSpec((tokens, HD), lambda k: (0, k)),
            pl.BlockSpec((tokens, HD), lambda k: (0, k)),
            whole((devices // 2, packed_rows, HD)),
            whole((devices // 2, packed_rows, HD)),
        ]
        + [prior_part(part) for part in range(2 * halves)],
        out_specs=pl.BlockSpec((tokens, group_size * HD), lambda k: (0, k)),
        out_shape=jax.ShapeDtypeStruct(queries.shape, BF16),
        scratch_shapes=[pltpu.VMEM((tokens, 2 * tokens), F32)],
        compiler_params=params(),
        name="attend",
    )(start, queries, answer_keys, answer_values, mine, other, *[tail] * (2 * halves))

    mixer_out = pl.pallas_call(
        functools.partial(final_kernel, state_rows=state_rows, **sizes),
        grid=(groups,),
        in_specs=[
            whole((tokens, LANES)),
            whole((tokens, 2 * heads)),
            pl.BlockSpec((state, width), lambda g: (0, g)),
            pl.BlockSpec((16, 2 * heads), lambda g: (0, columns // (2 * heads))),
            pl.BlockSpec((devices // groups // 2, packed_rows, HD), lambda g: (g, 0, 0)),
            pl.BlockSpec((devices // groups // 2, packed_rows, HD), lambda g: (g, 0, 0)),
            by_group(tokens),
            wide,
            wide,
            pl.BlockSpec((1, width), lambda g: (0, g)),
        ],
        out_specs=wide,
        out_shape=jax.ShapeDtypeStruct((tokens, columns), BF16),
        compiler_params=params(),
        name="final",
    )(start, level, tail, tail, mine, other, state_read, inner, gate_input, gain)
    return (mixer_out, attention_out)


def solution(mesh):
    rows = P(("group", "reader"), None)
    in_specs = (P("group"),) + (rows,) * 5 + (P(),) * 3 + (rows,) * 6
    return jax.shard_map(
        local, mesh=mesh, in_specs=in_specs, out_specs=(rows, rows), check_vma=False
    )
```

```python
import functools
import math

import jax
import jax.numpy as jnp
from jax import lax
from jax.experimental import pallas as pl
from jax.experimental.pallas import tpu as pltpu
from jax.sharding import PartitionSpec as P

HD = 128
LANES = 128
NEAR = 4
LOG2E = 1.4426950408889634
F32 = jnp.float32
BF16 = jnp.bfloat16
MIB = 1 << 20


def iota(shape, dim):
    return lax.broadcasted_iota(jnp.int32, shape, dim)


def dot(a, b, ca=1, cb=0):
    return lax.dot_general(a, b, (((ca,), (cb,)), ((), ())), preferred_element_type=F32)


def expander(heads, group, per_group, channels):
    shape = (2 * heads, per_group * channels)
    row = iota(shape, 0)
    head = jnp.where(row >= heads, row - heads, row) - group * per_group
    column = iota(shape, 1)
    first = head * channels
    return jnp.where((column >= first) & (column < first + channels), 1.0, 0.0).astype(BF16)


def two_parts(value, heads):
    high = value.astype(BF16).astype(F32)
    return jnp.where(iota(value.shape, 1) < heads, high, value - high).astype(BF16)


def pack_kernel(state_ref, keys_ref, values_ref, near_keys_ref, near_values_ref, out_ref, near_ref):
    rows = state_ref.shape[0]
    state = state_ref[...].astype(BF16)
    parts = []
    for ref in (keys_ref, values_ref):
        wide = ref[...].astype(F32)
        for head in range(wide.shape[1] // HD):
            parts.append(wide[:, head * HD : (head + 1) * HD])
    parts = jnp.concatenate(parts, axis=0).astype(BF16)
    for copy in range(out_ref.shape[0]):
        out_ref[copy, :rows, :] = state
        out_ref[copy, rows:, :] = parts
    width = near_keys_ref.shape[1]
    near_ref[:, :width] = near_keys_ref[...]
    near_ref[:, width:] = near_values_ref[...]


def tail_kernel(
    lengths_ref,
    raw_ref,
    rate_ref,
    x_ref,
    write_ref,
    tail_ref,
    level_ref,
    column_ref,
    start_ref,
    weight_ref,
    *,
    heads,
    per_group,
    channels,
):
    group = pl.program_id(0)
    tokens = x_ref.shape[0]
    columns = heads * channels

    @pl.when(group == 0)
    def _():
        base = (lax.axis_index("reader") * tokens).astype(F32)
        lengths = lengths_ref[...].astype(F32)
        answers = lengths.shape[1]
        square = (answers, answers)
        ends = jnp.sum(
            jnp.where(iota(square, 1) <= iota(square, 0), lengths, 0.0), axis=1, keepdims=True
        )
        place = base + iota((1, tokens), 1).astype(F32)
        start = jnp.max(jnp.where(ends <= place, ends, 0.0), axis=0, keepdims=True) - base
        start = jnp.broadcast_to(start, (LANES, tokens)).T
        start_ref[...] = start
        wide = jnp.concatenate([start] * (tokens // LANES), axis=1)
        square = (tokens, tokens)
        source = iota(square, 1)
        mask = (source.astype(F32) >= wide) & (source <= iota(square, 0))
        mask = jnp.where(mask, 1.0, 0.0).astype(BF16)
        raw = raw_ref[...]
        rate = jnp.broadcast_to(rate_ref[...], (heads, heads))
        diagonal = iota((heads, heads), 0) == iota((heads, heads), 1)
        rate = jnp.sum(jnp.where(diagonal, rate, 0.0), axis=1, keepdims=True)
        step = jnp.maximum(raw, 0.0) + jnp.log1p(jnp.exp(-jnp.abs(raw)))
        falling = -rate * step
        first = falling.astype(BF16)
        rest = falling - first.astype(F32)
        second = rest.astype(BF16)
        third = (rest - second.astype(F32)).astype(BF16)
        level = dot(first, mask, 1, 1) + (dot(second, mask, 1, 1) + dot(third, mask, 1, 1))
        column_ref[...] = level * LOG2E - jnp.log(step) * LOG2E
        level = jnp.concatenate([level, level], axis=0).T
        step = jnp.concatenate([step, step], axis=0).T
        level_ref[...] = level
        last = level[tokens - 1 :, :]
        own = iota((tokens, 2 * heads), 0).astype(F32) >= start[tokens - 1 :, : 2 * heads]
        weight = jnp.where(own, jnp.exp(last - level) * step, 0.0)
        weight_ref[...] = two_parts(weight, heads)
        decay = jnp.exp(jnp.broadcast_to(last, (16, 2 * heads)))
        high = decay.astype(BF16).astype(F32)
        row = iota(decay.shape, 0)
        decay = jnp.where(row == 0, high, jnp.where(row == 1, decay - high, 0.0))
        tail_ref[:, columns:] = jnp.zeros((tail_ref.shape[0], 2 * heads), BF16)
        tail_ref[:16, columns:] = decay.astype(BF16)

    spread = expander(heads, group, per_group, channels)
    weight = dot(weight_ref[...], spread)
    weighted = (x_ref[...].astype(F32) * weight).astype(BF16)
    width = per_group * channels
    tail_ref[:, pl.ds(pl.multiple_of(group * width, width), width)] = dot(
        write_ref[...], weighted, 0, 0
    ).astype(BF16)


def inner_kernel(
    start_ref,
    level_ref,
    column_ref,
    skip_ref,
    x_ref,
    write_ref,
    read_ref,
    *rest,
    first,
    heads,
    per_group,
    channels,
):
    out_ref = rest[-1]
    group = first + pl.program_id(0)
    tokens = x_ref.shape[0]
    both = dot(read_ref[...], write_ref[...], 1, 1)
    square = (tokens, tokens)
    source = iota(square, 1)
    wide = jnp.concatenate([start_ref[...]] * (tokens // LANES), axis=1)
    both = jnp.where((source.astype(F32) >= wide) & (source <= iota(square, 0)), both, 0.0)
    lanes = level_ref.shape[1]
    level = pltpu.roll(level_ref[...] * LOG2E, lanes - group * per_group, 1)
    skip = jnp.concatenate([skip_ref[...]] * 2, axis=1)
    skip = two_parts(jnp.broadcast_to(skip, (16, 2 * heads)), heads)
    skip = dot(skip, expander(heads, group, per_group, channels))[:1, :]
    per_tile = LANES // channels
    lane = iota((LANES, LANES), 1)
    for tile in range(per_group // per_tile):
        at = slice(tile * LANES, (tile + 1) * LANES)
        x = x_ref[:, at]
        for block in range(tokens // LANES):
            rows = slice(block * LANES, (block + 1) * LANES)
            reach = (block + 1) * LANES
            total = None
            for part in range(per_tile):
                head = tile * per_tile + part
                gap = level[rows, head : head + 1] - column_ref[head : head + 1, :reach]
                mixing = (jnp.exp2(jnp.minimum(gap, 64.0)) * both[rows, :reach]).astype(BF16)
                result = dot(mixing, x[:reach, :])
                total = result if total is None else jnp.where(
                    lane < part * channels, total, result
                )
            total = total + skip[:, at] * x[rows, :].astype(F32)
            out_ref[rows, at] = total.astype(BF16)


def attend_kernel(
    start_ref,
    query_ref,
    key_ref,
    value_ref,
    prior_key_ref,
    prior_value_ref,
    *rest,
    state_rows,
    prompt_rows,
    kv_count,
):
    gathered, (out_ref, bias_ref) = rest[:-2], rest[-2:]
    head = pl.program_id(0)
    tokens = query_ref.shape[0]
    devices = len(gathered) * gathered[0].shape[0]
    scale = LOG2E / math.sqrt(HD)

    @pl.when(head == 0)
    def _():
        shape = (tokens, 2 * tokens)
        place = iota(shape, 1) - tokens
        wide = jnp.concatenate([start_ref[...]] * (2 * tokens // LANES), axis=1)
        allowed = (place.astype(F32) >= wide) & (place <= iota(shape, 0))
        bias_ref[...] = jnp.where(allowed, 0.0, -jnp.inf)

    def prompt(which):
        at = pl.multiple_of(state_rows + (which * kv_count + head) // 2 * 2 * prompt_rows, 16)
        at = pl.ds(at, 2 * prompt_rows)
        pair = jnp.concatenate([ref[:, at, :] for ref in gathered], axis=0).astype(F32)
        odd = lax.rem(head, 2) == 1
        part = jnp.where(odd, pair[:, prompt_rows:, :], pair[:, :prompt_rows, :])
        return part.reshape(devices * prompt_rows, HD).astype(BF16)

    prompt_keys = prompt(0)
    ones = jnp.ones((tokens, LANES), BF16)
    prompt_values = prompt(1)
    prompt_values = jnp.concatenate(
        [prompt_values, jnp.ones((prompt_values.shape[0], LANES), BF16)], axis=1
    )
    near_keys = jnp.concatenate([prior_key_ref[...], key_ref[...]], axis=0)
    near_values = [prior_value_ref[...], value_ref[...]]
    near_values = jnp.concatenate(
        [jnp.concatenate(near_values, axis=0), jnp.concatenate([ones, ones], axis=0)], axis=1
    )
    for query in range(query_ref.shape[1] // HD):
        at = slice(query * HD, (query + 1) * HD)
        for block in range(tokens // LANES):
            rows = slice(block * LANES, (block + 1) * LANES)
            reach = tokens + (block + 1) * LANES
            q = query_ref[rows, at]
            far = dot(q, prompt_keys, 1, 1)
            near = dot(q, near_keys[:reach, :], 1, 1) + bias_ref[rows, :reach]
            top = jnp.maximum(
                jnp.max(far, axis=1, keepdims=True), jnp.max(near, axis=1, keepdims=True)
            )
            far = jnp.exp2((far - top) * scale).astype(BF16)
            near = jnp.exp2((near - top) * scale).astype(BF16)
            summed = dot(far, prompt_values) + dot(near, near_values[:reach, :])
            out_ref[rows, at] = (summed[:, :HD] / summed[:, HD:]).astype(BF16)


def final_kernel(
    start_ref,
    level_ref,
    tail_ref,
    decay_ref,
    read_ref,
    inner_ref,
    gate_ref,
    gain_ref,
    *rest,
    state_rows,
    heads,
    per_group,
    channels,
):
    gathered, out_ref = rest[:-1], rest[-1]
    group = pl.program_id(0)
    level = jnp.exp(level_ref[...])
    carried = start_ref[:, : 2 * heads] < 0
    decay = decay_ref[...].astype(F32)
    decay = decay[0:1, :] + decay[1:2, :]
    spread = expander(heads, group, per_group, channels)
    from_prompt = dot(two_parts(jnp.where(carried, level * decay, level), heads), spread)
    from_prior = dot(two_parts(jnp.where(carried, level, 0.0), heads), spread)
    own = lax.rem(lax.axis_index("reader"), NEAR)
    seeds = []
    for run in range(gathered[0].shape[0]):
        parts = [ref[run, :state_rows, :] for ref in gathered]
        bit = 1
        while bit < NEAR:
            swap = lax.rem(own // bit, 2) == 1
            parts = [jnp.where(swap, parts[i ^ bit], parts[i]) for i in range(NEAR)]
            bit *= 2
        seeds += parts
    seeds = jnp.concatenate(seeds, axis=0)
    read = read_ref[...]
    mixed = inner_ref[...].astype(F32)
    mixed = mixed + from_prompt * dot(read, seeds, 1, 1)
    mixed = mixed + from_prior * dot(read, tail_ref[...])
    gate = gate_ref[...].astype(F32)
    gated = mixed * (gate * (0.5 + 0.5 * jnp.tanh(0.5 * gate)))
    scale = lax.rsqrt(jnp.mean(gated * gated, axis=1, keepdims=True) + 1e-05)
    out_ref[...] = (gated * scale * gain_ref[...]).astype(BF16)


def shifted(value, axis, by):
    length = lax.axis_size(axis)
    return lax.ppermute(value, axis, [(i, i + by) for i in range(length - by)])


def params(limit=32):
    return pltpu.CompilerParams(vmem_limit_bytes=limit * MIB)


def whole(shape):
    return pl.BlockSpec(shape, lambda g: (0,) * len(shape))


def local(
    answer_lengths,
    mixer_input,
    gate_input,
    state_write,
    state_read,
    step_raw,
    decay_rate,
    skip_gain,
    norm_gain,
    prompt_state,
    queries,
    answer_keys,
    answer_values,
    prompt_keys,
    prompt_values,
):
    tokens, columns = mixer_input.shape
    heads = decay_rate.shape[0]
    state_rows, state = prompt_state.shape
    groups = state_write.shape[1] // state
    per_group = heads // groups
    channels = columns // heads
    width = per_group * channels
    prompt_rows, kv_width = prompt_keys.shape
    kv_count = kv_width // HD
    devices = lax.axis_size("reader")
    in_hbm = lambda value: pltpu.with_memory_space_constraint(value, pltpu.MemorySpace.HBM)
    mixer_input, gate_input, state_write, state_read = map(
        in_hbm, (mixer_input, gate_input, state_write, state_read)
    )
    prompt_state, queries, answer_keys, answer_values, prompt_keys, prompt_values = map(
        in_hbm, (prompt_state, queries, answer_keys, answer_values, prompt_keys, prompt_values)
    )
    lengths, rate, skip, gain = map(
        lambda value: in_hbm(value.reshape(1, -1)),
        (answer_lengths, decay_rate, skip_gain, norm_gain),
    )
    sizes = dict(heads=heads, per_group=per_group, channels=channels)
    packed_rows = state_rows + 2 * prompt_rows * kv_count

    packed, near = pl.pallas_call(
        pack_kernel,
        out_shape=(
            jax.ShapeDtypeStruct((devices // NEAR, packed_rows, HD), BF16),
            jax.ShapeDtypeStruct((tokens, 2 * kv_width), BF16),
        ),
        compiler_params=params(),
        name="pack",
    )(prompt_state, prompt_keys, prompt_values, answer_keys, answer_values)
    prior = shifted(near, "reader", 1)
    packed, raw = lax.optimization_barrier((packed, step_raw.T))
    lines = [list(range(first, devices, NEAR)) for first in range(NEAR)]
    line = lax.all_to_all(packed, "reader", 0, 0, axis_index_groups=lines, tiled=True)
    exchanged = lambda value, bit: lax.ppermute(
        value, "reader", [(i, i ^ bit) for i in range(devices)]
    )
    raw = in_hbm(raw)

    by_group = lambda rows: pl.BlockSpec((rows, state), lambda g: (0, g))
    wide = pl.BlockSpec((tokens, width), lambda g: (0, g))
    tail, level, column, start = pl.pallas_call(
        functools.partial(tail_kernel, **sizes),
        grid=(groups,),
        in_specs=[
            whole(lengths.shape),
            whole(raw.shape),
            whole((1, heads)),
            wide,
            by_group(tokens),
        ],
        out_specs=(
            whole((state, columns + 2 * heads)),
            whole((tokens, 2 * heads)),
            whole((heads, tokens)),
            whole((tokens, LANES)),
        ),
        out_shape=(
            jax.ShapeDtypeStruct((state, columns + 2 * heads), BF16),
            jax.ShapeDtypeStruct((tokens, 2 * heads), F32),
            jax.ShapeDtypeStruct((heads, tokens), F32),
            jax.ShapeDtypeStruct((tokens, LANES), F32),
        ),
        scratch_shapes=[pltpu.VMEM((tokens, 2 * heads), BF16)],
        compiler_params=params(),
        name="tail",
    )(lengths, raw, rate, mixer_input, state_write)
    tail = shifted(tail, "reader", 1)

    prior, line, column = lax.optimization_barrier((prior, line, column))

    def inner_part(first, count, *earlier):
        blocks = lambda rows, columns: pl.BlockSpec((rows, columns), lambda g: (0, first + g))
        return pl.pallas_call(
            functools.partial(inner_kernel, first=first, **sizes),
            grid=(count,),
            in_specs=[
                whole((tokens, LANES)),
                whole((tokens, 2 * heads)),
                pl.BlockSpec((per_group, tokens), lambda g: (first + g, 0)),
                whole((1, heads)),
                blocks(tokens, width),
                blocks(tokens, state),
                blocks(tokens, state),
            ]
            + [pl.BlockSpec(memory_space=pl.ANY)] * len(earlier),
            out_specs=blocks(tokens, width),
            out_shape=jax.ShapeDtypeStruct((tokens, columns), BF16),
            input_output_aliases={7: 0} if earlier else {},
            compiler_params=params(),
            cost_estimate=pl.CostEstimate(
                flops=count * per_group * tokens * tokens * channels * 8,
                bytes_accessed=count * tokens * width * 4,
                transcendentals=count * per_group * tokens * tokens,
            ),
            name="inner",
        )(start, level, column, skip, mixer_input, state_write, state_read, *earlier)

    half = groups // 2
    inner = inner_part(0, half)
    across = exchanged(line, 2)
    across, inner = lax.optimization_barrier((across, inner))
    gathered = (line, exchanged(line, 1), across, exchanged(across, 1))
    inner = inner_part(half, groups - half, inner)
    group_size = queries.shape[1] // kv_width
    attention_out = pl.pallas_call(
        functools.partial(
            attend_kernel,
            state_rows=state_rows,
            prompt_rows=prompt_rows,
            kv_count=kv_count,
        ),
        grid=(kv_count,),
        in_specs=[
            whole((tokens, LANES)),
            pl.BlockSpec((tokens, group_size * HD), lambda k: (0, k)),
            pl.BlockSpec((tokens, HD), lambda k: (0, k)),
            pl.BlockSpec((tokens, HD), lambda k: (0, k)),
            pl.BlockSpec((tokens, HD), lambda k: (0, k)),
            pl.BlockSpec((tokens, HD), lambda k: (0, kv_count + k)),
        ]
        + [whole((devices // NEAR, packed_rows, HD))] * NEAR,
        out_specs=pl.BlockSpec((tokens, group_size * HD), lambda k: (0, k)),
        out_shape=jax.ShapeDtypeStruct(queries.shape, BF16),
        scratch_shapes=[pltpu.VMEM((tokens, 2 * tokens), F32)],
        compiler_params=params(),
        name="attend",
    )(start, queries, answer_keys, answer_values, prior, prior, *gathered)

    mixer_out = pl.pallas_call(
        functools.partial(final_kernel, state_rows=state_rows, **sizes),
        grid=(groups,),
        in_specs=[
            whole((tokens, LANES)),
            whole((tokens, 2 * heads)),
            pl.BlockSpec((state, width), lambda g: (0, g)),
            pl.BlockSpec((16, 2 * heads), lambda g: (0, columns // (2 * heads))),
            by_group(tokens),
            wide,
            wide,
            pl.BlockSpec((1, width), lambda g: (0, g)),
        ]
        + [pl.BlockSpec((devices // groups // NEAR, packed_rows, HD), lambda g: (g, 0, 0))] * NEAR,
        out_specs=wide,
        out_shape=jax.ShapeDtypeStruct((tokens, columns), BF16),
        compiler_params=params(),
        name="final",
    )(start, level, tail, tail, state_read, inner, gate_input, gain, *gathered)
    return (mixer_out, attention_out)


def solution(mesh):
    rows = P(("group", "reader"), None)
    in_specs = (P("group"),) + (rows,) * 5 + (P(),) * 3 + (rows,) * 6
    return jax.shard_map(
        local, mesh=mesh, in_specs=in_specs, out_specs=(rows, rows), check_vma=False
    )
```

```python
import functools
import math

import jax
import jax.numpy as jnp
from jax import lax
from jax.experimental import pallas as pl
from jax.experimental.pallas import tpu as pltpu
from jax.sharding import PartitionSpec as P

HD = 128
LANES = 128
NEAR = 4
LOG2E = 1.4426950408889634
F32 = jnp.float32
BF16 = jnp.bfloat16
MIB = 1 << 20


def iota(shape, dim):
    return lax.broadcasted_iota(jnp.int32, shape, dim)


def dot(a, b, ca=1, cb=0):
    return lax.dot_general(a, b, (((ca,), (cb,)), ((), ())), preferred_element_type=F32)


def expander(heads, group, per_group, channels):
    shape = (2 * heads, per_group * channels)
    row = iota(shape, 0)
    head = jnp.where(row >= heads, row - heads, row) - group * per_group
    column = iota(shape, 1)
    first = head * channels
    return jnp.where((column >= first) & (column < first + channels), 1.0, 0.0).astype(BF16)


def two_parts(value, heads):
    high = value.astype(BF16).astype(F32)
    return jnp.where(iota(value.shape, 1) < heads, high, value - high).astype(BF16)


def pack_kernel(state_ref, keys_ref, values_ref, near_keys_ref, near_values_ref, out_ref, near_ref):
    rows = state_ref.shape[0]
    state = state_ref[...].astype(BF16)
    parts = []
    for ref in (keys_ref, values_ref):
        wide = ref[...].astype(F32)
        for head in range(wide.shape[1] // HD):
            parts.append(wide[:, head * HD : (head + 1) * HD])
    parts = jnp.concatenate(parts, axis=0).astype(BF16)
    for copy in range(out_ref.shape[0]):
        out_ref[copy, :rows, :] = state
        out_ref[copy, rows:, :] = parts
    width = near_keys_ref.shape[1]
    near_ref[:, :width] = near_keys_ref[...]
    near_ref[:, width:] = near_values_ref[...]


def tail_kernel(
    lengths_ref,
    raw_ref,
    rate_ref,
    x_ref,
    write_ref,
    tail_ref,
    level_ref,
    column_ref,
    start_ref,
    weight_ref,
    *,
    heads,
    per_group,
    channels,
):
    group = pl.program_id(0)
    tokens = x_ref.shape[0]
    columns = heads * channels

    @pl.when(group == 0)
    def _():
        base = (lax.axis_index("reader") * tokens).astype(F32)
        lengths = lengths_ref[...].astype(F32)
        answers = lengths.shape[1]
        square = (answers, answers)
        ends = jnp.sum(
            jnp.where(iota(square, 1) <= iota(square, 0), lengths, 0.0), axis=1, keepdims=True
        )
        place = base + iota((1, tokens), 1).astype(F32)
        start = jnp.max(jnp.where(ends <= place, ends, 0.0), axis=0, keepdims=True) - base
        start = jnp.broadcast_to(start, (LANES, tokens)).T
        start_ref[...] = start
        wide = jnp.concatenate([start] * (tokens // LANES), axis=1)
        square = (tokens, tokens)
        source = iota(square, 1)
        mask = (source.astype(F32) >= wide) & (source <= iota(square, 0))
        mask = jnp.where(mask, 1.0, 0.0).astype(BF16)
        raw = raw_ref[...]
        rate = jnp.broadcast_to(rate_ref[...], (heads, heads))
        diagonal = iota((heads, heads), 0) == iota((heads, heads), 1)
        rate = jnp.sum(jnp.where(diagonal, rate, 0.0), axis=1, keepdims=True)
        step = jnp.maximum(raw, 0.0) + jnp.log1p(jnp.exp(-jnp.abs(raw)))
        falling = -rate * step
        first = falling.astype(BF16)
        rest = falling - first.astype(F32)
        second = rest.astype(BF16)
        third = (rest - second.astype(F32)).astype(BF16)
        level = dot(first, mask, 1, 1) + (dot(second, mask, 1, 1) + dot(third, mask, 1, 1))
        column_ref[...] = level * LOG2E - jnp.log(step) * LOG2E
        level = jnp.concatenate([level, level], axis=0).T
        step = jnp.concatenate([step, step], axis=0).T
        level_ref[...] = level
        last = level[tokens - 1 :, :]
        own = iota((tokens, 2 * heads), 0).astype(F32) >= start[tokens - 1 :, : 2 * heads]
        weight = jnp.where(own, jnp.exp(last - level) * step, 0.0)
        weight_ref[...] = two_parts(weight, heads)
        decay = jnp.exp(jnp.broadcast_to(last, (16, 2 * heads)))
        high = decay.astype(BF16).astype(F32)
        row = iota(decay.shape, 0)
        decay = jnp.where(row == 0, high, jnp.where(row == 1, decay - high, 0.0))
        tail_ref[:, columns:] = jnp.zeros((tail_ref.shape[0], 2 * heads), BF16)
        tail_ref[:16, columns:] = decay.astype(BF16)

    spread = expander(heads, group, per_group, channels)
    weight = dot(weight_ref[...], spread)
    weighted = (x_ref[...].astype(F32) * weight).astype(BF16)
    width = per_group * channels
    tail_ref[:, pl.ds(pl.multiple_of(group * width, width), width)] = dot(
        write_ref[...], weighted, 0, 0
    ).astype(BF16)


def inner_kernel(
    start_ref,
    level_ref,
    column_ref,
    skip_ref,
    x_ref,
    write_ref,
    read_ref,
    *rest,
    first,
    heads,
    per_group,
    channels,
):
    out_ref = rest[-1]
    group = first + pl.program_id(0)
    tokens = x_ref.shape[0]
    both = dot(read_ref[...], write_ref[...], 1, 1)
    square = (tokens, tokens)
    source = iota(square, 1)
    wide = jnp.concatenate([start_ref[...]] * (tokens // LANES), axis=1)
    both = jnp.where((source.astype(F32) >= wide) & (source <= iota(square, 0)), both, 0.0)
    lanes = level_ref.shape[1]
    level = pltpu.roll(level_ref[...] * LOG2E, lanes - group * per_group, 1)
    skip = jnp.concatenate([skip_ref[...]] * 2, axis=1)
    skip = two_parts(jnp.broadcast_to(skip, (16, 2 * heads)), heads)
    skip = dot(skip, expander(heads, group, per_group, channels))[:1, :]
    per_tile = LANES // channels
    lane = iota((LANES, LANES), 1)
    for tile in range(per_group // per_tile):
        at = slice(tile * LANES, (tile + 1) * LANES)
        x = x_ref[:, at]
        for block in range(tokens // LANES):
            rows = slice(block * LANES, (block + 1) * LANES)
            reach = (block + 1) * LANES
            total = None
            for part in range(per_tile):
                head = tile * per_tile + part
                gap = level[rows, head : head + 1] - column_ref[head : head + 1, :reach]
                mixing = (jnp.exp2(jnp.minimum(gap, 64.0)) * both[rows, :reach]).astype(BF16)
                result = dot(mixing, x[:reach, :])
                total = result if total is None else jnp.where(
                    lane < part * channels, total, result
                )
            total = total + skip[:, at] * x[rows, :].astype(F32)
            out_ref[rows, at] = total.astype(BF16)


def attend_kernel(
    start_ref,
    query_ref,
    key_ref,
    value_ref,
    prior_key_ref,
    prior_value_ref,
    *rest,
    state_rows,
    prompt_rows,
    kv_count,
):
    gathered, (out_ref, bias_ref) = rest[:-2], rest[-2:]
    head = pl.program_id(0)
    tokens = query_ref.shape[0]
    devices = len(gathered) * gathered[0].shape[0]
    scale = LOG2E / math.sqrt(HD)

    @pl.when(head == 0)
    def _():
        shape = (tokens, 2 * tokens)
        place = iota(shape, 1) - tokens
        wide = jnp.concatenate([start_ref[...]] * (2 * tokens // LANES), axis=1)
        allowed = (place.astype(F32) >= wide) & (place <= iota(shape, 0))
        bias_ref[...] = jnp.where(allowed, 0.0, -jnp.inf)

    def prompt(which):
        at = pl.multiple_of(state_rows + (which * kv_count + head) // 2 * 2 * prompt_rows, 16)
        at = pl.ds(at, 2 * prompt_rows)
        pair = jnp.concatenate([ref[:, at, :] for ref in gathered], axis=0).astype(F32)
        odd = lax.rem(head, 2) == 1
        part = jnp.where(odd, pair[:, prompt_rows:, :], pair[:, :prompt_rows, :])
        return part.reshape(devices * prompt_rows, HD).astype(BF16)

    prompt_keys = prompt(0)
    ones = jnp.ones((tokens, LANES), BF16)
    prompt_values = prompt(1)
    prompt_values = jnp.concatenate(
        [prompt_values, jnp.ones((prompt_values.shape[0], LANES), BF16)], axis=1
    )
    near_keys = jnp.concatenate([prior_key_ref[...], key_ref[...]], axis=0)
    near_values = [prior_value_ref[...], value_ref[...]]
    near_values = jnp.concatenate(
        [jnp.concatenate(near_values, axis=0), jnp.concatenate([ones, ones], axis=0)], axis=1
    )
    for query in range(query_ref.shape[1] // HD):
        at = slice(query * HD, (query + 1) * HD)
        for block in range(tokens // LANES):
            rows = slice(block * LANES, (block + 1) * LANES)
            reach = tokens + (block + 1) * LANES
            q = query_ref[rows, at]
            far = dot(q, prompt_keys, 1, 1)
            near = dot(q, near_keys[:reach, :], 1, 1) + bias_ref[rows, :reach]
            top = jnp.maximum(
                jnp.max(far, axis=1, keepdims=True), jnp.max(near, axis=1, keepdims=True)
            )
            far = jnp.exp2((far - top) * scale).astype(BF16)
            near = jnp.exp2((near - top) * scale).astype(BF16)
            summed = dot(far, prompt_values) + dot(near, near_values[:reach, :])
            out_ref[rows, at] = (summed[:, :HD] / summed[:, HD:]).astype(BF16)


def final_kernel(
    start_ref,
    level_ref,
    tail_ref,
    decay_ref,
    read_ref,
    inner_ref,
    gate_ref,
    gain_ref,
    *rest,
    state_rows,
    heads,
    per_group,
    channels,
):
    gathered, out_ref = rest[:-1], rest[-1]
    group = pl.program_id(0)
    level = jnp.exp(level_ref[...])
    carried = start_ref[:, : 2 * heads] < 0
    decay = decay_ref[...].astype(F32)
    decay = decay[0:1, :] + decay[1:2, :]
    spread = expander(heads, group, per_group, channels)
    from_prompt = dot(two_parts(jnp.where(carried, level * decay, level), heads), spread)
    from_prior = dot(two_parts(jnp.where(carried, level, 0.0), heads), spread)
    own = lax.rem(lax.axis_index("reader"), NEAR)
    seeds = []
    for run in range(gathered[0].shape[0]):
        parts = [ref[run, :state_rows, :] for ref in gathered]
        bit = 1
        while bit < NEAR:
            swap = lax.rem(own // bit, 2) == 1
            parts = [jnp.where(swap, parts[i ^ bit], parts[i]) for i in range(NEAR)]
            bit *= 2
        seeds += parts
    seeds = jnp.concatenate(seeds, axis=0)
    read = read_ref[...]
    mixed = inner_ref[...].astype(F32)
    mixed = mixed + from_prompt * dot(read, seeds, 1, 1)
    mixed = mixed + from_prior * dot(read, tail_ref[...])
    gate = gate_ref[...].astype(F32)
    gated = mixed * (gate * (0.5 + 0.5 * jnp.tanh(0.5 * gate)))
    scale = lax.rsqrt(jnp.mean(gated * gated, axis=1, keepdims=True) + 1e-05)
    out_ref[...] = (gated * scale * gain_ref[...]).astype(BF16)


def shifted(value, axis, by):
    length = lax.axis_size(axis)
    return lax.ppermute(value, axis, [(i, i + by) for i in range(length - by)])


def params(limit=32):
    return pltpu.CompilerParams(vmem_limit_bytes=limit * MIB)


def whole(shape):
    return pl.BlockSpec(shape, lambda g: (0,) * len(shape))


def local(
    answer_lengths,
    mixer_input,
    gate_input,
    state_write,
    state_read,
    step_raw,
    decay_rate,
    skip_gain,
    norm_gain,
    prompt_state,
    queries,
    answer_keys,
    answer_values,
    prompt_keys,
    prompt_values,
):
    tokens, columns = mixer_input.shape
    heads = decay_rate.shape[0]
    state_rows, state = prompt_state.shape
    groups = state_write.shape[1] // state
    per_group = heads // groups
    channels = columns // heads
    width = per_group * channels
    prompt_rows, kv_width = prompt_keys.shape
    kv_count = kv_width // HD
    devices = lax.axis_size("reader")
    in_hbm = lambda value: pltpu.with_memory_space_constraint(value, pltpu.MemorySpace.HBM)
    mixer_input, gate_input, state_write, state_read = map(
        in_hbm, (mixer_input, gate_input, state_write, state_read)
    )
    prompt_state, queries, answer_keys, answer_values, prompt_keys, prompt_values = map(
        in_hbm, (prompt_state, queries, answer_keys, answer_values, prompt_keys, prompt_values)
    )
    lengths, rate, skip, gain = map(
        lambda value: in_hbm(value.reshape(1, -1)),
        (answer_lengths, decay_rate, skip_gain, norm_gain),
    )
    sizes = dict(heads=heads, per_group=per_group, channels=channels)
    packed_rows = state_rows + 2 * prompt_rows * kv_count

    packed, near = pl.pallas_call(
        pack_kernel,
        out_shape=(
            jax.ShapeDtypeStruct((devices // NEAR, packed_rows, HD), BF16),
            jax.ShapeDtypeStruct((tokens, 2 * kv_width), BF16),
        ),
        compiler_params=params(),
        name="pack",
    )(prompt_state, prompt_keys, prompt_values, answer_keys, answer_values)
    packed, raw = lax.optimization_barrier((packed, step_raw.T))
    lines = [list(range(first, devices, NEAR)) for first in range(NEAR)]
    line = lax.all_to_all(packed, "reader", 0, 0, axis_index_groups=lines, tiled=True)
    prior = shifted(near, "reader", 1)
    exchanged = lambda value, bit: lax.ppermute(
        value, "reader", [(i, i ^ bit) for i in range(devices)]
    )
    raw = in_hbm(raw)

    by_group = lambda rows: pl.BlockSpec((rows, state), lambda g: (0, g))
    wide = pl.BlockSpec((tokens, width), lambda g: (0, g))
    tail, level, column, start = pl.pallas_call(
        functools.partial(tail_kernel, **sizes),
        grid=(groups,),
        in_specs=[
            whole(lengths.shape),
            whole(raw.shape),
            whole((1, heads)),
            wide,
            by_group(tokens),
        ],
        out_specs=(
            whole((state, columns + 2 * heads)),
            whole((tokens, 2 * heads)),
            whole((heads, tokens)),
            whole((tokens, LANES)),
        ),
        out_shape=(
            jax.ShapeDtypeStruct((state, columns + 2 * heads), BF16),
            jax.ShapeDtypeStruct((tokens, 2 * heads), F32),
            jax.ShapeDtypeStruct((heads, tokens), F32),
            jax.ShapeDtypeStruct((tokens, LANES), F32),
        ),
        scratch_shapes=[pltpu.VMEM((tokens, 2 * heads), BF16)],
        compiler_params=params(),
        name="tail",
    )(lengths, raw, rate, mixer_input, state_write)

    prior, line, column = lax.optimization_barrier((prior, line, column))

    def inner_part(first, count, *earlier):
        blocks = lambda rows, columns: pl.BlockSpec((rows, columns), lambda g: (0, first + g))
        return pl.pallas_call(
            functools.partial(inner_kernel, first=first, **sizes),
            grid=(count,),
            in_specs=[
                whole((tokens, LANES)),
                whole((tokens, 2 * heads)),
                pl.BlockSpec((per_group, tokens), lambda g: (first + g, 0)),
                whole((1, heads)),
                blocks(tokens, width),
                blocks(tokens, state),
                blocks(tokens, state),
            ]
            + [pl.BlockSpec(memory_space=pl.ANY)] * len(earlier),
            out_specs=blocks(tokens, width),
            out_shape=jax.ShapeDtypeStruct((tokens, columns), BF16),
            input_output_aliases={7: 0} if earlier else {},
            compiler_params=params(),
            cost_estimate=pl.CostEstimate(
                flops=count * per_group * tokens * tokens * channels * 8,
                bytes_accessed=count * tokens * width * 4,
                transcendentals=count * per_group * tokens * tokens,
            ),
            name="inner",
        )(start, level, column, skip, mixer_input, state_write, state_read, *earlier)

    half = groups // 2
    inner = inner_part(0, half)
    across = exchanged(line, 2)
    tail, inner = lax.optimization_barrier((tail, inner))
    tail = shifted(tail, "reader", 1)
    across, inner = lax.optimization_barrier((across, inner))
    gathered = (line, exchanged(line, 1), across, exchanged(across, 1))
    inner = inner_part(half, groups - half, inner)
    group_size = queries.shape[1] // kv_width
    attention_out = pl.pallas_call(
        functools.partial(
            attend_kernel,
            state_rows=state_rows,
            prompt_rows=prompt_rows,
            kv_count=kv_count,
        ),
        grid=(kv_count,),
        in_specs=[
            whole((tokens, LANES)),
            pl.BlockSpec((tokens, group_size * HD), lambda k: (0, k)),
            pl.BlockSpec((tokens, HD), lambda k: (0, k)),
            pl.BlockSpec((tokens, HD), lambda k: (0, k)),
            pl.BlockSpec((tokens, HD), lambda k: (0, k)),
            pl.BlockSpec((tokens, HD), lambda k: (0, kv_count + k)),
        ]
        + [whole((devices // NEAR, packed_rows, HD))] * NEAR,
        out_specs=pl.BlockSpec((tokens, group_size * HD), lambda k: (0, k)),
        out_shape=jax.ShapeDtypeStruct(queries.shape, BF16),
        scratch_shapes=[pltpu.VMEM((tokens, 2 * tokens), F32)],
        compiler_params=params(),
        name="attend",
    )(start, queries, answer_keys, answer_values, prior, prior, *gathered)

    mixer_out = pl.pallas_call(
        functools.partial(final_kernel, state_rows=state_rows, **sizes),
        grid=(groups,),
        in_specs=[
            whole((tokens, LANES)),
            whole((tokens, 2 * heads)),
            pl.BlockSpec((state, width), lambda g: (0, g)),
            pl.BlockSpec((16, 2 * heads), lambda g: (0, columns // (2 * heads))),
            by_group(tokens),
            wide,
            wide,
            pl.BlockSpec((1, width), lambda g: (0, g)),
        ]
        + [pl.BlockSpec((devices // groups // NEAR, packed_rows, HD), lambda g: (g, 0, 0))] * NEAR,
        out_specs=wide,
        out_shape=jax.ShapeDtypeStruct((tokens, columns), BF16),
        compiler_params=params(),
        name="final",
    )(start, level, tail, tail, state_read, inner, gate_input, gain, *gathered)
    return (mixer_out, attention_out)


def solution(mesh):
    rows = P(("group", "reader"), None)
    in_specs = (P("group"),) + (rows,) * 5 + (P(),) * 3 + (rows,) * 6
    return jax.shard_map(
        local, mesh=mesh, in_specs=in_specs, out_specs=(rows, rows), check_vma=False
    )
```

```python
import functools
import math

import jax
import jax.numpy as jnp
from jax import lax
from jax.experimental import pallas as pl
from jax.experimental.pallas import tpu as pltpu
from jax.sharding import PartitionSpec as P

HD = 128
LANES = 128
NEAR = 2
LOG2E = 1.4426950408889634
F32 = jnp.float32
BF16 = jnp.bfloat16
MIB = 1 << 20


def iota(shape, dim):
    return lax.broadcasted_iota(jnp.int32, shape, dim)


def dot(a, b, ca=1, cb=0):
    return lax.dot_general(a, b, (((ca,), (cb,)), ((), ())), preferred_element_type=F32)


def expander(heads, group, per_group, channels):
    shape = (2 * heads, per_group * channels)
    row = iota(shape, 0)
    head = jnp.where(row >= heads, row - heads, row) - group * per_group
    column = iota(shape, 1)
    first = head * channels
    return jnp.where((column >= first) & (column < first + channels), 1.0, 0.0).astype(BF16)


def two_parts(value, heads):
    high = value.astype(BF16).astype(F32)
    return jnp.where(iota(value.shape, 1) < heads, high, value - high).astype(BF16)


def pack_kernel(state_ref, keys_ref, values_ref, near_keys_ref, near_values_ref, out_ref, near_ref):
    rows = state_ref.shape[0]
    state = state_ref[...].astype(BF16)
    parts = []
    for ref in (keys_ref, values_ref):
        wide = ref[...].astype(F32)
        for head in range(wide.shape[1] // HD):
            parts.append(wide[:, head * HD : (head + 1) * HD])
    parts = jnp.concatenate(parts, axis=0).astype(BF16)
    for copy in range(out_ref.shape[0]):
        out_ref[copy, :rows, :] = state
        out_ref[copy, rows:, :] = parts
    width = near_keys_ref.shape[1]
    near_ref[:, :width] = near_keys_ref[...]
    near_ref[:, width:] = near_values_ref[...]


def tail_kernel(
    lengths_ref,
    raw_ref,
    rate_ref,
    x_ref,
    write_ref,
    tail_ref,
    level_ref,
    column_ref,
    start_ref,
    weight_ref,
    *,
    heads,
    per_group,
    channels,
):
    group = pl.program_id(0)
    tokens = x_ref.shape[0]
    columns = heads * channels

    @pl.when(group == 0)
    def _():
        base = (lax.axis_index("reader") * tokens).astype(F32)
        lengths = lengths_ref[...].astype(F32)
        answers = lengths.shape[1]
        square = (answers, answers)
        ends = jnp.sum(
            jnp.where(iota(square, 1) <= iota(square, 0), lengths, 0.0), axis=1, keepdims=True
        )
        place = base + iota((1, tokens), 1).astype(F32)
        start = jnp.max(jnp.where(ends <= place, ends, 0.0), axis=0, keepdims=True) - base
        start = jnp.broadcast_to(start, (LANES, tokens)).T
        start_ref[...] = start
        wide = jnp.concatenate([start] * (tokens // LANES), axis=1)
        square = (tokens, tokens)
        source = iota(square, 1)
        mask = (source.astype(F32) >= wide) & (source <= iota(square, 0))
        mask = jnp.where(mask, 1.0, 0.0).astype(BF16)
        raw = raw_ref[...]
        rate = jnp.broadcast_to(rate_ref[...], (heads, heads))
        diagonal = iota((heads, heads), 0) == iota((heads, heads), 1)
        rate = jnp.sum(jnp.where(diagonal, rate, 0.0), axis=1, keepdims=True)
        step = jnp.maximum(raw, 0.0) + jnp.log1p(jnp.exp(-jnp.abs(raw)))
        falling = -rate * step
        first = falling.astype(BF16)
        rest = falling - first.astype(F32)
        second = rest.astype(BF16)
        third = (rest - second.astype(F32)).astype(BF16)
        level = dot(first, mask, 1, 1) + (dot(second, mask, 1, 1) + dot(third, mask, 1, 1))
        column_ref[...] = level * LOG2E - jnp.log(step) * LOG2E
        level = jnp.concatenate([level, level], axis=0).T
        step = jnp.concatenate([step, step], axis=0).T
        level_ref[...] = level
        last = level[tokens - 1 :, :]
        own = iota((tokens, 2 * heads), 0).astype(F32) >= start[tokens - 1 :, : 2 * heads]
        weight = jnp.where(own, jnp.exp(last - level) * step, 0.0)
        weight_ref[...] = two_parts(weight, heads)
        decay = jnp.exp(jnp.broadcast_to(last, (16, 2 * heads)))
        high = decay.astype(BF16).astype(F32)
        row = iota(decay.shape, 0)
        decay = jnp.where(row == 0, high, jnp.where(row == 1, decay - high, 0.0))
        tail_ref[:, columns:] = jnp.zeros((tail_ref.shape[0], 2 * heads), BF16)
        tail_ref[:16, columns:] = decay.astype(BF16)

    spread = expander(heads, group, per_group, channels)
    weight = dot(weight_ref[...], spread)
    weighted = (x_ref[...].astype(F32) * weight).astype(BF16)
    width = per_group * channels
    tail_ref[:, pl.ds(pl.multiple_of(group * width, width), width)] = dot(
        write_ref[...], weighted, 0, 0
    ).astype(BF16)


def inner_kernel(
    start_ref,
    level_ref,
    column_ref,
    skip_ref,
    x_ref,
    write_ref,
    read_ref,
    *rest,
    first,
    heads,
    per_group,
    channels,
):
    out_ref = rest[-1]
    group = first + pl.program_id(0)
    tokens = x_ref.shape[0]
    both = dot(read_ref[...], write_ref[...], 1, 1)
    square = (tokens, tokens)
    source = iota(square, 1)
    wide = jnp.concatenate([start_ref[...]] * (tokens // LANES), axis=1)
    both = jnp.where((source.astype(F32) >= wide) & (source <= iota(square, 0)), both, 0.0)
    lanes = level_ref.shape[1]
    level = pltpu.roll(level_ref[...] * LOG2E, lanes - group * per_group, 1)
    skip = jnp.concatenate([skip_ref[...]] * 2, axis=1)
    skip = two_parts(jnp.broadcast_to(skip, (16, 2 * heads)), heads)
    skip = dot(skip, expander(heads, group, per_group, channels))[:1, :]
    per_tile = LANES // channels
    lane = iota((LANES, LANES), 1)
    for tile in range(per_group // per_tile):
        at = slice(tile * LANES, (tile + 1) * LANES)
        x = x_ref[:, at]
        for block in range(tokens // LANES):
            rows = slice(block * LANES, (block + 1) * LANES)
            reach = (block + 1) * LANES
            total = None
            for part in range(per_tile):
                head = tile * per_tile + part
                gap = level[rows, head : head + 1] - column_ref[head : head + 1, :reach]
                mixing = (jnp.exp2(jnp.minimum(gap, 64.0)) * both[rows, :reach]).astype(BF16)
                result = dot(mixing, x[:reach, :])
                total = result if total is None else jnp.where(
                    lane < part * channels, total, result
                )
            total = total + skip[:, at] * x[rows, :].astype(F32)
            out_ref[rows, at] = total.astype(BF16)


def attend_kernel(
    start_ref,
    query_ref,
    key_ref,
    value_ref,
    prior_key_ref,
    prior_value_ref,
    *rest,
    state_rows,
    prompt_rows,
    kv_count,
):
    gathered, (out_ref, bias_ref) = rest[:-2], rest[-2:]
    head = pl.program_id(0)
    tokens = query_ref.shape[0]
    devices = len(gathered) * gathered[0].shape[0]
    scale = LOG2E / math.sqrt(HD)

    @pl.when(head == 0)
    def _():
        shape = (tokens, 2 * tokens)
        place = iota(shape, 1) - tokens
        wide = jnp.concatenate([start_ref[...]] * (2 * tokens // LANES), axis=1)
        allowed = (place.astype(F32) >= wide) & (place <= iota(shape, 0))
        bias_ref[...] = jnp.where(allowed, 0.0, -jnp.inf)

    def prompt(which):
        at = pl.multiple_of(state_rows + (which * kv_count + head) // 2 * 2 * prompt_rows, 16)
        at = pl.ds(at, 2 * prompt_rows)
        pair = jnp.concatenate([ref[:, at, :] for ref in gathered], axis=0).astype(F32)
        odd = lax.rem(head, 2) == 1
        part = jnp.where(odd, pair[:, prompt_rows:, :], pair[:, :prompt_rows, :])
        return part.reshape(devices * prompt_rows, HD).astype(BF16)

    prompt_keys = prompt(0)
    ones = jnp.ones((tokens, LANES), BF16)
    prompt_values = prompt(1)
    prompt_values = jnp.concatenate(
        [prompt_values, jnp.ones((prompt_values.shape[0], LANES), BF16)], axis=1
    )
    near_keys = jnp.concatenate([prior_key_ref[...], key_ref[...]], axis=0)
    near_values = [prior_value_ref[...], value_ref[...]]
    near_values = jnp.concatenate(
        [jnp.concatenate(near_values, axis=0), jnp.concatenate([ones, ones], axis=0)], axis=1
    )
    for query in range(query_ref.shape[1] // HD):
        at = slice(query * HD, (query + 1) * HD)
        for block in range(tokens // LANES):
            rows = slice(block * LANES, (block + 1) * LANES)
            reach = tokens + (block + 1) * LANES
            q = query_ref[rows, at]
            far = dot(q, prompt_keys, 1, 1)
            near = dot(q, near_keys[:reach, :], 1, 1) + bias_ref[rows, :reach]
            top = jnp.maximum(
                jnp.max(far, axis=1, keepdims=True), jnp.max(near, axis=1, keepdims=True)
            )
            far = jnp.exp2((far - top) * scale).astype(BF16)
            near = jnp.exp2((near - top) * scale).astype(BF16)
            summed = dot(far, prompt_values) + dot(near, near_values[:reach, :])
            out_ref[rows, at] = (summed[:, :HD] / summed[:, HD:]).astype(BF16)


def final_kernel(
    start_ref,
    level_ref,
    tail_ref,
    decay_ref,
    read_ref,
    inner_ref,
    gate_ref,
    gain_ref,
    *rest,
    state_rows,
    heads,
    per_group,
    channels,
):
    gathered, out_ref = rest[:-1], rest[-1]
    group = pl.program_id(0)
    level = jnp.exp(level_ref[...])
    carried = start_ref[:, : 2 * heads] < 0
    decay = decay_ref[...].astype(F32)
    decay = decay[0:1, :] + decay[1:2, :]
    spread = expander(heads, group, per_group, channels)
    from_prompt = dot(two_parts(jnp.where(carried, level * decay, level), heads), spread)
    from_prior = dot(two_parts(jnp.where(carried, level, 0.0), heads), spread)
    own = lax.rem(lax.axis_index("reader"), NEAR)
    seeds = []
    for run in range(gathered[0].shape[0]):
        parts = [ref[run, :state_rows, :] for ref in gathered]
        bit = 1
        while bit < NEAR:
            swap = lax.rem(own // bit, 2) == 1
            parts = [jnp.where(swap, parts[i ^ bit], parts[i]) for i in range(NEAR)]
            bit *= 2
        seeds += parts
    seeds = jnp.concatenate(seeds, axis=0)
    read = read_ref[...]
    mixed = inner_ref[...].astype(F32)
    mixed = mixed + from_prompt * dot(read, seeds, 1, 1)
    mixed = mixed + from_prior * dot(read, tail_ref[...])
    gate = gate_ref[...].astype(F32)
    gated = mixed * (gate * (0.5 + 0.5 * jnp.tanh(0.5 * gate)))
    scale = lax.rsqrt(jnp.mean(gated * gated, axis=1, keepdims=True) + 1e-05)
    out_ref[...] = (gated * scale * gain_ref[...]).astype(BF16)


def shifted(value, axis, by):
    length = lax.axis_size(axis)
    return lax.ppermute(value, axis, [(i, i + by) for i in range(length - by)])


def params(limit=32):
    return pltpu.CompilerParams(vmem_limit_bytes=limit * MIB)


def whole(shape):
    return pl.BlockSpec(shape, lambda g: (0,) * len(shape))


def local(
    answer_lengths,
    mixer_input,
    gate_input,
    state_write,
    state_read,
    step_raw,
    decay_rate,
    skip_gain,
    norm_gain,
    prompt_state,
    queries,
    answer_keys,
    answer_values,
    prompt_keys,
    prompt_values,
):
    tokens, columns = mixer_input.shape
    heads = decay_rate.shape[0]
    state_rows, state = prompt_state.shape
    groups = state_write.shape[1] // state
    per_group = heads // groups
    channels = columns // heads
    width = per_group * channels
    prompt_rows, kv_width = prompt_keys.shape
    kv_count = kv_width // HD
    devices = lax.axis_size("reader")
    in_hbm = lambda value: pltpu.with_memory_space_constraint(value, pltpu.MemorySpace.HBM)
    mixer_input, gate_input, state_write, state_read = map(
        in_hbm, (mixer_input, gate_input, state_write, state_read)
    )
    prompt_state, queries, answer_keys, answer_values, prompt_keys, prompt_values = map(
        in_hbm, (prompt_state, queries, answer_keys, answer_values, prompt_keys, prompt_values)
    )
    lengths, rate, skip, gain = map(
        lambda value: in_hbm(value.reshape(1, -1)),
        (answer_lengths, decay_rate, skip_gain, norm_gain),
    )
    sizes = dict(heads=heads, per_group=per_group, channels=channels)
    packed_rows = state_rows + 2 * prompt_rows * kv_count

    packed, near = pl.pallas_call(
        pack_kernel,
        out_shape=(
            jax.ShapeDtypeStruct((devices // NEAR, packed_rows, HD), BF16),
            jax.ShapeDtypeStruct((tokens, 2 * kv_width), BF16),
        ),
        compiler_params=params(),
        name="pack",
    )(prompt_state, prompt_keys, prompt_values, answer_keys, answer_values)
    packed, raw = lax.optimization_barrier((packed, step_raw.T))
    lines = [list(range(first, devices, NEAR)) for first in range(NEAR)]
    line = lax.all_to_all(packed, "reader", 0, 0, axis_index_groups=lines, tiled=True)
    prior = shifted(near, "reader", 1)
    raw = in_hbm(raw)

    by_group = lambda rows: pl.BlockSpec((rows, state), lambda g: (0, g))
    wide = pl.BlockSpec((tokens, width), lambda g: (0, g))
    tail, level, column, start = pl.pallas_call(
        functools.partial(tail_kernel, **sizes),
        grid=(groups,),
        in_specs=[
            whole(lengths.shape),
            whole(raw.shape),
            whole((1, heads)),
            wide,
            by_group(tokens),
        ],
        out_specs=(
            whole((state, columns + 2 * heads)),
            whole((tokens, 2 * heads)),
            whole((heads, tokens)),
            whole((tokens, LANES)),
        ),
        out_shape=(
            jax.ShapeDtypeStruct((state, columns + 2 * heads), BF16),
            jax.ShapeDtypeStruct((tokens, 2 * heads), F32),
            jax.ShapeDtypeStruct((heads, tokens), F32),
            jax.ShapeDtypeStruct((tokens, LANES), F32),
        ),
        scratch_shapes=[pltpu.VMEM((tokens, 2 * heads), BF16)],
        compiler_params=params(),
        name="tail",
    )(lengths, raw, rate, mixer_input, state_write)

    tail = shifted(tail, "reader", 1)
    prior, column = lax.optimization_barrier((prior, column))

    def inner_part(first, count, *earlier):
        blocks = lambda rows, columns: pl.BlockSpec((rows, columns), lambda g: (0, first + g))
        return pl.pallas_call(
            functools.partial(inner_kernel, first=first, **sizes),
            grid=(count,),
            in_specs=[
                whole((tokens, LANES)),
                whole((tokens, 2 * heads)),
                pl.BlockSpec((per_group, tokens), lambda g: (first + g, 0)),
                whole((1, heads)),
                blocks(tokens, width),
                blocks(tokens, state),
                blocks(tokens, state),
            ]
            + [pl.BlockSpec(memory_space=pl.ANY)] * len(earlier),
            out_specs=blocks(tokens, width),
            out_shape=jax.ShapeDtypeStruct((tokens, columns), BF16),
            input_output_aliases={7: 0} if earlier else {},
            compiler_params=params(),
            cost_estimate=pl.CostEstimate(
                flops=count * per_group * tokens * tokens * channels * 8,
                bytes_accessed=count * tokens * width * 4,
                transcendentals=count * per_group * tokens * tokens,
            ),
            name="inner",
        )(start, level, column, skip, mixer_input, state_write, state_read, *earlier)

    inner = inner_part(0, groups - 1)
    line, inner = lax.optimization_barrier((line, inner))
    exchanged = lax.ppermute(line, "reader", [(i, i ^ 1) for i in range(devices)])
    gathered = (line, exchanged)
    inner = inner_part(groups - 1, 1, inner)
    group_size = queries.shape[1] // kv_width
    attention_out = pl.pallas_call(
        functools.partial(
            attend_kernel,
            state_rows=state_rows,
            prompt_rows=prompt_rows,
            kv_count=kv_count,
        ),
        grid=(kv_count,),
        in_specs=[
            whole((tokens, LANES)),
            pl.BlockSpec((tokens, group_size * HD), lambda k: (0, k)),
            pl.BlockSpec((tokens, HD), lambda k: (0, k)),
            pl.BlockSpec((tokens, HD), lambda k: (0, k)),
            pl.BlockSpec((tokens, HD), lambda k: (0, k)),
            pl.BlockSpec((tokens, HD), lambda k: (0, kv_count + k)),
        ]
        + [whole((devices // NEAR, packed_rows, HD))] * NEAR,
        out_specs=pl.BlockSpec((tokens, group_size * HD), lambda k: (0, k)),
        out_shape=jax.ShapeDtypeStruct(queries.shape, BF16),
        scratch_shapes=[pltpu.VMEM((tokens, 2 * tokens), F32)],
        compiler_params=params(),
        name="attend",
    )(start, queries, answer_keys, answer_values, prior, prior, *gathered)

    mixer_out = pl.pallas_call(
        functools.partial(final_kernel, state_rows=state_rows, **sizes),
        grid=(groups,),
        in_specs=[
            whole((tokens, LANES)),
            whole((tokens, 2 * heads)),
            pl.BlockSpec((state, width), lambda g: (0, g)),
            pl.BlockSpec((16, 2 * heads), lambda g: (0, columns // (2 * heads))),
            by_group(tokens),
            wide,
            wide,
            pl.BlockSpec((1, width), lambda g: (0, g)),
        ]
        + [pl.BlockSpec((devices // groups // NEAR, packed_rows, HD), lambda g: (g, 0, 0))] * NEAR,
        out_specs=wide,
        out_shape=jax.ShapeDtypeStruct((tokens, columns), BF16),
        compiler_params=params(),
        name="final",
    )(start, level, tail, tail, state_read, inner, gate_input, gain, *gathered)
    return (mixer_out, attention_out)


def solution(mesh):
    rows = P(("group", "reader"), None)
    in_specs = (P("group"),) + (rows,) * 5 + (P(),) * 3 + (rows,) * 6
    return jax.shard_map(
        local, mesh=mesh, in_specs=in_specs, out_specs=(rows, rows), check_vma=False
    )
```

```python
import functools
import math

import jax
import jax.numpy as jnp
from jax import lax
from jax.experimental import pallas as pl
from jax.experimental.pallas import tpu as pltpu
from jax.sharding import PartitionSpec as P

HD = 128
LANES = 128
WIDE = 256
NEAR = 2
LOG2E = 1.4426950408889634
F32 = jnp.float32
BF16 = jnp.bfloat16
MIB = 1 << 20


def iota(shape, dim):
    return lax.broadcasted_iota(jnp.int32, shape, dim)


def dot(a, b, ca=1, cb=0):
    return lax.dot_general(a, b, (((ca,), (cb,)), ((), ())), preferred_element_type=F32)


def expander(heads, group, per_group, channels):
    shape = (2 * heads, per_group * channels)
    row = iota(shape, 0)
    head = jnp.where(row >= heads, row - heads, row) - group * per_group
    column = iota(shape, 1)
    first = head * channels
    return jnp.where((column >= first) & (column < first + channels), 1.0, 0.0).astype(BF16)


def two_parts(value, heads):
    high = value.astype(BF16).astype(F32)
    return jnp.where(iota(value.shape, 1) < heads, high, value - high)


def to_front(value, head):
    return pltpu.roll(value, value.shape[1] - head, 1)


def spread(value, first, channels):
    lane = iota(value.shape, 1)
    source = sum(
        [jnp.where(lane >= part * channels, 1, 0) for part in range(1, LANES // channels)],
        jnp.full(value.shape, first, jnp.int32),
    )
    return jnp.take_along_axis(value, source, axis=1, mode="promise_in_bounds")


def pack_kernel(
    state_ref,
    keys_ref,
    values_ref,
    near_keys_ref,
    near_values_ref,
    out_ref,
    near_ref,
    own_state_ref,
    own_keys_ref,
    own_values_ref,
    held_ref,
    in_sems,
    near_sems,
    out_sems,
):
    width = near_keys_ref.shape[1]
    loads = [
        pltpu.make_async_copy(source, target, in_sems.at[place])
        for place, (source, target) in enumerate(
            ((state_ref, own_state_ref), (keys_ref, own_keys_ref), (values_ref, own_values_ref))
        )
    ]
    for load in loads:
        load.start()
    moves = [
        pltpu.make_async_copy(ref, near_ref.at[:, part * width : (part + 1) * width], near_sems.at[part])
        for part, ref in enumerate((near_keys_ref, near_values_ref))
    ]
    for move in moves:
        move.start()
    for load in loads:
        load.wait()
    rows = own_state_ref.shape[0]
    held_ref[:rows, :] = own_state_ref[...].astype(BF16)
    parts = []
    for ref in (own_keys_ref, own_values_ref):
        wide = ref[...].astype(F32)
        for head in range(wide.shape[1] // HD):
            parts.append(wide[:, head * HD : (head + 1) * HD])
    held_ref[rows:, :] = jnp.concatenate(parts, axis=0).astype(BF16)
    copies = [
        pltpu.make_async_copy(held_ref, out_ref.at[copy], out_sems.at[copy])
        for copy in range(out_ref.shape[0])
    ]
    for copy in copies:
        copy.start()
    for move in moves + copies:
        move.wait()


def level_part(lengths_ref, raw_ref, rate_ref, level_ref, column_ref, start_ref, weight_ref, tail_ref):
    heads, tokens = raw_ref.shape
    base = (lax.axis_index("reader") * tokens).astype(F32)
    lengths = lengths_ref[...].astype(F32)
    answers = lengths.shape[1]
    square = (answers, answers)
    ends = jnp.sum(
        jnp.where(iota(square, 1) <= iota(square, 0), lengths, 0.0), axis=1, keepdims=True
    )
    place = base + iota((1, tokens), 1).astype(F32)
    start = jnp.max(jnp.where(ends <= place, ends, 0.0), axis=0, keepdims=True) - base
    start = jnp.broadcast_to(start, (LANES, tokens)).T
    start_ref[...] = start
    wide = jnp.concatenate([start] * (tokens // LANES), axis=1)
    square = (tokens, tokens)
    source = iota(square, 1)
    mask = (source.astype(F32) >= wide) & (source <= iota(square, 0))
    mask = jnp.where(mask, 1.0, 0.0).astype(BF16)
    raw = raw_ref[...]
    rate = jnp.broadcast_to(rate_ref[...], (heads, heads))
    diagonal = iota((heads, heads), 0) == iota((heads, heads), 1)
    rate = jnp.sum(jnp.where(diagonal, rate, 0.0), axis=1, keepdims=True)
    step = jnp.maximum(raw, 0.0) + jnp.log1p(jnp.exp(-jnp.abs(raw)))
    falling = -rate * step
    first = falling.astype(BF16)
    rest = falling - first.astype(F32)
    second = rest.astype(BF16)
    third = (rest - second.astype(F32)).astype(BF16)
    level = dot(first, mask, 1, 1) + (dot(second, mask, 1, 1) + dot(third, mask, 1, 1))
    column_ref[...] = level * LOG2E - jnp.log(step) * LOG2E
    last = level[:, tokens - 1 :]
    decay = jnp.exp(jnp.broadcast_to(last, (heads, tail_ref.shape[1])))
    high = decay.astype(BF16)
    low = (decay - high.astype(F32)).astype(BF16)
    tail_ref[tail_ref.shape[0] - 2 * heads :, :] = jnp.concatenate([high, low], axis=0)
    own = iota((heads, tokens), 1).astype(F32) >= start[tokens - 1 :, :1]
    weight = jnp.where(own, jnp.exp(last - level) * step, 0.0)
    weight_ref[...] = jnp.concatenate([weight, weight], axis=0).T
    level_ref[...] = jnp.concatenate([level, level], axis=0).T


def tail_part(group, at, weight_ref, x_ref, write_ref, tail_ref, per_group, channels):
    tokens, width = x_ref.shape
    weight = to_front(weight_ref[...], group * per_group)
    weighted = []
    for tile in range(width // LANES):
        scale = spread(weight, tile * LANES // channels, channels)
        x = x_ref[:, tile * LANES : (tile + 1) * LANES].astype(F32)
        weighted.append((x * scale).astype(BF16))
    state = dot(jnp.concatenate(weighted, axis=1), write_ref[...], 0, 0)
    tail_ref[pl.ds(pl.multiple_of(at, width), width), :] = state.astype(BF16)


def tail_kernel(
    lengths_ref,
    raw_ref,
    rate_ref,
    x_ref,
    write_ref,
    tail_ref,
    level_ref,
    column_ref,
    start_ref,
    weight_ref,
    *,
    per_group,
    channels,
):
    group = pl.program_id(0)

    @pl.when(group == 0)
    def _():
        level_part(
            lengths_ref, raw_ref, rate_ref, level_ref, column_ref, start_ref, weight_ref, tail_ref
        )

    at = group * x_ref.shape[1]
    tail_part(group, at, weight_ref, x_ref, write_ref, tail_ref, per_group, channels)


def inner_kernel(
    start_ref,
    level_ref,
    column_ref,
    skip_ref,
    x_ref,
    write_ref,
    read_ref,
    out_ref,
    *,
    heads,
    per_group,
    channels,
):
    group = pl.program_id(0)
    tokens = x_ref.shape[0]
    both = dot(read_ref[...], write_ref[...], 1, 1)
    square = (tokens, tokens)
    source = iota(square, 1)
    wide = jnp.concatenate([start_ref[...]] * (tokens // LANES), axis=1)
    both = jnp.where((source.astype(F32) >= wide) & (source <= iota(square, 0)), both, 0.0)
    lanes = level_ref.shape[1]
    level = pltpu.roll(level_ref[...] * LOG2E, lanes - group * per_group, 1)
    skip = jnp.concatenate([skip_ref[...]] * 2, axis=1)
    skip = two_parts(jnp.broadcast_to(skip, (16, 2 * heads)), heads).astype(BF16)
    skip = dot(skip, expander(heads, group, per_group, channels))[:1, :]
    per_tile = LANES // channels
    lane = iota((tokens, LANES), 1)
    for tile in range(per_group // per_tile):
        at = slice(tile * LANES, (tile + 1) * LANES)
        x = x_ref[:, at].astype(F32)
        owned = []
        for part in range(per_tile):
            mine = (lane >= part * channels) & (lane < (part + 1) * channels)
            owned.append(jnp.where(mine, x, 0.0).astype(BF16))
        for block in range(tokens // LANES):
            rows = slice(block * LANES, (block + 1) * LANES)
            reach = (block + 1) * LANES
            mixing = []
            for part in range(per_tile):
                head = tile * per_tile + part
                gap = level[rows, head : head + 1] - column_ref[head : head + 1, :reach]
                mixing.append(
                    (jnp.exp2(jnp.minimum(gap, 64.0)) * both[rows, :reach]).astype(BF16)
                )
            total = dot(
                jnp.concatenate(mixing, axis=1),
                jnp.concatenate([value[:reach, :] for value in owned], axis=0),
            )
            out_ref[rows, at] = (total + skip[:, at] * x[rows, :]).astype(BF16)


def attend_kernel(
    start_ref,
    query_ref,
    key_ref,
    value_ref,
    prior_key_ref,
    prior_value_ref,
    *rest,
    state_rows,
    prompt_rows,
    kv_count,
):
    gathered, (out_ref, bias_ref) = rest[:-2], rest[-2:]
    head = pl.program_id(0)
    tokens = query_ref.shape[0]
    prompt_count = len(gathered) * gathered[0].shape[0] * prompt_rows
    queries = query_ref.shape[1] // HD
    scale = LOG2E / math.sqrt(HD)
    reach = tokens + LANES

    @pl.when(head == 0)
    def _():
        shape = (LANES, reach)
        wide = jnp.concatenate([start_ref[...]] * (reach // LANES), axis=1)
        for block in range(tokens // LANES):
            rows = slice(block * LANES, (block + 1) * LANES)
            place = iota(shape, 1) + (block * LANES - tokens)
            allowed = (place.astype(F32) >= wide[rows, :]) & (
                place <= iota(shape, 0) + block * LANES
            )
            bias_ref[rows, :] = jnp.where(allowed, 0.0, -jnp.inf)

    def prompt(which):
        at = pl.multiple_of(state_rows + (which * kv_count + head) // 2 * 2 * prompt_rows, 16)
        at = pl.ds(at, 2 * prompt_rows)
        pair = jnp.concatenate([ref[:, at, :] for ref in gathered], axis=0).astype(F32)
        odd = lax.rem(head, 2) == 1
        part = jnp.where(odd, pair[:, prompt_rows:, :], pair[:, :prompt_rows, :])
        return part.reshape(prompt_count, HD).astype(BF16)

    prompt_keys, prompt_values = prompt(0), prompt(1)
    near_keys = jnp.concatenate([prior_key_ref[...], key_ref[...]], axis=0)
    near_values = jnp.concatenate([prior_value_ref[...], value_ref[...]], axis=0)
    ones = jnp.ones((prompt_count + reach, LANES), BF16)
    for block in range(tokens // LANES):
        rows = slice(block * LANES, (block + 1) * LANES)
        window = slice(block * LANES, block * LANES + reach)
        keys = jnp.concatenate([prompt_keys, near_keys[window, :]], axis=0)
        values = jnp.concatenate([prompt_values, near_values[window, :]], axis=0)
        values = jnp.concatenate([values, ones], axis=1)
        stacked = [query_ref[rows, query * HD : (query + 1) * HD] for query in range(queries)]
        scores = dot(jnp.concatenate(stacked, axis=0), keys, 1, 1)
        weights = []
        for query in range(queries):
            own = scores[query * LANES : (query + 1) * LANES, :]
            far, near = own[:, :prompt_count], own[:, prompt_count:] + bias_ref[rows, :]
            own = jnp.concatenate([far, near], axis=1)
            top = jnp.max(own, axis=1, keepdims=True)
            weights.append(jnp.exp2((own - top) * scale).astype(BF16))
        summed = dot(jnp.concatenate(weights, axis=0), values)
        for query in range(queries):
            own = summed[query * LANES : (query + 1) * LANES, :]
            out_ref[rows, query * HD : (query + 1) * HD] = (own[:, :HD] / own[:, HD:]).astype(BF16)


def final_kernel(
    start_ref,
    level_ref,
    tail_ref,
    decay_ref,
    read_ref,
    inner_ref,
    gate_ref,
    gain_ref,
    *rest,
    state_rows,
    heads,
    per_group,
    channels,
):
    gathered, (out_ref, value_ref) = rest[:NEAR], rest[-2:]
    group = pl.program_id(0)
    tokens, state = read_ref.shape
    width = per_group * channels

    scale = to_front(jnp.exp(level_ref[...]), group * per_group)
    carried = start_ref[:, :state] < 0
    read = read_ref[...].astype(F32)
    read = jnp.concatenate([jnp.where(carried, 0.0, read), jnp.where(carried, read, 0.0)], axis=1)
    read = read.astype(BF16)
    at = pl.multiple_of(group * per_group, per_group)
    decay = decay_ref[pl.ds(at, per_group), :].astype(F32)
    decay = decay + decay_ref[pl.ds(heads + at, per_group), :].astype(F32)
    own = lax.rem(lax.axis_index("reader"), NEAR)
    seeds = []
    for run in range(gathered[0].shape[0]):
        parts = [ref[run, :state_rows, :] for ref in gathered]
        bit = 1
        while bit < NEAR:
            swap = lax.rem(own // bit, 2) == 1
            parts = [jnp.where(swap, parts[i ^ bit], parts[i]) for i in range(NEAR)]
            bit *= 2
        seeds += parts
    seeds = jnp.concatenate(seeds, axis=0)
    squares = [None] * (tokens // LANES)
    for tile in range(width // WIDE):
        at = slice(tile * WIDE, (tile + 1) * WIDE)
        tile_heads = range(at.start // channels, at.stop // channels)
        falls = [jnp.broadcast_to(decay[h : h + 1, :], (channels, state)) for h in tile_heads]
        seed = seeds[at, :]
        entering = seed.astype(F32) * jnp.concatenate(falls, axis=0) + tail_ref[at, :].astype(F32)
        states = jnp.concatenate([seed, entering.astype(BF16)], axis=1)
        for block in range(tokens // LANES):
            rows = slice(block * LANES, (block + 1) * LANES)
            inflow = dot(read[rows, :], states, 1, 1)
            falls = [
                spread(scale[rows, :], (at.start + begin) // channels, channels)
                for begin in range(0, WIDE, LANES)
            ]
            inflow = inflow * jnp.concatenate(falls, axis=1)
            gate = gate_ref[rows, at].astype(F32)
            gated = inner_ref[rows, at].astype(F32) + inflow
            gated = gated * (gate * (0.5 + 0.5 * jnp.tanh(0.5 * gate)))
            value_ref[rows, at] = gated
            square = gated * gated
            for part in range(WIDE // LANES):
                piece = square[:, part * LANES : (part + 1) * LANES]
                squares[block] = piece if squares[block] is None else squares[block] + piece
    for block in range(tokens // LANES):
        rows = slice(block * LANES, (block + 1) * LANES)
        mean = jnp.sum(squares[block], axis=1, keepdims=True) * (1.0 / width)
        norm = lax.rsqrt(mean + 1e-05)
        for tile in range(width // WIDE):
            at = slice(tile * WIDE, (tile + 1) * WIDE)
            out_ref[rows, at] = (value_ref[rows, at] * norm * gain_ref[:, at]).astype(BF16)


def shifted(value, axis, by):
    length = lax.axis_size(axis)
    return lax.ppermute(value, axis, [(i, i + by) for i in range(length - by)])


def params(limit=32):
    return pltpu.CompilerParams(vmem_limit_bytes=limit * MIB)


def whole(shape):
    return pl.BlockSpec(shape, lambda g: (0,) * len(shape))


def local(
    answer_lengths,
    mixer_input,
    gate_input,
    state_write,
    state_read,
    step_raw,
    decay_rate,
    skip_gain,
    norm_gain,
    prompt_state,
    queries,
    answer_keys,
    answer_values,
    prompt_keys,
    prompt_values,
):
    tokens, columns = mixer_input.shape
    heads = decay_rate.shape[0]
    state_rows, state = prompt_state.shape
    groups = state_write.shape[1] // state
    per_group = heads // groups
    channels = columns // heads
    width = per_group * channels
    prompt_rows, kv_width = prompt_keys.shape
    kv_count = kv_width // HD
    devices = lax.axis_size("reader")
    in_hbm = lambda value: pltpu.with_memory_space_constraint(value, pltpu.MemorySpace.HBM)
    mixer_input, gate_input, state_write, state_read = map(
        in_hbm, (mixer_input, gate_input, state_write, state_read)
    )
    prompt_state, queries, answer_keys, answer_values, prompt_keys, prompt_values = map(
        in_hbm, (prompt_state, queries, answer_keys, answer_values, prompt_keys, prompt_values)
    )
    lengths, rate, skip, gain = map(
        lambda value: in_hbm(value.reshape(1, -1)),
        (answer_lengths, decay_rate, skip_gain, norm_gain),
    )
    sizes = dict(heads=heads, per_group=per_group, channels=channels)
    packed_rows = state_rows + 2 * prompt_rows * kv_count

    packed, near = pl.pallas_call(
        pack_kernel,
        out_shape=(
            jax.ShapeDtypeStruct((devices // NEAR, packed_rows, HD), BF16),
            jax.ShapeDtypeStruct((tokens, 2 * kv_width), BF16),
        ),
        in_specs=[pl.BlockSpec(memory_space=pl.ANY)] * 5,
        out_specs=(pl.BlockSpec(memory_space=pl.ANY), pl.BlockSpec(memory_space=pl.ANY)),
        scratch_shapes=[
            pltpu.VMEM(prompt_state.shape, F32),
            pltpu.VMEM(prompt_keys.shape, BF16),
            pltpu.VMEM(prompt_values.shape, BF16),
            pltpu.VMEM((packed_rows, HD), BF16),
            pltpu.SemaphoreType.DMA((3,)),
            pltpu.SemaphoreType.DMA((2,)),
            pltpu.SemaphoreType.DMA((devices // NEAR,)),
        ],
        compiler_params=params(),
        name="pack",
    )(prompt_state, prompt_keys, prompt_values, answer_keys, answer_values)
    packed, raw = lax.optimization_barrier((packed, step_raw.T))
    lines = [list(range(first, devices, NEAR)) for first in range(NEAR)]
    line = lax.all_to_all(packed, "reader", 0, 0, axis_index_groups=lines, tiled=True)
    prior = shifted(near, "reader", 1)
    raw = in_hbm(raw)

    small = pl.CostEstimate(flops=0, bytes_accessed=0, transcendentals=0)
    by_group = lambda rows: pl.BlockSpec((rows, state), lambda g: (0, g))
    wide = pl.BlockSpec((tokens, width), lambda g: (0, g))
    tail, level, column, start, weight = pl.pallas_call(
        functools.partial(tail_kernel, per_group=per_group, channels=channels),
        grid=(groups,),
        in_specs=[
            whole(lengths.shape),
            whole(raw.shape),
            whole((1, heads)),
            wide,
            by_group(tokens),
        ],
        out_specs=(
            whole((columns + 2 * heads, state)),
            whole((tokens, 2 * heads)),
            whole((heads, tokens)),
            whole((tokens, LANES)),
            whole((tokens, 2 * heads)),
        ),
        out_shape=(
            jax.ShapeDtypeStruct((columns + 2 * heads, state), BF16),
            jax.ShapeDtypeStruct((tokens, 2 * heads), F32),
            jax.ShapeDtypeStruct((heads, tokens), F32),
            jax.ShapeDtypeStruct((tokens, LANES), F32),
            jax.ShapeDtypeStruct((tokens, 2 * heads), F32),
        ),
        compiler_params=params(),
        cost_estimate=small,
        name="tail",
    )(lengths, raw, rate, mixer_input, state_write)
    tail = shifted(tail, "reader", 1)
    inner = pl.pallas_call(
        functools.partial(inner_kernel, **sizes),
        grid=(groups,),
        in_specs=[
            whole((tokens, LANES)),
            whole((tokens, 2 * heads)),
            pl.BlockSpec((per_group, tokens), lambda g: (g, 0)),
            whole((1, heads)),
            wide,
            by_group(tokens),
            by_group(tokens),
        ],
        out_specs=wide,
        out_shape=jax.ShapeDtypeStruct((tokens, columns), BF16),
        compiler_params=params(),
        cost_estimate=small,
        name="inner",
    )(start, level, column, skip, mixer_input, state_write, state_read)
    prior, line, inner = lax.optimization_barrier((prior, line, inner))
    gathered = (line, lax.ppermute(line, "reader", [(i, i ^ 1) for i in range(devices)]))

    group_size = queries.shape[1] // kv_width
    attention_out = pl.pallas_call(
        functools.partial(
            attend_kernel,
            state_rows=state_rows,
            prompt_rows=prompt_rows,
            kv_count=kv_count,
        ),
        grid=(kv_count,),
        in_specs=[
            whole((tokens, LANES)),
            pl.BlockSpec((tokens, group_size * HD), lambda k: (0, k)),
            pl.BlockSpec((tokens, HD), lambda k: (0, k)),
            pl.BlockSpec((tokens, HD), lambda k: (0, k)),
            pl.BlockSpec((tokens, HD), lambda k: (0, k)),
            pl.BlockSpec((tokens, HD), lambda k: (0, kv_count + k)),
        ]
        + [whole((devices // NEAR, packed_rows, HD))] * NEAR,
        out_specs=pl.BlockSpec((tokens, group_size * HD), lambda k: (0, k)),
        out_shape=jax.ShapeDtypeStruct(queries.shape, BF16),
        scratch_shapes=[pltpu.VMEM((tokens, tokens + LANES), F32)],
        compiler_params=params(),
        cost_estimate=small,
        name="attend",
    )(start, queries, answer_keys, answer_values, prior, prior, *gathered)

    inner, attention_out = lax.optimization_barrier((inner, attention_out))
    mixer_out = pl.pallas_call(
        functools.partial(final_kernel, state_rows=state_rows, **sizes),
        grid=(groups,),
        in_specs=[
            whole((tokens, LANES)),
            whole((tokens, 2 * heads)),
            pl.BlockSpec((width, state), lambda g: (g, 0)),
            pl.BlockSpec((2 * heads, state), lambda g: (columns // (2 * heads), 0)),
            by_group(tokens),
            wide,
            wide,
            pl.BlockSpec((1, width), lambda g: (0, g)),
        ]
        + [pl.BlockSpec((devices // groups // NEAR, packed_rows, HD), lambda g: (g, 0, 0))] * NEAR,
        out_specs=wide,
        out_shape=jax.ShapeDtypeStruct((tokens, columns), BF16),
        scratch_shapes=[pltpu.VMEM((tokens, width), F32)],
        compiler_params=params(),
        cost_estimate=small,
        name="final",
    )(start, level, tail, tail, state_read, inner, gate_input, gain, *gathered)
    return (mixer_out, attention_out)


def solution(mesh):
    rows = P(("group", "reader"), None)
    in_specs = (P("group"),) + (rows,) * 5 + (P(),) * 3 + (rows,) * 6
    return jax.shard_map(
        local, mesh=mesh, in_specs=in_specs, out_specs=(rows, rows), check_vma=False
    )
```

```python
import functools
import math

import jax
import jax.numpy as jnp
from jax import lax
from jax.experimental import pallas as pl
from jax.experimental.pallas import tpu as pltpu
from jax.sharding import PartitionSpec as P

HD = 128
LANES = 128
WIDE = 256
NEAR = 2
LOG2E = 1.4426950408889634
F32 = jnp.float32
BF16 = jnp.bfloat16
MIB = 1 << 20


def iota(shape, dim):
    return lax.broadcasted_iota(jnp.int32, shape, dim)


def dot(a, b, ca=1, cb=0):
    return lax.dot_general(a, b, (((ca,), (cb,)), ((), ())), preferred_element_type=F32)


def expander(heads, group, per_group, channels):
    shape = (2 * heads, per_group * channels)
    row = iota(shape, 0)
    head = jnp.where(row >= heads, row - heads, row) - group * per_group
    column = iota(shape, 1)
    first = head * channels
    return jnp.where((column >= first) & (column < first + channels), 1.0, 0.0).astype(BF16)


def two_parts(value, heads):
    high = value.astype(BF16).astype(F32)
    return jnp.where(iota(value.shape, 1) < heads, high, value - high)


def to_front(value, head):
    return pltpu.roll(value, value.shape[1] - head, 1)


def spread(value, first, channels):
    lane = iota((8, LANES), 1)
    source = jnp.full((8, LANES), first, jnp.int32)
    for part in range(1, LANES // channels):
        source = source + jnp.where(lane >= part * channels, 1, 0)
    source = jnp.concatenate([source] * (value.shape[0] // 8), axis=0)
    return jnp.take_along_axis(value, source, axis=1, mode="promise_in_bounds")


def join_kernel(keys_ref, values_ref, out_ref):
    width = keys_ref.shape[1]
    out_ref[:, :width] = keys_ref[...]
    out_ref[:, width:] = values_ref[...]


def pack_kernel(state_ref, keys_ref, values_ref, out_ref):
    rows = state_ref.shape[0]
    state = state_ref[...].astype(BF16)
    parts = []
    for ref in (keys_ref, values_ref):
        wide = ref[...].astype(F32)
        for head in range(wide.shape[1] // HD):
            parts.append(wide[:, head * HD : (head + 1) * HD])
    parts = jnp.concatenate(parts, axis=0).astype(BF16)
    for copy in range(out_ref.shape[0]):
        out_ref[copy, :rows, :] = state
        out_ref[copy, rows:, :] = parts


def level_part(lengths_ref, raw_ref, rate_ref, level_ref, column_ref, start_ref, weight_ref, tail_ref):
    heads, tokens = raw_ref.shape
    base = (lax.axis_index("reader") * tokens).astype(F32)
    lengths = lengths_ref[...].astype(F32)
    answers = lengths.shape[1]
    square = (answers, answers)
    ends = jnp.sum(
        jnp.where(iota(square, 1) <= iota(square, 0), lengths, 0.0), axis=1, keepdims=True
    )
    place = base + iota((1, tokens), 1).astype(F32)
    start = jnp.max(jnp.where(ends <= place, ends, 0.0), axis=0, keepdims=True) - base
    start = jnp.broadcast_to(start, (LANES, tokens)).T
    start_ref[...] = start
    wide = jnp.concatenate([start] * (tokens // LANES), axis=1)
    square = (tokens, tokens)
    source = iota(square, 1)
    mask = (source.astype(F32) >= wide) & (source <= iota(square, 0))
    mask = jnp.where(mask, 1.0, 0.0).astype(BF16)
    raw = raw_ref[...]
    rate = jnp.broadcast_to(rate_ref[...], (heads, heads))
    diagonal = iota((heads, heads), 0) == iota((heads, heads), 1)
    rate = jnp.sum(jnp.where(diagonal, rate, 0.0), axis=1, keepdims=True)
    step = jnp.maximum(raw, 0.0) + jnp.log1p(jnp.exp(-jnp.abs(raw)))
    falling = -rate * step
    first = falling.astype(BF16)
    rest = falling - first.astype(F32)
    second = rest.astype(BF16)
    third = (rest - second.astype(F32)).astype(BF16)
    level = dot(first, mask, 1, 1) + (dot(second, mask, 1, 1) + dot(third, mask, 1, 1))
    column_ref[...] = level * LOG2E - jnp.log(step) * LOG2E
    last = level[:, tokens - 1 :]
    decay = jnp.exp(jnp.broadcast_to(last, (heads, tail_ref.shape[1])))
    high = decay.astype(BF16)
    low = (decay - high.astype(F32)).astype(BF16)
    tail_ref[tail_ref.shape[0] - 2 * heads :, :] = jnp.concatenate([high, low], axis=0)
    own = iota((heads, tokens), 1).astype(F32) >= start[tokens - 1 :, :1]
    weight = jnp.where(own, jnp.exp(last - level) * step, 0.0)
    weight_ref[...] = jnp.concatenate([weight, weight], axis=0).T
    level_ref[...] = jnp.concatenate([level, level], axis=0).T


def tail_part(group, at, weight_ref, x_ref, write_ref, tail_ref, per_group, channels):
    tokens, width = x_ref.shape
    weight = to_front(weight_ref[...], group * per_group)
    weighted = []
    for tile in range(width // LANES):
        scale = spread(weight, tile * LANES // channels, channels)
        x = x_ref[:, tile * LANES : (tile + 1) * LANES].astype(F32)
        weighted.append((x * scale).astype(BF16))
    state = dot(jnp.concatenate(weighted, axis=1), write_ref[...], 0, 0)
    tail_ref[pl.ds(pl.multiple_of(at, width), width), :] = state.astype(BF16)


def tail_kernel(
    lengths_ref,
    raw_ref,
    rate_ref,
    x_ref,
    write_ref,
    tail_ref,
    level_ref,
    column_ref,
    start_ref,
    weight_ref,
    *,
    per_group,
    channels,
):
    group = pl.program_id(0)

    @pl.when(group == 0)
    def _():
        level_part(
            lengths_ref, raw_ref, rate_ref, level_ref, column_ref, start_ref, weight_ref, tail_ref
        )

    at = group * x_ref.shape[1]
    tail_part(group, at, weight_ref, x_ref, write_ref, tail_ref, per_group, channels)


def inner_kernel(
    start_ref,
    level_ref,
    column_ref,
    skip_ref,
    x_ref,
    write_ref,
    read_ref,
    out_ref,
    *,
    heads,
    per_group,
    channels,
):
    group = pl.program_id(0)
    tokens = x_ref.shape[0]
    both = dot(read_ref[...], write_ref[...], 1, 1)
    square = (tokens, tokens)
    source = iota(square, 1)
    wide = jnp.concatenate([start_ref[...]] * (tokens // LANES), axis=1)
    both = jnp.where((source.astype(F32) >= wide) & (source <= iota(square, 0)), both, 0.0)
    lanes = level_ref.shape[1]
    level = pltpu.roll(level_ref[...] * LOG2E, lanes - group * per_group, 1)
    column = column_ref[pl.ds(pl.multiple_of(group * per_group, per_group), per_group), :]
    begin = pl.multiple_of(group * per_group * channels, per_group * channels)
    skip = jnp.concatenate([skip_ref[...]] * 2, axis=1)
    skip = two_parts(jnp.broadcast_to(skip, (16, 2 * heads)), heads).astype(BF16)
    skip = dot(skip, expander(heads, group, per_group, channels))[:1, :]
    per_tile = LANES // channels
    lane = iota((16, LANES), 1)
    own = []
    for part in range(per_tile):
        mine = (lane >= part * channels) & (lane < (part + 1) * channels)
        own.append(jnp.concatenate([jnp.where(mine, 1.0, 0.0).astype(BF16)] * (tokens // 16), axis=0))
    for tile in range(per_group // per_tile):
        at = slice(tile * LANES, (tile + 1) * LANES)
        x = x_ref[:, at]
        owned = [x * mine for mine in own]
        for block in range(tokens // LANES):
            rows = slice(block * LANES, (block + 1) * LANES)
            reach = (block + 1) * LANES
            mixing = []
            for part in range(per_tile):
                head = tile * per_tile + part
                gap = level[rows, head : head + 1] - column[head : head + 1, :reach]
                mixing.append(
                    (jnp.exp2(jnp.minimum(gap, 64.0)) * both[rows, :reach]).astype(BF16)
                )
            total = dot(
                jnp.concatenate(mixing, axis=1),
                jnp.concatenate([value[:reach, :] for value in owned], axis=0),
            )
            out_ref[rows, pl.ds(begin + at.start, LANES)] = (
                total + skip[:, at] * x[rows, :].astype(F32)
            ).astype(BF16)


def attend_kernel(
    start_ref,
    query_ref,
    key_ref,
    value_ref,
    prior_ref,
    *rest,
    state_rows,
    prompt_rows,
    kv_count,
):
    gathered, (out_ref, bias_ref) = rest[:-2], rest[-2:]
    head = pl.program_id(0)
    tokens = query_ref.shape[0]
    prompt_count = len(gathered) * gathered[0].shape[0] * prompt_rows
    queries = query_ref.shape[1] // HD
    scale = LOG2E / math.sqrt(HD)
    reach = tokens + LANES

    @pl.when(head == 0)
    def _():
        shape = (LANES, reach)
        wide = jnp.concatenate([start_ref[...]] * (reach // LANES), axis=1)
        for block in range(tokens // LANES):
            rows = slice(block * LANES, (block + 1) * LANES)
            place = iota(shape, 1) + (block * LANES - tokens)
            allowed = (place.astype(F32) >= wide[rows, :]) & (
                place <= iota(shape, 0) + block * LANES
            )
            bias_ref[rows, :] = jnp.where(allowed, 0.0, -jnp.inf)

    def prompt(which):
        at = pl.multiple_of(state_rows + (which * kv_count + head) // 2 * 2 * prompt_rows, 16)
        at = pl.ds(at, 2 * prompt_rows)
        pair = jnp.concatenate([ref[:, at, :] for ref in gathered], axis=0).astype(F32)
        odd = lax.rem(head, 2) == 1
        part = jnp.where(odd, pair[:, prompt_rows:, :], pair[:, :prompt_rows, :])
        return part.reshape(prompt_count, HD).astype(BF16)

    prompt_keys, prompt_values = prompt(0), prompt(1)
    prior = [
        prior_ref[:, pl.ds(pl.multiple_of((which * kv_count + head) * HD, HD), HD)]
        for which in range(2)
    ]
    near_keys = jnp.concatenate([prior[0], key_ref[...]], axis=0)
    near_values = jnp.concatenate([prior[1], value_ref[...]], axis=0)
    ones = jnp.ones((prompt_count + reach, LANES), BF16)
    for block in range(tokens // LANES):
        rows = slice(block * LANES, (block + 1) * LANES)
        window = slice(block * LANES, block * LANES + reach)
        keys = jnp.concatenate([prompt_keys, near_keys[window, :]], axis=0)
        values = jnp.concatenate([prompt_values, near_values[window, :]], axis=0)
        values = jnp.concatenate([values, ones], axis=1)
        stacked = [query_ref[rows, query * HD : (query + 1) * HD] for query in range(queries)]
        scores = dot(jnp.concatenate(stacked, axis=0), keys, 1, 1)
        weights = []
        for query in range(queries):
            own = scores[query * LANES : (query + 1) * LANES, :]
            far, near = own[:, :prompt_count], own[:, prompt_count:]
            bias = bias_ref[rows, :]
            top = jnp.maximum(
                jnp.max(far, axis=1, keepdims=True), jnp.max(near + bias, axis=1, keepdims=True)
            )
            level = top * scale
            far = jnp.exp2(far * scale - level)
            near = jnp.exp2(near * scale + (bias - level))
            weights.append(jnp.concatenate([far, near], axis=1).astype(BF16))
        summed = dot(jnp.concatenate(weights, axis=0), values)
        for query in range(queries):
            own = summed[query * LANES : (query + 1) * LANES, :]
            out_ref[rows, query * HD : (query + 1) * HD] = (own[:, :HD] / own[:, HD:]).astype(BF16)


def final_kernel(
    start_ref,
    level_ref,
    tail_ref,
    read_ref,
    inner_ref,
    gate_ref,
    gain_ref,
    *rest,
    state_rows,
    heads,
    per_group,
    channels,
):
    gathered, (out_ref, value_ref) = rest[:NEAR], rest[-2:]
    group = pl.program_id(0)
    tokens, state = read_ref.shape
    width = per_group * channels

    scale = to_front(jnp.exp(level_ref[...]), group * per_group)
    carried = start_ref[:, :state] < 0
    read = read_ref[...].astype(F32)
    read = jnp.concatenate([jnp.where(carried, 0.0, read), jnp.where(carried, read, 0.0)], axis=1)
    read = read.astype(BF16)
    falls_at = heads * channels + pl.multiple_of(group * per_group, per_group)
    decay = tail_ref[pl.ds(falls_at, per_group), :].astype(F32)
    decay = decay + tail_ref[pl.ds(falls_at + heads, per_group), :].astype(F32)
    begin = pl.multiple_of(group * width, width)
    own = lax.rem(lax.axis_index("reader"), NEAR)
    seeds = []
    runs = width // (NEAR * state_rows)
    for run in range(runs):
        parts = [ref[group * runs + run, :state_rows, :] for ref in gathered]
        bit = 1
        while bit < NEAR:
            swap = lax.rem(own // bit, 2) == 1
            parts = [jnp.where(swap, parts[i ^ bit], parts[i]) for i in range(NEAR)]
            bit *= 2
        seeds += parts
    seeds = jnp.concatenate(seeds, axis=0)
    squares = [None] * (tokens // LANES)
    for tile in range(width // WIDE):
        at = slice(tile * WIDE, (tile + 1) * WIDE)
        tile_heads = range(at.start // channels, at.stop // channels)
        falls = [jnp.broadcast_to(decay[h : h + 1, :], (channels, state)) for h in tile_heads]
        seed = seeds[at, :]
        entering = seed.astype(F32) * jnp.concatenate(falls, axis=0)
        entering = entering + tail_ref[pl.ds(begin + at.start, WIDE), :].astype(F32)
        states = jnp.concatenate([seed, entering.astype(BF16)], axis=1)
        for block in range(tokens // LANES):
            rows = slice(block * LANES, (block + 1) * LANES)
            inflow = dot(read[rows, :], states, 1, 1)
            falls = [
                spread(scale[rows, :], (at.start + offset) // channels, channels)
                for offset in range(0, WIDE, LANES)
            ]
            inflow = inflow * jnp.concatenate(falls, axis=1)
            half = 0.5 * gate_ref[rows, at].astype(F32)
            gated = inner_ref[rows, pl.ds(begin + at.start, WIDE)].astype(F32) + inflow
            gated = gated * (half + half * jnp.tanh(half))
            value_ref[rows, at] = gated
            square = gated * gated
            for part in range(WIDE // LANES):
                piece = square[:, part * LANES : (part + 1) * LANES]
                squares[block] = piece if squares[block] is None else squares[block] + piece
    for block in range(tokens // LANES):
        rows = slice(block * LANES, (block + 1) * LANES)
        mean = jnp.sum(squares[block], axis=1, keepdims=True) * (1.0 / width)
        norm = lax.rsqrt(mean + 1e-05)
        for tile in range(width // WIDE):
            at = slice(tile * WIDE, (tile + 1) * WIDE)
            out_ref[rows, at] = (value_ref[rows, at] * norm * gain_ref[:, at]).astype(BF16)


def shifted(value, axis, by):
    length = lax.axis_size(axis)
    return lax.ppermute(value, axis, [(i, i + by) for i in range(length - by)])


def params(limit=32):
    return pltpu.CompilerParams(vmem_limit_bytes=limit * MIB)


def whole(shape):
    return pl.BlockSpec(shape, lambda g: (0,) * len(shape))


def local(
    answer_lengths,
    mixer_input,
    gate_input,
    state_write,
    state_read,
    step_raw,
    decay_rate,
    skip_gain,
    norm_gain,
    prompt_state,
    queries,
    answer_keys,
    answer_values,
    prompt_keys,
    prompt_values,
):
    tokens, columns = mixer_input.shape
    heads = decay_rate.shape[0]
    state_rows, state = prompt_state.shape
    groups = state_write.shape[1] // state
    per_group = heads // groups
    channels = columns // heads
    width = per_group * channels
    prompt_rows, kv_width = prompt_keys.shape
    kv_count = kv_width // HD
    devices = lax.axis_size("reader")
    in_hbm = lambda value: pltpu.with_memory_space_constraint(value, pltpu.MemorySpace.HBM)
    mixer_input, gate_input, state_write, state_read = map(
        in_hbm, (mixer_input, gate_input, state_write, state_read)
    )
    prompt_state, queries, prompt_keys, prompt_values = map(
        in_hbm, (prompt_state, queries, prompt_keys, prompt_values)
    )
    lengths, rate, skip, gain = map(
        lambda value: in_hbm(value.reshape(1, -1)),
        (answer_lengths, decay_rate, skip_gain, norm_gain),
    )
    at_hand = pl.BlockSpec(memory_space=pltpu.VMEM)
    sizes = dict(heads=heads, per_group=per_group, channels=channels)
    packed_rows = state_rows + 2 * prompt_rows * kv_count

    packed = pl.pallas_call(
        pack_kernel,
        out_shape=jax.ShapeDtypeStruct((devices // NEAR, packed_rows, HD), BF16),
        out_specs=at_hand,
        compiler_params=params(),
        name="pack",
    )(prompt_state, prompt_keys, prompt_values)
    packed, near_keys = lax.optimization_barrier((packed, answer_keys))
    near = pl.pallas_call(
        join_kernel,
        out_shape=jax.ShapeDtypeStruct((tokens, 2 * kv_width), BF16),
        out_specs=at_hand,
        compiler_params=params(),
        name="join",
    )(in_hbm(near_keys), in_hbm(answer_values))
    packed, raw = lax.optimization_barrier((packed, step_raw.T))
    lines = [list(range(first, devices, NEAR)) for first in range(NEAR)]
    line = lax.all_to_all(packed, "reader", 0, 0, axis_index_groups=lines, tiled=True)
    prior = shifted(near, "reader", 1)
    raw = in_hbm(raw)

    small = pl.CostEstimate(flops=0, bytes_accessed=0, transcendentals=0)
    by_group = lambda rows: pl.BlockSpec((rows, state), lambda g: (0, g))
    wide = pl.BlockSpec((tokens, width), lambda g: (0, g))
    tail, level, column, start = pl.pallas_call(
        functools.partial(tail_kernel, per_group=per_group, channels=channels),
        grid=(groups,),
        in_specs=[
            whole(lengths.shape),
            whole(raw.shape),
            whole((1, heads)),
            wide,
            by_group(tokens),
        ],
        out_specs=(at_hand, at_hand, at_hand, at_hand),
        out_shape=(
            jax.ShapeDtypeStruct((columns + 2 * heads, state), BF16),
            jax.ShapeDtypeStruct((tokens, 2 * heads), F32),
            jax.ShapeDtypeStruct((heads, tokens), F32),
            jax.ShapeDtypeStruct((tokens, LANES), F32),
        ),
        scratch_shapes=[pltpu.VMEM((tokens, 2 * heads), F32)],
        compiler_params=params(),
        cost_estimate=small,
        name="tail",
    )(lengths, raw, rate, mixer_input, state_write)
    tail = shifted(tail, "reader", 1)
    inner = pl.pallas_call(
        functools.partial(inner_kernel, **sizes),
        grid=(groups,),
        in_specs=[
            at_hand,
            at_hand,
            at_hand,
            whole((1, heads)),
            wide,
            by_group(tokens),
            by_group(tokens),
        ],
        out_specs=at_hand,
        out_shape=jax.ShapeDtypeStruct((tokens, columns), BF16),
        compiler_params=params(),
        cost_estimate=small,
        name="inner",
    )(start, level, column, skip, mixer_input, state_write, state_read)
    prior, line, inner = lax.optimization_barrier((prior, line, inner))
    gathered = (line, lax.ppermute(line, "reader", [(i, i ^ 1) for i in range(devices)]))

    group_size = queries.shape[1] // kv_width
    attention_out = pl.pallas_call(
        functools.partial(
            attend_kernel,
            state_rows=state_rows,
            prompt_rows=prompt_rows,
            kv_count=kv_count,
        ),
        grid=(kv_count,),
        in_specs=[
            at_hand,
            pl.BlockSpec((tokens, group_size * HD), lambda k: (0, k)),
            pl.BlockSpec((tokens, HD), lambda k: (0, k)),
            pl.BlockSpec((tokens, HD), lambda k: (0, k)),
            at_hand,
        ]
        + [at_hand] * NEAR,
        out_specs=pl.BlockSpec((tokens, group_size * HD), lambda k: (0, k)),
        out_shape=jax.ShapeDtypeStruct(queries.shape, BF16),
        scratch_shapes=[pltpu.VMEM((tokens, tokens + LANES), F32)],
        compiler_params=params(),
        cost_estimate=small,
        name="attend",
    )(start, queries, in_hbm(answer_keys), in_hbm(answer_values), prior, *gathered)

    inner, attention_out = lax.optimization_barrier((inner, attention_out))
    mixer_out = pl.pallas_call(
        functools.partial(final_kernel, state_rows=state_rows, **sizes),
        grid=(groups,),
        in_specs=[
            at_hand,
            at_hand,
            at_hand,
            by_group(tokens),
            at_hand,
            wide,
            pl.BlockSpec((1, width), lambda g: (0, g)),
        ]
        + [at_hand] * NEAR,
        out_specs=wide,
        out_shape=jax.ShapeDtypeStruct((tokens, columns), BF16),
        scratch_shapes=[pltpu.VMEM((tokens, width), F32)],
        compiler_params=params(),
        cost_estimate=small,
        name="final",
    )(start, level, tail, state_read, inner, gate_input, gain, *gathered)
    return (mixer_out, attention_out)


def solution(mesh):
    rows = P(("group", "reader"), None)
    in_specs = (P("group"),) + (rows,) * 5 + (P(),) * 3 + (rows,) * 6
    return jax.shard_map(
        local, mesh=mesh, in_specs=in_specs, out_specs=(rows, rows), check_vma=False
    )
```

```python
import functools
import math

import jax
import jax.numpy as jnp
from jax import lax
from jax.experimental import pallas as pl
from jax.experimental.pallas import tpu as pltpu
from jax.sharding import PartitionSpec as P

HD = 128
LANES = 128
WIDE = 256
NEAR = 2
LOG2E = 1.4426950408889634
F32 = jnp.float32
BF16 = jnp.bfloat16
MIB = 1 << 20


def iota(shape, dim):
    return lax.broadcasted_iota(jnp.int32, shape, dim)


def dot(a, b, ca=1, cb=0):
    return lax.dot_general(a, b, (((ca,), (cb,)), ((), ())), preferred_element_type=F32)


def expander(heads, group, per_group, channels):
    shape = (2 * heads, per_group * channels)
    row = iota(shape, 0)
    head = jnp.where(row >= heads, row - heads, row) - group * per_group
    column = iota(shape, 1)
    first = head * channels
    return jnp.where((column >= first) & (column < first + channels), 1.0, 0.0).astype(BF16)


def two_parts(value, heads):
    high = value.astype(BF16).astype(F32)
    return jnp.where(iota(value.shape, 1) < heads, high, value - high)


def to_front(value, head):
    return pltpu.roll(value, value.shape[1] - head, 1)


def spread(value, first, channels):
    lane = iota((8, LANES), 1)
    source = jnp.full((8, LANES), first, jnp.int32)
    for part in range(1, LANES // channels):
        source = source + jnp.where(lane >= part * channels, 1, 0)
    source = jnp.concatenate([source] * (value.shape[0] // 8), axis=0)
    return jnp.take_along_axis(value, source, axis=1, mode="promise_in_bounds")


def join_kernel(keys_ref, values_ref, out_ref):
    width = keys_ref.shape[1]
    out_ref[:, :width] = keys_ref[...]
    out_ref[:, width:] = values_ref[...]


def pack_kernel(state_ref, keys_ref, values_ref, out_ref):
    rows = state_ref.shape[0]
    state = state_ref[...].astype(BF16)
    parts = []
    for ref in (keys_ref, values_ref):
        wide = ref[...].astype(F32)
        for head in range(wide.shape[1] // HD):
            parts.append(wide[:, head * HD : (head + 1) * HD])
    parts = jnp.concatenate(parts, axis=0).astype(BF16)
    for copy in range(out_ref.shape[0]):
        out_ref[copy, :rows, :] = state
        out_ref[copy, rows:, :] = parts


def level_part(lengths_ref, raw_ref, rate_ref, level_ref, column_ref, start_ref, weight_ref, tail_ref):
    heads, tokens = raw_ref.shape
    base = (lax.axis_index("reader") * tokens).astype(F32)
    lengths = lengths_ref[...].astype(F32)
    answers = lengths.shape[1]
    square = (answers, answers)
    ends = jnp.sum(
        jnp.where(iota(square, 1) <= iota(square, 0), lengths, 0.0), axis=1, keepdims=True
    )
    place = base + iota((1, tokens), 1).astype(F32)
    start = jnp.max(jnp.where(ends <= place, ends, 0.0), axis=0, keepdims=True) - base
    start = jnp.broadcast_to(start, (LANES, tokens)).T
    start_ref[...] = start
    wide = jnp.concatenate([start] * (tokens // LANES), axis=1)
    square = (tokens, tokens)
    source = iota(square, 1)
    mask = (source.astype(F32) >= wide) & (source <= iota(square, 0))
    mask = jnp.where(mask, 1.0, 0.0).astype(BF16)
    raw = raw_ref[...]
    rate = jnp.broadcast_to(rate_ref[...], (heads, heads))
    diagonal = iota((heads, heads), 0) == iota((heads, heads), 1)
    rate = jnp.sum(jnp.where(diagonal, rate, 0.0), axis=1, keepdims=True)
    step = jnp.maximum(raw, 0.0) + jnp.log1p(jnp.exp(-jnp.abs(raw)))
    falling = -rate * step
    first = falling.astype(BF16)
    rest = falling - first.astype(F32)
    second = rest.astype(BF16)
    third = (rest - second.astype(F32)).astype(BF16)
    level = dot(first, mask, 1, 1) + (dot(second, mask, 1, 1) + dot(third, mask, 1, 1))
    column_ref[...] = level * LOG2E - jnp.log(step) * LOG2E
    last = level[:, tokens - 1 :]
    decay = jnp.exp(jnp.broadcast_to(last, (heads, tail_ref.shape[1])))
    high = decay.astype(BF16)
    low = (decay - high.astype(F32)).astype(BF16)
    tail_ref[tail_ref.shape[0] - 2 * heads :, :] = jnp.concatenate([high, low], axis=0)
    own = iota((heads, tokens), 1).astype(F32) >= start[tokens - 1 :, :1]
    weight = jnp.where(own, jnp.exp(last - level) * step, 0.0)
    weight_ref[...] = jnp.concatenate([weight, weight], axis=0).T
    level_ref[...] = jnp.concatenate([level, level], axis=0).T


def tail_part(group, weight_ref, x_ref, write_ref, tail_ref, per_group, channels):
    width = per_group * channels
    begin = pl.multiple_of(group * width, width)
    weight = to_front(weight_ref[...], group * per_group)
    weighted = []
    for tile in range(width // LANES):
        scale = spread(weight, tile * LANES // channels, channels)
        x = x_ref[:, tile * LANES : (tile + 1) * LANES].astype(F32)
        weighted.append((x * scale).astype(BF16))
    state = dot(jnp.concatenate(weighted, axis=1), write_ref[...], 0, 0)
    tail_ref[pl.ds(begin, width), :] = state.astype(BF16)


def tail_kernel(
    lengths_ref,
    raw_ref,
    rate_ref,
    x_ref,
    write_ref,
    tail_ref,
    level_ref,
    column_ref,
    start_ref,
    weight_ref,
    *,
    per_group,
    channels,
):
    group = pl.program_id(0)

    @pl.when(group == 0)
    def _():
        level_part(
            lengths_ref, raw_ref, rate_ref, level_ref, column_ref, start_ref, weight_ref, tail_ref
        )

    tail_part(group, weight_ref, x_ref, write_ref, tail_ref, per_group, channels)


def inner_kernel(
    start_ref,
    level_ref,
    column_ref,
    skip_ref,
    x_ref,
    write_ref,
    read_ref,
    out_ref,
    *,
    heads,
    per_group,
    channels,
):
    group = pl.program_id(0)
    tokens = x_ref.shape[0]
    size = read_ref.shape[1] // (heads // per_group)
    own = pl.ds(pl.multiple_of(group * size, size), size)
    both = dot(read_ref[:, own], write_ref[:, own], 1, 1)
    square = (tokens, tokens)
    source = iota(square, 1)
    wide = jnp.concatenate([start_ref[...]] * (tokens // LANES), axis=1)
    both = jnp.where((source.astype(F32) >= wide) & (source <= iota(square, 0)), both, 0.0)
    lanes = level_ref.shape[1]
    level = pltpu.roll(level_ref[...] * LOG2E, lanes - group * per_group, 1)
    column = column_ref[pl.ds(pl.multiple_of(group * per_group, per_group), per_group), :]
    begin = pl.multiple_of(group * per_group * channels, per_group * channels)
    skip = jnp.concatenate([skip_ref[...]] * 2, axis=1)
    skip = two_parts(jnp.broadcast_to(skip, (16, 2 * heads)), heads).astype(BF16)
    skip = dot(skip, expander(heads, group, per_group, channels))[:1, :]
    per_tile = LANES // channels
    lane = iota((tokens, LANES), 1)
    for tile in range(per_group // per_tile):
        at = slice(tile * LANES, (tile + 1) * LANES)
        x = x_ref[:, pl.ds(begin + at.start, LANES)].astype(F32)
        owned = []
        for part in range(per_tile):
            mine = (lane >= part * channels) & (lane < (part + 1) * channels)
            owned.append(jnp.where(mine, x, 0.0).astype(BF16))
        for block in range(tokens // LANES):
            rows = slice(block * LANES, (block + 1) * LANES)
            reach = (block + 1) * LANES
            mixing = []
            for part in range(per_tile):
                head = tile * per_tile + part
                gap = level[rows, head : head + 1] - column[head : head + 1, :reach]
                mixing.append(
                    (jnp.exp2(jnp.minimum(gap, 64.0)) * both[rows, :reach]).astype(BF16)
                )
            total = dot(
                jnp.concatenate(mixing, axis=1),
                jnp.concatenate([value[:reach, :] for value in owned], axis=0),
            )
            out_ref[rows, pl.ds(begin + at.start, LANES)] = (
                total + skip[:, at] * x[rows, :]
            ).astype(BF16)


def attend_kernel(
    start_ref,
    query_ref,
    key_ref,
    value_ref,
    prior_ref,
    *rest,
    state_rows,
    prompt_rows,
    kv_count,
):
    gathered, (out_ref, bias_ref) = rest[:-2], rest[-2:]
    head = pl.program_id(0)
    tokens = query_ref.shape[0]
    own = pl.ds(pl.multiple_of(head * HD, HD), HD)
    prompt_count = len(gathered) * gathered[0].shape[0] * prompt_rows
    queries = query_ref.shape[1] // HD // kv_count
    scale = LOG2E / math.sqrt(HD)
    reach = tokens + LANES

    @pl.when(head == 0)
    def _():
        shape = (LANES, reach)
        wide = jnp.concatenate([start_ref[...]] * (reach // LANES), axis=1)
        for block in range(tokens // LANES):
            rows = slice(block * LANES, (block + 1) * LANES)
            place = iota(shape, 1) + (block * LANES - tokens)
            allowed = (place.astype(F32) >= wide[rows, :]) & (
                place <= iota(shape, 0) + block * LANES
            )
            bias_ref[rows, :] = jnp.where(allowed, 0.0, -jnp.inf)

    def prompt(which):
        at = pl.multiple_of(state_rows + (which * kv_count + head) // 2 * 2 * prompt_rows, 16)
        at = pl.ds(at, 2 * prompt_rows)
        pair = jnp.concatenate([ref[:, at, :] for ref in gathered], axis=0).astype(F32)
        odd = lax.rem(head, 2) == 1
        part = jnp.where(odd, pair[:, prompt_rows:, :], pair[:, :prompt_rows, :])
        return part.reshape(prompt_count, HD).astype(BF16)

    prompt_keys, prompt_values = prompt(0), prompt(1)
    prior = [
        prior_ref[:, pl.ds(pl.multiple_of((which * kv_count + head) * HD, HD), HD)]
        for which in range(2)
    ]
    near_keys = jnp.concatenate([prior[0], key_ref[:, own]], axis=0)
    near_values = jnp.concatenate([prior[1], value_ref[:, own]], axis=0)
    ones = jnp.ones((prompt_count + reach, LANES), BF16)
    for block in range(tokens // LANES):
        rows = slice(block * LANES, (block + 1) * LANES)
        window = slice(block * LANES, block * LANES + reach)
        keys = jnp.concatenate([prompt_keys, near_keys[window, :]], axis=0)
        values = jnp.concatenate([prompt_values, near_values[window, :]], axis=0)
        values = jnp.concatenate([values, ones], axis=1)
        begin = pl.multiple_of(head * queries * HD, queries * HD)
        stacked = [query_ref[rows, pl.ds(begin + query * HD, HD)] for query in range(queries)]
        scores = dot(jnp.concatenate(stacked, axis=0), keys, 1, 1)
        weights = []
        for query in range(queries):
            own = scores[query * LANES : (query + 1) * LANES, :]
            far, near = own[:, :prompt_count], own[:, prompt_count:] + bias_ref[rows, :]
            own = jnp.concatenate([far, near], axis=1)
            top = jnp.max(own, axis=1, keepdims=True)
            weights.append(jnp.exp2((own - top) * scale).astype(BF16))
        summed = dot(jnp.concatenate(weights, axis=0), values)
        for query in range(queries):
            own = summed[query * LANES : (query + 1) * LANES, :]
            out_ref[rows, query * HD : (query + 1) * HD] = (own[:, :HD] / own[:, HD:]).astype(BF16)


def final_kernel(
    start_ref,
    level_ref,
    tail_ref,
    read_ref,
    inner_ref,
    gate_ref,
    gain_ref,
    *rest,
    state_rows,
    heads,
    per_group,
    channels,
):
    gathered, (out_ref, value_ref) = rest[:NEAR], rest[-2:]
    group = pl.program_id(0)
    tokens = read_ref.shape[0]
    width, state = per_group * channels, tail_ref.shape[1]

    scale = to_front(jnp.exp(level_ref[...]), group * per_group)
    carried = start_ref[:, :state] < 0
    read = read_ref[:, pl.ds(pl.multiple_of(group * state, state), state)].astype(F32)
    read = jnp.concatenate([jnp.where(carried, 0.0, read), jnp.where(carried, read, 0.0)], axis=1)
    read = read.astype(BF16)
    falls_at = heads * channels + pl.multiple_of(group * per_group, per_group)
    decay = tail_ref[pl.ds(falls_at, per_group), :].astype(F32)
    decay = decay + tail_ref[pl.ds(falls_at + heads, per_group), :].astype(F32)
    begin = pl.multiple_of(group * width, width)
    own = lax.rem(lax.axis_index("reader"), NEAR)
    seeds = []
    runs = width // (NEAR * state_rows)
    for run in range(runs):
        parts = [ref[group * runs + run, :state_rows, :] for ref in gathered]
        bit = 1
        while bit < NEAR:
            swap = lax.rem(own // bit, 2) == 1
            parts = [jnp.where(swap, parts[i ^ bit], parts[i]) for i in range(NEAR)]
            bit *= 2
        seeds += parts
    seeds = jnp.concatenate(seeds, axis=0)
    squares = [None] * (tokens // LANES)
    for tile in range(width // WIDE):
        at = slice(tile * WIDE, (tile + 1) * WIDE)
        tile_heads = range(at.start // channels, at.stop // channels)
        falls = [jnp.broadcast_to(decay[h : h + 1, :], (channels, state)) for h in tile_heads]
        seed = seeds[at, :]
        entering = seed.astype(F32) * jnp.concatenate(falls, axis=0)
        entering = entering + tail_ref[pl.ds(begin + at.start, WIDE), :].astype(F32)
        states = jnp.concatenate([seed, entering.astype(BF16)], axis=1)
        for block in range(tokens // LANES):
            rows = slice(block * LANES, (block + 1) * LANES)
            inflow = dot(read[rows, :], states, 1, 1)
            falls = [
                spread(scale[rows, :], (at.start + offset) // channels, channels)
                for offset in range(0, WIDE, LANES)
            ]
            inflow = inflow * jnp.concatenate(falls, axis=1)
            half = 0.5 * gate_ref[rows, pl.ds(begin + at.start, WIDE)].astype(F32)
            gated = inner_ref[rows, pl.ds(begin + at.start, WIDE)].astype(F32) + inflow
            gated = gated * (half + half * jnp.tanh(half))
            value_ref[rows, at] = gated
            square = gated * gated
            for part in range(WIDE // LANES):
                piece = square[:, part * LANES : (part + 1) * LANES]
                squares[block] = piece if squares[block] is None else squares[block] + piece
    for block in range(tokens // LANES):
        rows = slice(block * LANES, (block + 1) * LANES)
        mean = jnp.sum(squares[block], axis=1, keepdims=True) * (1.0 / width)
        norm = lax.rsqrt(mean + 1e-05)
        for tile in range(width // WIDE):
            at = slice(tile * WIDE, (tile + 1) * WIDE)
            out_ref[rows, at] = (value_ref[rows, at] * norm * gain_ref[:, at]).astype(BF16)


def shifted(value, axis, by):
    length = lax.axis_size(axis)
    return lax.ppermute(value, axis, [(i, i + by) for i in range(length - by)])


def params(limit=32):
    return pltpu.CompilerParams(vmem_limit_bytes=limit * MIB)


def whole(shape):
    return pl.BlockSpec(shape, lambda g: (0,) * len(shape))


def local(
    answer_lengths,
    mixer_input,
    gate_input,
    state_write,
    state_read,
    step_raw,
    decay_rate,
    skip_gain,
    norm_gain,
    prompt_state,
    queries,
    answer_keys,
    answer_values,
    prompt_keys,
    prompt_values,
):
    tokens, columns = mixer_input.shape
    heads = decay_rate.shape[0]
    state_rows, state = prompt_state.shape
    groups = state_write.shape[1] // state
    per_group = heads // groups
    channels = columns // heads
    width = per_group * channels
    prompt_rows, kv_width = prompt_keys.shape
    kv_count = kv_width // HD
    devices = lax.axis_size("reader")
    in_hbm = lambda value: pltpu.with_memory_space_constraint(value, pltpu.MemorySpace.HBM)
    prompt_state, prompt_keys, prompt_values = map(
        in_hbm, (prompt_state, prompt_keys, prompt_values)
    )
    lengths, rate, skip, gain = map(
        lambda value: in_hbm(value.reshape(1, -1)),
        (answer_lengths, decay_rate, skip_gain, norm_gain),
    )
    at_hand = pl.BlockSpec(memory_space=pltpu.VMEM)
    sizes = dict(heads=heads, per_group=per_group, channels=channels)
    packed_rows = state_rows + 2 * prompt_rows * kv_count

    packed = pl.pallas_call(
        pack_kernel,
        out_shape=jax.ShapeDtypeStruct((devices // NEAR, packed_rows, HD), BF16),
        out_specs=at_hand,
        compiler_params=params(),
        name="pack",
    )(prompt_state, prompt_keys, prompt_values)
    packed, near_keys = lax.optimization_barrier((packed, answer_keys))
    near = pl.pallas_call(
        join_kernel,
        out_shape=jax.ShapeDtypeStruct((tokens, 2 * kv_width), BF16),
        out_specs=at_hand,
        compiler_params=params(),
        name="join",
    )(in_hbm(near_keys), in_hbm(answer_values))
    packed, raw = lax.optimization_barrier((packed, step_raw.T))
    lines = [list(range(first, devices, NEAR)) for first in range(NEAR)]
    line = lax.all_to_all(packed, "reader", 0, 0, axis_index_groups=lines, tiled=True)
    prior = shifted(near, "reader", 1)
    raw = in_hbm(raw)

    small = pl.CostEstimate(flops=0, bytes_accessed=0, transcendentals=0)
    wide = pl.BlockSpec((tokens, width), lambda g: (0, g))
    tail, level, column, start = pl.pallas_call(
        functools.partial(tail_kernel, per_group=per_group, channels=channels),
        grid=(groups,),
        in_specs=[
            whole(lengths.shape),
            whole(raw.shape),
            whole((1, heads)),
            wide,
            pl.BlockSpec((tokens, state), lambda g: (0, g)),
        ],
        out_specs=(at_hand, at_hand, at_hand, at_hand),
        out_shape=(
            jax.ShapeDtypeStruct((columns + 2 * heads, state), BF16),
            jax.ShapeDtypeStruct((tokens, 2 * heads), F32),
            jax.ShapeDtypeStruct((heads, tokens), F32),
            jax.ShapeDtypeStruct((tokens, LANES), F32),
        ),
        scratch_shapes=[pltpu.VMEM((tokens, 2 * heads), F32)],
        compiler_params=params(),
        cost_estimate=small,
        name="tail",
    )(lengths, raw, rate, in_hbm(mixer_input), in_hbm(state_write))
    tail = shifted(tail, "reader", 1)
    inner = pl.pallas_call(
        functools.partial(inner_kernel, **sizes),
        grid=(groups,),
        in_specs=[
            at_hand,
            at_hand,
            at_hand,
            whole((1, heads)),
            at_hand,
            at_hand,
            at_hand,
        ],
        out_specs=at_hand,
        out_shape=jax.ShapeDtypeStruct((tokens, columns), BF16),
        compiler_params=params(),
        cost_estimate=small,
        name="inner",
    )(start, level, column, skip, mixer_input, state_write, state_read)
    prior, line, inner = lax.optimization_barrier((prior, line, inner))
    gathered = (line, lax.ppermute(line, "reader", [(i, i ^ 1) for i in range(devices)]))

    group_size = queries.shape[1] // kv_width
    attention_out = pl.pallas_call(
        functools.partial(
            attend_kernel,
            state_rows=state_rows,
            prompt_rows=prompt_rows,
            kv_count=kv_count,
        ),
        grid=(kv_count,),
        in_specs=[at_hand] * 5
        + [at_hand] * NEAR,
        out_specs=pl.BlockSpec((tokens, group_size * HD), lambda k: (0, k)),
        out_shape=jax.ShapeDtypeStruct(queries.shape, BF16),
        scratch_shapes=[pltpu.VMEM((tokens, tokens + LANES), F32)],
        compiler_params=params(),
        cost_estimate=small,
        name="attend",
    )(start, queries, answer_keys, answer_values, prior, *gathered)

    inner, attention_out = lax.optimization_barrier((inner, attention_out))
    mixer_out = pl.pallas_call(
        functools.partial(final_kernel, state_rows=state_rows, **sizes),
        grid=(groups,),
        in_specs=[
            at_hand,
            at_hand,
            at_hand,
            at_hand,
            at_hand,
            at_hand,
            pl.BlockSpec((1, width), lambda g: (0, g)),
        ]
        + [at_hand] * NEAR,
        out_specs=wide,
        out_shape=jax.ShapeDtypeStruct((tokens, columns), BF16),
        scratch_shapes=[pltpu.VMEM((tokens, width), F32)],
        compiler_params=params(),
        cost_estimate=small,
        name="final",
    )(start, level, tail, state_read, inner, gate_input, gain, *gathered)
    return (mixer_out, attention_out)


def solution(mesh):
    rows = P(("group", "reader"), None)
    in_specs = (P("group"),) + (rows,) * 5 + (P(),) * 3 + (rows,) * 6
    return jax.shard_map(
        local, mesh=mesh, in_specs=in_specs, out_specs=(rows, rows), check_vma=False
    )
```

```python
import functools
import math

import jax
import jax.numpy as jnp
from jax import lax
from jax.experimental import pallas as pl
from jax.experimental.pallas import tpu as pltpu
from jax.sharding import PartitionSpec as P

HD = 128
LANES = 128
WIDE = 256
NEAR = 2
LOG2E = 1.4426950408889634
F32 = jnp.float32
BF16 = jnp.bfloat16
MIB = 1 << 20


def iota(shape, dim):
    return lax.broadcasted_iota(jnp.int32, shape, dim)


def dot(a, b, ca=1, cb=0):
    return lax.dot_general(a, b, (((ca,), (cb,)), ((), ())), preferred_element_type=F32)


def expander(heads, group, per_group, channels):
    shape = (2 * heads, per_group * channels)
    row = iota(shape, 0)
    head = jnp.where(row >= heads, row - heads, row) - group * per_group
    column = iota(shape, 1)
    first = head * channels
    return jnp.where((column >= first) & (column < first + channels), 1.0, 0.0).astype(BF16)


def two_parts(value, heads):
    high = value.astype(BF16).astype(F32)
    return jnp.where(iota(value.shape, 1) < heads, high, value - high)


def to_front(value, head):
    return pltpu.roll(value, value.shape[1] - head, 1)


def spread(value, first, channels):
    lane = iota((8, LANES), 1)
    source = jnp.full((8, LANES), first, jnp.int32)
    for part in range(1, LANES // channels):
        source = source + jnp.where(lane >= part * channels, 1, 0)
    source = jnp.concatenate([source] * (value.shape[0] // 8), axis=0)
    return jnp.take_along_axis(value, source, axis=1, mode="promise_in_bounds")


def join_kernel(keys_ref, values_ref, out_ref):
    width = keys_ref.shape[1]
    out_ref[:, :width] = keys_ref[...]
    out_ref[:, width:] = values_ref[...]


def pack_kernel(state_ref, keys_ref, values_ref, out_ref):
    rows = state_ref.shape[0]
    state = state_ref[...].astype(BF16)
    parts = []
    for ref in (keys_ref, values_ref):
        wide = ref[...].astype(F32)
        for head in range(wide.shape[1] // HD):
            parts.append(wide[:, head * HD : (head + 1) * HD])
    parts = jnp.concatenate(parts, axis=0).astype(BF16)
    for copy in range(out_ref.shape[0]):
        out_ref[copy, :rows, :] = state
        out_ref[copy, rows:, :] = parts


def level_part(lengths_ref, raw_ref, rate_ref, level_ref, column_ref, start_ref, weight_ref, tail_ref):
    heads, tokens = raw_ref.shape
    base = (lax.axis_index("reader") * tokens).astype(F32)
    lengths = lengths_ref[...].astype(F32)
    answers = lengths.shape[1]
    square = (answers, answers)
    ends = jnp.sum(
        jnp.where(iota(square, 1) <= iota(square, 0), lengths, 0.0), axis=1, keepdims=True
    )
    place = base + iota((1, tokens), 1).astype(F32)
    start = jnp.max(jnp.where(ends <= place, ends, 0.0), axis=0, keepdims=True) - base
    start = jnp.broadcast_to(start, (LANES, tokens)).T
    start_ref[...] = start
    wide = jnp.concatenate([start] * (tokens // LANES), axis=1)
    square = (tokens, tokens)
    source = iota(square, 1)
    mask = (source.astype(F32) >= wide) & (source <= iota(square, 0))
    mask = jnp.where(mask, 1.0, 0.0).astype(BF16)
    raw = raw_ref[...]
    rate = jnp.broadcast_to(rate_ref[...], (heads, heads))
    diagonal = iota((heads, heads), 0) == iota((heads, heads), 1)
    rate = jnp.sum(jnp.where(diagonal, rate, 0.0), axis=1, keepdims=True)
    step = jnp.maximum(raw, 0.0) + jnp.log1p(jnp.exp(-jnp.abs(raw)))
    falling = -rate * step
    first = falling.astype(BF16)
    rest = falling - first.astype(F32)
    second = rest.astype(BF16)
    third = (rest - second.astype(F32)).astype(BF16)
    level = dot(first, mask, 1, 1) + (dot(second, mask, 1, 1) + dot(third, mask, 1, 1))
    column_ref[...] = level * LOG2E - jnp.log(step) * LOG2E
    last = level[:, tokens - 1 :]
    decay = jnp.exp(jnp.broadcast_to(last, (heads, tail_ref.shape[1])))
    high = decay.astype(BF16)
    low = (decay - high.astype(F32)).astype(BF16)
    tail_ref[tail_ref.shape[0] - 2 * heads :, :] = jnp.concatenate([high, low], axis=0)
    own = iota((heads, tokens), 1).astype(F32) >= start[tokens - 1 :, :1]
    weight = jnp.where(own, jnp.exp(last - level) * step, 0.0)
    weight_ref[...] = jnp.concatenate([weight, weight], axis=0).T
    level_ref[...] = jnp.concatenate([level, level], axis=0).T


def tail_part(group, weight_ref, x_ref, write_ref, tail_ref, per_group, channels):
    width = per_group * channels
    begin = pl.multiple_of(group * width, width)
    weight = to_front(weight_ref[...], group * per_group)
    weighted = []
    for tile in range(width // LANES):
        scale = spread(weight, tile * LANES // channels, channels)
        x = x_ref[:, tile * LANES : (tile + 1) * LANES].astype(F32)
        weighted.append((x * scale).astype(BF16))
    state = dot(jnp.concatenate(weighted, axis=1), write_ref[...], 0, 0)
    tail_ref[pl.ds(begin, width), :] = state.astype(BF16)


def tail_kernel(
    lengths_ref,
    raw_ref,
    rate_ref,
    x_ref,
    write_ref,
    tail_ref,
    level_ref,
    column_ref,
    start_ref,
    weight_ref,
    *,
    per_group,
    channels,
):
    group = pl.program_id(0)

    @pl.when(group == 0)
    def _():
        level_part(
            lengths_ref, raw_ref, rate_ref, level_ref, column_ref, start_ref, weight_ref, tail_ref
        )

    tail_part(group, weight_ref, x_ref, write_ref, tail_ref, per_group, channels)


def inner_kernel(
    start_ref,
    level_ref,
    column_ref,
    skip_ref,
    x_ref,
    write_ref,
    read_ref,
    out_ref,
    mark_ref,
    *,
    heads,
    per_group,
    channels,
):
    group = pl.program_id(0)
    tokens = x_ref.shape[0]
    mark_ref[...] = jnp.zeros_like(mark_ref)
    size = read_ref.shape[1] // (heads // per_group)
    own = pl.ds(pl.multiple_of(group * size, size), size)
    both = dot(read_ref[:, own], write_ref[:, own], 1, 1)
    square = (tokens, tokens)
    source = iota(square, 1)
    wide = jnp.concatenate([start_ref[...]] * (tokens // LANES), axis=1)
    both = jnp.where((source.astype(F32) >= wide) & (source <= iota(square, 0)), both, 0.0)
    lanes = level_ref.shape[1]
    level = pltpu.roll(level_ref[...] * LOG2E, lanes - group * per_group, 1)
    column = column_ref[pl.ds(pl.multiple_of(group * per_group, per_group), per_group), :]
    begin = pl.multiple_of(group * per_group * channels, per_group * channels)
    skip = jnp.concatenate([skip_ref[...]] * 2, axis=1)
    skip = two_parts(jnp.broadcast_to(skip, (16, 2 * heads)), heads).astype(BF16)
    skip = dot(skip, expander(heads, group, per_group, channels))[:1, :]
    per_tile = LANES // channels
    lane = iota((tokens, LANES), 1)
    for tile in range(per_group // per_tile):
        at = slice(tile * LANES, (tile + 1) * LANES)
        x = x_ref[:, pl.ds(begin + at.start, LANES)].astype(F32)
        owned = []
        for part in range(per_tile):
            mine = (lane >= part * channels) & (lane < (part + 1) * channels)
            owned.append(jnp.where(mine, x, 0.0).astype(BF16))
        for block in range(tokens // LANES):
            rows = slice(block * LANES, (block + 1) * LANES)
            reach = (block + 1) * LANES
            mixing = []
            for part in range(per_tile):
                head = tile * per_tile + part
                gap = level[rows, head : head + 1] - column[head : head + 1, :reach]
                mixing.append(
                    (jnp.exp2(jnp.minimum(gap, 64.0)) * both[rows, :reach]).astype(BF16)
                )
            total = dot(
                jnp.concatenate(mixing, axis=1),
                jnp.concatenate([value[:reach, :] for value in owned], axis=0),
            )
            out_ref[rows, pl.ds(begin + at.start, LANES)] = (
                total + skip[:, at] * x[rows, :]
            ).astype(BF16)


def attend_kernel(
    start_ref,
    query_ref,
    key_ref,
    value_ref,
    prior_ref,
    *rest,
    state_rows,
    prompt_rows,
    kv_count,
):
    gathered, (out_ref, mark_ref, bias_ref) = rest[:NEAR], rest[-3:]
    head = pl.program_id(0)
    mark_ref[...] = jnp.zeros_like(mark_ref)
    tokens = query_ref.shape[0]
    own = pl.ds(pl.multiple_of(head * HD, HD), HD)
    prompt_count = len(gathered) * gathered[0].shape[0] * prompt_rows
    queries = query_ref.shape[1] // HD
    scale = LOG2E / math.sqrt(HD)
    reach = tokens + LANES

    @pl.when(head == 0)
    def _():
        shape = (LANES, reach)
        wide = jnp.concatenate([start_ref[...]] * (reach // LANES), axis=1)
        for block in range(tokens // LANES):
            rows = slice(block * LANES, (block + 1) * LANES)
            place = iota(shape, 1) + (block * LANES - tokens)
            allowed = (place.astype(F32) >= wide[rows, :]) & (
                place <= iota(shape, 0) + block * LANES
            )
            bias_ref[rows, :] = jnp.where(allowed, 0.0, -jnp.inf)

    def prompt(which):
        at = pl.multiple_of(state_rows + (which * kv_count + head) // 2 * 2 * prompt_rows, 16)
        at = pl.ds(at, 2 * prompt_rows)
        pair = jnp.concatenate([ref[:, at, :] for ref in gathered], axis=0).astype(F32)
        odd = lax.rem(head, 2) == 1
        part = jnp.where(odd, pair[:, prompt_rows:, :], pair[:, :prompt_rows, :])
        return part.reshape(prompt_count, HD).astype(BF16)

    prompt_keys, prompt_values = prompt(0), prompt(1)
    prior = [
        prior_ref[:, pl.ds(pl.multiple_of((which * kv_count + head) * HD, HD), HD)]
        for which in range(2)
    ]
    near_keys = jnp.concatenate([prior[0], key_ref[:, own]], axis=0)
    near_values = jnp.concatenate([prior[1], value_ref[:, own]], axis=0)
    ones = jnp.ones((prompt_count + reach, LANES), BF16)
    for block in range(tokens // LANES):
        rows = slice(block * LANES, (block + 1) * LANES)
        window = slice(block * LANES, block * LANES + reach)
        keys = jnp.concatenate([prompt_keys, near_keys[window, :]], axis=0)
        values = jnp.concatenate([prompt_values, near_values[window, :]], axis=0)
        values = jnp.concatenate([values, ones], axis=1)
        stacked = [query_ref[rows, query * HD : (query + 1) * HD] for query in range(queries)]
        scores = dot(jnp.concatenate(stacked, axis=0), keys, 1, 1)
        weights = []
        for query in range(queries):
            own = scores[query * LANES : (query + 1) * LANES, :]
            far, near = own[:, :prompt_count], own[:, prompt_count:] + bias_ref[rows, :]
            own = jnp.concatenate([far, near], axis=1)
            top = jnp.max(own, axis=1, keepdims=True)
            weights.append(jnp.exp2((own - top) * scale).astype(BF16))
        summed = dot(jnp.concatenate(weights, axis=0), values)
        for query in range(queries):
            own = summed[query * LANES : (query + 1) * LANES, :]
            out_ref[rows, query * HD : (query + 1) * HD] = (own[:, :HD] / own[:, HD:]).astype(BF16)


def final_kernel(
    start_ref,
    level_ref,
    tail_ref,
    read_ref,
    inner_ref,
    gate_ref,
    gain_ref,
    *rest,
    state_rows,
    heads,
    per_group,
    channels,
):
    gathered, (out_ref, value_ref) = rest[:NEAR], rest[-2:]
    group = pl.program_id(0)
    tokens = read_ref.shape[0]
    width, state = per_group * channels, tail_ref.shape[1]

    scale = to_front(jnp.exp(level_ref[...]), group * per_group)
    carried = start_ref[:, :state] < 0
    read = read_ref[:, pl.ds(pl.multiple_of(group * state, state), state)].astype(F32)
    read = jnp.concatenate([jnp.where(carried, 0.0, read), jnp.where(carried, read, 0.0)], axis=1)
    read = read.astype(BF16)
    falls_at = heads * channels + pl.multiple_of(group * per_group, per_group)
    decay = tail_ref[pl.ds(falls_at, per_group), :].astype(F32)
    decay = decay + tail_ref[pl.ds(falls_at + heads, per_group), :].astype(F32)
    begin = pl.multiple_of(group * width, width)
    own = lax.rem(lax.axis_index("reader"), NEAR)
    seeds = []
    runs = width // (NEAR * state_rows)
    for run in range(runs):
        parts = [ref[group * runs + run, :state_rows, :] for ref in gathered]
        bit = 1
        while bit < NEAR:
            swap = lax.rem(own // bit, 2) == 1
            parts = [jnp.where(swap, parts[i ^ bit], parts[i]) for i in range(NEAR)]
            bit *= 2
        seeds += parts
    seeds = jnp.concatenate(seeds, axis=0)
    squares = [None] * (tokens // LANES)
    for tile in range(width // WIDE):
        at = slice(tile * WIDE, (tile + 1) * WIDE)
        tile_heads = range(at.start // channels, at.stop // channels)
        falls = [jnp.broadcast_to(decay[h : h + 1, :], (channels, state)) for h in tile_heads]
        seed = seeds[at, :]
        entering = seed.astype(F32) * jnp.concatenate(falls, axis=0)
        entering = entering + tail_ref[pl.ds(begin + at.start, WIDE), :].astype(F32)
        states = jnp.concatenate([seed, entering.astype(BF16)], axis=1)
        for block in range(tokens // LANES):
            rows = slice(block * LANES, (block + 1) * LANES)
            inflow = dot(read[rows, :], states, 1, 1)
            falls = [
                spread(scale[rows, :], (at.start + offset) // channels, channels)
                for offset in range(0, WIDE, LANES)
            ]
            inflow = inflow * jnp.concatenate(falls, axis=1)
            half = 0.5 * gate_ref[rows, pl.ds(begin + at.start, WIDE)].astype(F32)
            gated = inner_ref[rows, pl.ds(begin + at.start, WIDE)].astype(F32) + inflow
            gated = gated * (half + half * jnp.tanh(half))
            value_ref[rows, at] = gated
            square = gated * gated
            for part in range(WIDE // LANES):
                piece = square[:, part * LANES : (part + 1) * LANES]
                squares[block] = piece if squares[block] is None else squares[block] + piece
    for block in range(tokens // LANES):
        rows = slice(block * LANES, (block + 1) * LANES)
        mean = jnp.sum(squares[block], axis=1, keepdims=True) * (1.0 / width)
        norm = lax.rsqrt(mean + 1e-05)
        for tile in range(width // WIDE):
            at = slice(tile * WIDE, (tile + 1) * WIDE)
            out_ref[rows, at] = (value_ref[rows, at] * norm * gain_ref[:, at]).astype(BF16)


def shifted(value, axis, by):
    length = lax.axis_size(axis)
    return lax.ppermute(value, axis, [(i, i + by) for i in range(length - by)])


def params(limit=32):
    return pltpu.CompilerParams(vmem_limit_bytes=limit * MIB)


def whole(shape):
    return pl.BlockSpec(shape, lambda g: (0,) * len(shape))


def local(
    answer_lengths,
    mixer_input,
    gate_input,
    state_write,
    state_read,
    step_raw,
    decay_rate,
    skip_gain,
    norm_gain,
    prompt_state,
    queries,
    answer_keys,
    answer_values,
    prompt_keys,
    prompt_values,
):
    tokens, columns = mixer_input.shape
    heads = decay_rate.shape[0]
    state_rows, state = prompt_state.shape
    groups = state_write.shape[1] // state
    per_group = heads // groups
    channels = columns // heads
    width = per_group * channels
    prompt_rows, kv_width = prompt_keys.shape
    kv_count = kv_width // HD
    devices = lax.axis_size("reader")
    in_hbm = lambda value: pltpu.with_memory_space_constraint(value, pltpu.MemorySpace.HBM)
    prompt_state, prompt_keys, prompt_values = map(
        in_hbm, (prompt_state, prompt_keys, prompt_values)
    )
    lengths, rate, skip, gain = map(
        lambda value: in_hbm(value.reshape(1, -1)),
        (answer_lengths, decay_rate, skip_gain, norm_gain),
    )
    at_hand = pl.BlockSpec(memory_space=pltpu.VMEM)
    sizes = dict(heads=heads, per_group=per_group, channels=channels)
    packed_rows = state_rows + 2 * prompt_rows * kv_count

    packed = pl.pallas_call(
        pack_kernel,
        out_shape=jax.ShapeDtypeStruct((devices // NEAR, packed_rows, HD), BF16),
        out_specs=at_hand,
        compiler_params=params(),
        name="pack",
    )(prompt_state, prompt_keys, prompt_values)
    packed, near_keys = lax.optimization_barrier((packed, answer_keys))
    near = pl.pallas_call(
        join_kernel,
        out_shape=jax.ShapeDtypeStruct((tokens, 2 * kv_width), BF16),
        out_specs=at_hand,
        compiler_params=params(),
        name="join",
    )(in_hbm(near_keys), in_hbm(answer_values))
    packed, raw = lax.optimization_barrier((packed, step_raw.T))
    lines = [list(range(first, devices, NEAR)) for first in range(NEAR)]
    line = lax.all_to_all(packed, "reader", 0, 0, axis_index_groups=lines, tiled=True)
    prior = shifted(near, "reader", 1)
    raw = in_hbm(raw)

    small = pl.CostEstimate(flops=0, bytes_accessed=0, transcendentals=0)
    wide = pl.BlockSpec((tokens, width), lambda g: (0, g))
    tail, level, column, start = pl.pallas_call(
        functools.partial(tail_kernel, per_group=per_group, channels=channels),
        grid=(groups,),
        in_specs=[
            whole(lengths.shape),
            whole(raw.shape),
            whole((1, heads)),
            wide,
            pl.BlockSpec((tokens, state), lambda g: (0, g)),
        ],
        out_specs=(at_hand, at_hand, at_hand, at_hand),
        out_shape=(
            jax.ShapeDtypeStruct((columns + 2 * heads, state), BF16),
            jax.ShapeDtypeStruct((tokens, 2 * heads), F32),
            jax.ShapeDtypeStruct((heads, tokens), F32),
            jax.ShapeDtypeStruct((tokens, LANES), F32),
        ),
        scratch_shapes=[pltpu.VMEM((tokens, 2 * heads), F32)],
        compiler_params=params(),
        cost_estimate=small,
        name="tail",
    )(lengths, raw, rate, in_hbm(mixer_input), in_hbm(state_write))
    tail = shifted(tail, "reader", 1)
    inner, mark = pl.pallas_call(
        functools.partial(inner_kernel, **sizes),
        grid=(groups,),
        in_specs=[
            at_hand,
            at_hand,
            at_hand,
            whole((1, heads)),
            at_hand,
            at_hand,
            at_hand,
        ],
        out_specs=(at_hand, at_hand),
        out_shape=(
            jax.ShapeDtypeStruct((tokens, columns), BF16),
            jax.ShapeDtypeStruct((8, LANES), F32),
        ),
        compiler_params=params(),
        cost_estimate=small,
        name="inner",
    )(start, level, column, skip, mixer_input, state_write, state_read)
    prior, line, mark = lax.optimization_barrier((prior, line, mark))
    gathered = (line, lax.ppermute(line, "reader", [(i, i ^ 1) for i in range(devices)]))

    group_size = queries.shape[1] // kv_width
    attention_out, mark = pl.pallas_call(
        functools.partial(
            attend_kernel,
            state_rows=state_rows,
            prompt_rows=prompt_rows,
            kv_count=kv_count,
        ),
        grid=(kv_count,),
        in_specs=[
            at_hand,
            pl.BlockSpec((tokens, group_size * HD), lambda k: (0, k)),
            at_hand,
            at_hand,
            at_hand,
        ]
        + [at_hand] * NEAR
        + [pl.BlockSpec(memory_space=pl.ANY)],
        out_specs=(pl.BlockSpec((tokens, group_size * HD), lambda k: (0, k)), at_hand),
        out_shape=(
            jax.ShapeDtypeStruct(queries.shape, BF16),
            jax.ShapeDtypeStruct((8, LANES), F32),
        ),
        scratch_shapes=[pltpu.VMEM((tokens, tokens + LANES), F32)],
        compiler_params=params(),
        cost_estimate=small,
        name="attend",
    )(start, in_hbm(queries), answer_keys, answer_values, prior, *gathered, mark)

    mixer_out = pl.pallas_call(
        functools.partial(final_kernel, state_rows=state_rows, **sizes),
        grid=(groups,),
        in_specs=[
            at_hand,
            at_hand,
            at_hand,
            at_hand,
            at_hand,
            at_hand,
            pl.BlockSpec((1, width), lambda g: (0, g)),
        ]
        + [at_hand] * NEAR
        + [pl.BlockSpec(memory_space=pl.ANY)],
        out_specs=wide,
        out_shape=jax.ShapeDtypeStruct((tokens, columns), BF16),
        scratch_shapes=[pltpu.VMEM((tokens, width), F32)],
        compiler_params=params(),
        cost_estimate=small,
        name="final",
    )(start, level, tail, state_read, inner, gate_input, gain, *gathered, mark)
    return (mixer_out, attention_out)


def solution(mesh):
    rows = P(("group", "reader"), None)
    in_specs = (P("group"),) + (rows,) * 5 + (P(),) * 3 + (rows,) * 6
    return jax.shard_map(
        local, mesh=mesh, in_specs=in_specs, out_specs=(rows, rows), check_vma=False
    )
```

```python
import functools
import math

import jax
import jax.numpy as jnp
from jax import lax
from jax.experimental import pallas as pl
from jax.experimental.pallas import tpu as pltpu
from jax.sharding import PartitionSpec as P

HD = 128
LANES = 128
WIDE = 256
NEAR = 2
LOG2E = 1.4426950408889634
F32 = jnp.float32
BF16 = jnp.bfloat16
MIB = 1 << 20


def iota(shape, dim):
    return lax.broadcasted_iota(jnp.int32, shape, dim)


def dot(a, b, ca=1, cb=0):
    return lax.dot_general(a, b, (((ca,), (cb,)), ((), ())), preferred_element_type=F32)


def expander(heads, group, per_group, channels):
    shape = (2 * heads, per_group * channels)
    row = iota(shape, 0)
    head = jnp.where(row >= heads, row - heads, row) - group * per_group
    column = iota(shape, 1)
    first = head * channels
    return jnp.where((column >= first) & (column < first + channels), 1.0, 0.0).astype(BF16)


def two_parts(value, heads):
    high = value.astype(BF16).astype(F32)
    return jnp.where(iota(value.shape, 1) < heads, high, value - high)


def to_front(value, head):
    return pltpu.roll(value, value.shape[1] - head, 1)


def spread(value, first, channels):
    lane = iota((8, LANES), 1)
    source = jnp.full((8, LANES), first, jnp.int32)
    for part in range(1, LANES // channels):
        source = source + jnp.where(lane >= part * channels, 1, 0)
    source = jnp.concatenate([source] * (value.shape[0] // 8), axis=0)
    return jnp.take_along_axis(value, source, axis=1, mode="promise_in_bounds")


def join_kernel(keys_ref, values_ref, out_ref):
    width = keys_ref.shape[1]
    out_ref[:, :width] = keys_ref[...]
    out_ref[:, width:] = values_ref[...]


def pack_kernel(state_ref, keys_ref, values_ref, out_ref):
    rows = state_ref.shape[0]
    state = state_ref[...].astype(BF16)
    parts = []
    for ref in (keys_ref, values_ref):
        wide = ref[...].astype(F32)
        for head in range(wide.shape[1] // HD):
            parts.append(wide[:, head * HD : (head + 1) * HD])
    parts = jnp.concatenate(parts, axis=0).astype(BF16)
    for copy in range(out_ref.shape[0]):
        out_ref[copy, :rows, :] = state
        out_ref[copy, rows:, :] = parts


def level_part(lengths_ref, raw_ref, rate_ref, level_ref, column_ref, start_ref, weight_ref, tail_ref):
    heads, tokens = raw_ref.shape
    base = (lax.axis_index("reader") * tokens).astype(F32)
    lengths = lengths_ref[...].astype(F32)
    answers = lengths.shape[1]
    square = (answers, answers)
    ends = jnp.sum(
        jnp.where(iota(square, 1) <= iota(square, 0), lengths, 0.0), axis=1, keepdims=True
    )
    place = base + iota((1, tokens), 1).astype(F32)
    start = jnp.max(jnp.where(ends <= place, ends, 0.0), axis=0, keepdims=True) - base
    start = jnp.broadcast_to(start, (LANES, tokens)).T
    start_ref[...] = start
    wide = jnp.concatenate([start] * (tokens // LANES), axis=1)
    square = (tokens, tokens)
    source = iota(square, 1)
    mask = (source.astype(F32) >= wide) & (source <= iota(square, 0))
    mask = jnp.where(mask, 1.0, 0.0).astype(BF16)
    raw = raw_ref[...]
    rate = jnp.broadcast_to(rate_ref[...], (heads, heads))
    diagonal = iota((heads, heads), 0) == iota((heads, heads), 1)
    rate = jnp.sum(jnp.where(diagonal, rate, 0.0), axis=1, keepdims=True)
    step = jnp.maximum(raw, 0.0) + jnp.log1p(jnp.exp(-jnp.abs(raw)))
    falling = -rate * step
    first = falling.astype(BF16)
    rest = falling - first.astype(F32)
    second = rest.astype(BF16)
    third = (rest - second.astype(F32)).astype(BF16)
    level = dot(first, mask, 1, 1) + (dot(second, mask, 1, 1) + dot(third, mask, 1, 1))
    column_ref[...] = level * LOG2E - jnp.log(step) * LOG2E
    last = level[:, tokens - 1 :]
    decay = jnp.exp(jnp.broadcast_to(last, (heads, tail_ref.shape[1])))
    high = decay.astype(BF16)
    low = (decay - high.astype(F32)).astype(BF16)
    tail_ref[tail_ref.shape[0] - 2 * heads :, :] = jnp.concatenate([high, low], axis=0)
    own = iota((heads, tokens), 1).astype(F32) >= start[tokens - 1 :, :1]
    weight = jnp.where(own, jnp.exp(last - level) * step, 0.0)
    weight_ref[...] = jnp.concatenate([weight, weight], axis=0).T
    level_ref[...] = jnp.concatenate([level, level], axis=0).T


def tail_part(group, weight_ref, x_ref, write_ref, tail_ref, per_group, channels):
    width = per_group * channels
    begin = pl.multiple_of(group * width, width)
    weight = to_front(weight_ref[...], group * per_group)
    weighted = []
    for tile in range(width // LANES):
        scale = spread(weight, tile * LANES // channels, channels)
        x = x_ref[:, tile * LANES : (tile + 1) * LANES].astype(F32)
        weighted.append((x * scale).astype(BF16))
    state = dot(jnp.concatenate(weighted, axis=1), write_ref[...], 0, 0)
    tail_ref[pl.ds(begin, width), :] = state.astype(BF16)


def tail_kernel(
    lengths_ref,
    raw_ref,
    rate_ref,
    x_ref,
    write_ref,
    tail_ref,
    level_ref,
    column_ref,
    start_ref,
    weight_ref,
    *,
    per_group,
    channels,
):
    group = pl.program_id(0)

    @pl.when(group == 0)
    def _():
        level_part(
            lengths_ref, raw_ref, rate_ref, level_ref, column_ref, start_ref, weight_ref, tail_ref
        )

    tail_part(group, weight_ref, x_ref, write_ref, tail_ref, per_group, channels)


def inner_kernel(
    start_ref,
    level_ref,
    column_ref,
    skip_ref,
    x_ref,
    write_ref,
    read_ref,
    out_ref,
    mark_ref,
    *,
    heads,
    per_group,
    channels,
):
    group = pl.program_id(0)
    tokens = x_ref.shape[0]
    mark_ref[...] = jnp.zeros_like(mark_ref)
    size = read_ref.shape[1] // (heads // per_group)
    own = pl.ds(pl.multiple_of(group * size, size), size)
    both = dot(read_ref[:, own], write_ref[:, own], 1, 1)
    square = (tokens, tokens)
    source = iota(square, 1)
    wide = jnp.concatenate([start_ref[...]] * (tokens // LANES), axis=1)
    both = jnp.where((source.astype(F32) >= wide) & (source <= iota(square, 0)), both, 0.0)
    lanes = level_ref.shape[1]
    level = pltpu.roll(level_ref[...] * LOG2E, lanes - group * per_group, 1)
    column = column_ref[pl.ds(pl.multiple_of(group * per_group, per_group), per_group), :]
    begin = pl.multiple_of(group * per_group * channels, per_group * channels)
    skip = jnp.concatenate([skip_ref[...]] * 2, axis=1)
    skip = two_parts(jnp.broadcast_to(skip, (16, 2 * heads)), heads).astype(BF16)
    skip = dot(skip, expander(heads, group, per_group, channels))[:1, :]
    per_tile = LANES // channels
    lane = iota((tokens, LANES), 1)
    for tile in range(per_group // per_tile):
        at = slice(tile * LANES, (tile + 1) * LANES)
        x = x_ref[:, pl.ds(begin + at.start, LANES)].astype(F32)
        owned = []
        for part in range(per_tile):
            mine = (lane >= part * channels) & (lane < (part + 1) * channels)
            owned.append(jnp.where(mine, x, 0.0).astype(BF16))
        for block in range(tokens // LANES):
            rows = slice(block * LANES, (block + 1) * LANES)
            reach = (block + 1) * LANES
            mixing = []
            for part in range(per_tile):
                head = tile * per_tile + part
                gap = level[rows, head : head + 1] - column[head : head + 1, :reach]
                mixing.append(
                    (jnp.exp2(jnp.minimum(gap, 64.0)) * both[rows, :reach]).astype(BF16)
                )
            total = dot(
                jnp.concatenate(mixing, axis=1),
                jnp.concatenate([value[:reach, :] for value in owned], axis=0),
            )
            out_ref[rows, pl.ds(begin + at.start, LANES)] = (
                total + skip[:, at] * x[rows, :]
            ).astype(BF16)


def attend_kernel(
    start_ref,
    query_ref,
    key_ref,
    value_ref,
    prior_key_ref,
    prior_value_ref,
    *rest,
    state_rows,
    prompt_rows,
    kv_count,
):
    gathered, (out_ref, mark_ref, bias_ref) = rest[:NEAR], rest[-3:]
    head = pl.program_id(0)
    mark_ref[...] = jnp.zeros_like(mark_ref)
    tokens = query_ref.shape[0]
    prompt_count = len(gathered) * gathered[0].shape[0] * prompt_rows
    queries = query_ref.shape[1] // HD
    scale = LOG2E / math.sqrt(HD)
    reach = tokens + LANES

    @pl.when(head == 0)
    def _():
        shape = (LANES, reach)
        wide = jnp.concatenate([start_ref[...]] * (reach // LANES), axis=1)
        for block in range(tokens // LANES):
            rows = slice(block * LANES, (block + 1) * LANES)
            place = iota(shape, 1) + (block * LANES - tokens)
            allowed = (place.astype(F32) >= wide[rows, :]) & (
                place <= iota(shape, 0) + block * LANES
            )
            bias_ref[rows, :] = jnp.where(allowed, 0.0, -jnp.inf)

    def prompt(which):
        at = pl.multiple_of(state_rows + (which * kv_count + head) // 2 * 2 * prompt_rows, 16)
        at = pl.ds(at, 2 * prompt_rows)
        pair = jnp.concatenate([ref[:, at, :] for ref in gathered], axis=0).astype(F32)
        odd = lax.rem(head, 2) == 1
        part = jnp.where(odd, pair[:, prompt_rows:, :], pair[:, :prompt_rows, :])
        return part.reshape(prompt_count, HD).astype(BF16)

    prompt_keys, prompt_values = prompt(0), prompt(1)
    near_keys = jnp.concatenate([prior_key_ref[...], key_ref[...]], axis=0)
    near_values = jnp.concatenate([prior_value_ref[...], value_ref[...]], axis=0)
    ones = jnp.ones((prompt_count + reach, LANES), BF16)
    for block in range(tokens // LANES):
        rows = slice(block * LANES, (block + 1) * LANES)
        window = slice(block * LANES, block * LANES + reach)
        keys = jnp.concatenate([prompt_keys, near_keys[window, :]], axis=0)
        values = jnp.concatenate([prompt_values, near_values[window, :]], axis=0)
        values = jnp.concatenate([values, ones], axis=1)
        stacked = [query_ref[rows, query * HD : (query + 1) * HD] for query in range(queries)]
        scores = dot(jnp.concatenate(stacked, axis=0), keys, 1, 1)
        weights = []
        for query in range(queries):
            own = scores[query * LANES : (query + 1) * LANES, :]
            far, near = own[:, :prompt_count], own[:, prompt_count:] + bias_ref[rows, :]
            own = jnp.concatenate([far, near], axis=1)
            top = jnp.max(own, axis=1, keepdims=True)
            weights.append(jnp.exp2((own - top) * scale).astype(BF16))
        summed = dot(jnp.concatenate(weights, axis=0), values)
        for query in range(queries):
            own = summed[query * LANES : (query + 1) * LANES, :]
            out_ref[rows, query * HD : (query + 1) * HD] = (own[:, :HD] / own[:, HD:]).astype(BF16)


def final_kernel(
    start_ref,
    level_ref,
    tail_ref,
    decay_ref,
    read_ref,
    inner_ref,
    gate_ref,
    gain_ref,
    *rest,
    state_rows,
    heads,
    per_group,
    channels,
):
    gathered, (out_ref, value_ref) = rest[:NEAR], rest[-2:]
    group = pl.program_id(0)
    tokens = read_ref.shape[0]
    width, state = per_group * channels, tail_ref.shape[1]

    scale = to_front(jnp.exp(level_ref[...]), group * per_group)
    carried = start_ref[:, :state] < 0
    read = read_ref[...].astype(F32)
    read = jnp.concatenate([jnp.where(carried, 0.0, read), jnp.where(carried, read, 0.0)], axis=1)
    read = read.astype(BF16)
    falls_at = pl.multiple_of(group * per_group, per_group)
    decay = decay_ref[pl.ds(falls_at, per_group), :].astype(F32)
    decay = decay + decay_ref[pl.ds(falls_at + heads, per_group), :].astype(F32)
    begin = pl.multiple_of(group * width, width)
    own = lax.rem(lax.axis_index("reader"), NEAR)
    seeds = []
    runs = width // (NEAR * state_rows)
    for run in range(runs):
        parts = [ref[group * runs + run, :state_rows, :] for ref in gathered]
        bit = 1
        while bit < NEAR:
            swap = lax.rem(own // bit, 2) == 1
            parts = [jnp.where(swap, parts[i ^ bit], parts[i]) for i in range(NEAR)]
            bit *= 2
        seeds += parts
    seeds = jnp.concatenate(seeds, axis=0)
    squares = [None] * (tokens // LANES)
    for tile in range(width // WIDE):
        at = slice(tile * WIDE, (tile + 1) * WIDE)
        tile_heads = range(at.start // channels, at.stop // channels)
        falls = [jnp.broadcast_to(decay[h : h + 1, :], (channels, state)) for h in tile_heads]
        seed = seeds[at, :]
        entering = seed.astype(F32) * jnp.concatenate(falls, axis=0)
        entering = entering + tail_ref[at, :].astype(F32)
        states = jnp.concatenate([seed, entering.astype(BF16)], axis=1)
        for block in range(tokens // LANES):
            rows = slice(block * LANES, (block + 1) * LANES)
            inflow = dot(read[rows, :], states, 1, 1)
            falls = [
                spread(scale[rows, :], (at.start + offset) // channels, channels)
                for offset in range(0, WIDE, LANES)
            ]
            inflow = inflow * jnp.concatenate(falls, axis=1)
            half = 0.5 * gate_ref[rows, at].astype(F32)
            gated = inner_ref[rows, pl.ds(begin + at.start, WIDE)].astype(F32) + inflow
            gated = gated * (half + half * jnp.tanh(half))
            value_ref[rows, at] = gated
            square = gated * gated
            for part in range(WIDE // LANES):
                piece = square[:, part * LANES : (part + 1) * LANES]
                squares[block] = piece if squares[block] is None else squares[block] + piece
    for block in range(tokens // LANES):
        rows = slice(block * LANES, (block + 1) * LANES)
        mean = jnp.sum(squares[block], axis=1, keepdims=True) * (1.0 / width)
        norm = lax.rsqrt(mean + 1e-05)
        for tile in range(width // WIDE):
            at = slice(tile * WIDE, (tile + 1) * WIDE)
            out_ref[rows, at] = (value_ref[rows, at] * norm * gain_ref[:, at]).astype(BF16)


def shifted(value, axis, by):
    length = lax.axis_size(axis)
    return lax.ppermute(value, axis, [(i, i + by) for i in range(length - by)])


def params(limit=32):
    return pltpu.CompilerParams(vmem_limit_bytes=limit * MIB)


def whole(shape):
    return pl.BlockSpec(shape, lambda g: (0,) * len(shape))


def local(
    answer_lengths,
    mixer_input,
    gate_input,
    state_write,
    state_read,
    step_raw,
    decay_rate,
    skip_gain,
    norm_gain,
    prompt_state,
    queries,
    answer_keys,
    answer_values,
    prompt_keys,
    prompt_values,
):
    tokens, columns = mixer_input.shape
    heads = decay_rate.shape[0]
    state_rows, state = prompt_state.shape
    groups = state_write.shape[1] // state
    per_group = heads // groups
    channels = columns // heads
    width = per_group * channels
    prompt_rows, kv_width = prompt_keys.shape
    kv_count = kv_width // HD
    devices = lax.axis_size("reader")
    in_hbm = lambda value: pltpu.with_memory_space_constraint(value, pltpu.MemorySpace.HBM)
    prompt_state, prompt_keys, prompt_values = map(
        in_hbm, (prompt_state, prompt_keys, prompt_values)
    )
    lengths, rate, skip, gain = map(
        lambda value: in_hbm(value.reshape(1, -1)),
        (answer_lengths, decay_rate, skip_gain, norm_gain),
    )
    at_hand = pl.BlockSpec(memory_space=pltpu.VMEM)
    sizes = dict(heads=heads, per_group=per_group, channels=channels)
    packed_rows = state_rows + 2 * prompt_rows * kv_count

    packed = pl.pallas_call(
        pack_kernel,
        out_shape=jax.ShapeDtypeStruct((devices // NEAR, packed_rows, HD), BF16),
        out_specs=at_hand,
        compiler_params=params(),
        name="pack",
    )(prompt_state, prompt_keys, prompt_values)
    packed, near_keys = lax.optimization_barrier((packed, answer_keys))
    near = pl.pallas_call(
        join_kernel,
        out_shape=jax.ShapeDtypeStruct((tokens, 2 * kv_width), BF16),
        out_specs=at_hand,
        compiler_params=params(),
        name="join",
    )(in_hbm(near_keys), in_hbm(answer_values))
    packed, raw = lax.optimization_barrier((packed, step_raw.T))
    lines = [list(range(first, devices, NEAR)) for first in range(NEAR)]
    line = lax.all_to_all(packed, "reader", 0, 0, axis_index_groups=lines, tiled=True)
    prior = shifted(near, "reader", 1)
    raw = in_hbm(raw)

    small = pl.CostEstimate(flops=0, bytes_accessed=0, transcendentals=0)
    wide = pl.BlockSpec((tokens, width), lambda g: (0, g))
    tail, level, column, start = pl.pallas_call(
        functools.partial(tail_kernel, per_group=per_group, channels=channels),
        grid=(groups,),
        in_specs=[
            whole(lengths.shape),
            whole(raw.shape),
            whole((1, heads)),
            wide,
            pl.BlockSpec((tokens, state), lambda g: (0, g)),
        ],
        out_specs=(at_hand, at_hand, at_hand, at_hand),
        out_shape=(
            jax.ShapeDtypeStruct((columns + 2 * heads, state), BF16),
            jax.ShapeDtypeStruct((tokens, 2 * heads), F32),
            jax.ShapeDtypeStruct((heads, tokens), F32),
            jax.ShapeDtypeStruct((tokens, LANES), F32),
        ),
        scratch_shapes=[pltpu.VMEM((tokens, 2 * heads), F32)],
        compiler_params=params(),
        cost_estimate=small,
        name="tail",
    )(lengths, raw, rate, in_hbm(mixer_input), in_hbm(state_write))
    tail = shifted(tail, "reader", 1)
    inner, mark = pl.pallas_call(
        functools.partial(inner_kernel, **sizes),
        grid=(groups,),
        in_specs=[
            at_hand,
            at_hand,
            at_hand,
            whole((1, heads)),
            at_hand,
            at_hand,
            at_hand,
        ],
        out_specs=(at_hand, at_hand),
        out_shape=(
            jax.ShapeDtypeStruct((tokens, columns), BF16),
            jax.ShapeDtypeStruct((8, LANES), F32),
        ),
        compiler_params=params(),
        cost_estimate=small,
        name="inner",
    )(start, level, column, skip, mixer_input, state_write, state_read)
    prior, line, mark = lax.optimization_barrier((prior, line, mark))
    gathered = (line, lax.ppermute(line, "reader", [(i, i ^ 1) for i in range(devices)]))

    group_size = queries.shape[1] // kv_width
    attention_out, mark = pl.pallas_call(
        functools.partial(
            attend_kernel,
            state_rows=state_rows,
            prompt_rows=prompt_rows,
            kv_count=kv_count,
        ),
        grid=(kv_count,),
        in_specs=[
            at_hand,
            pl.BlockSpec((tokens, group_size * HD), lambda k: (0, k)),
            pl.BlockSpec((tokens, HD), lambda k: (0, k)),
            pl.BlockSpec((tokens, HD), lambda k: (0, k)),
            pl.BlockSpec((tokens, HD), lambda k: (0, k)),
            pl.BlockSpec((tokens, HD), lambda k: (0, kv_count + k)),
        ]
        + [at_hand] * NEAR
        + [pl.BlockSpec(memory_space=pl.ANY)],
        out_specs=(pl.BlockSpec((tokens, group_size * HD), lambda k: (0, k)), at_hand),
        out_shape=(
            jax.ShapeDtypeStruct(queries.shape, BF16),
            jax.ShapeDtypeStruct((8, LANES), F32),
        ),
        scratch_shapes=[pltpu.VMEM((tokens, tokens + LANES), F32)],
        compiler_params=params(),
        cost_estimate=small,
        name="attend",
    )(start, *map(in_hbm, (queries, answer_keys, answer_values)), prior, prior, *gathered, mark)

    mixer_out = pl.pallas_call(
        functools.partial(final_kernel, state_rows=state_rows, **sizes),
        grid=(groups,),
        in_specs=[
            at_hand,
            at_hand,
            pl.BlockSpec((width, state), lambda g: (g, 0)),
            pl.BlockSpec((2 * heads, state), lambda g: (columns // (2 * heads), 0)),
            pl.BlockSpec((tokens, state), lambda g: (0, g)),
            at_hand,
            wide,
            pl.BlockSpec((1, width), lambda g: (0, g)),
        ]
        + [at_hand] * NEAR
        + [pl.BlockSpec(memory_space=pl.ANY)],
        out_specs=wide,
        out_shape=jax.ShapeDtypeStruct((tokens, columns), BF16),
        scratch_shapes=[pltpu.VMEM((tokens, width), F32)],
        compiler_params=params(),
        cost_estimate=small,
        name="final",
    )(start, level, tail, tail, in_hbm(state_read), inner, in_hbm(gate_input), gain, *gathered, mark)
    return (mixer_out, attention_out)


def solution(mesh):
    rows = P(("group", "reader"), None)
    in_specs = (P("group"),) + (rows,) * 5 + (P(),) * 3 + (rows,) * 6
    return jax.shard_map(
        local, mesh=mesh, in_specs=in_specs, out_specs=(rows, rows), check_vma=False
    )
```

```python
import functools
import math

import jax
import jax.numpy as jnp
from jax import lax
from jax.experimental import pallas as pl
from jax.experimental.pallas import tpu as pltpu
from jax.sharding import PartitionSpec as P

HD = 128
LANES = 128
WIDE = 256
NEAR = 2
LOG2E = 1.4426950408889634
F32 = jnp.float32
BF16 = jnp.bfloat16
MIB = 1 << 20


def iota(shape, dim):
    return lax.broadcasted_iota(jnp.int32, shape, dim)


def dot(a, b, ca=1, cb=0):
    return lax.dot_general(a, b, (((ca,), (cb,)), ((), ())), preferred_element_type=F32)


def expander(heads, group, per_group, channels):
    shape = (2 * heads, per_group * channels)
    row = iota(shape, 0)
    head = jnp.where(row >= heads, row - heads, row) - group * per_group
    column = iota(shape, 1)
    first = head * channels
    return jnp.where((column >= first) & (column < first + channels), 1.0, 0.0).astype(BF16)


def two_parts(value, heads):
    high = value.astype(BF16).astype(F32)
    return jnp.where(iota(value.shape, 1) < heads, high, value - high)


def to_front(value, head):
    return pltpu.roll(value, value.shape[1] - head, 1)


def spread(value, first, channels):
    lane = iota((8, LANES), 1)
    source = jnp.full((8, LANES), first, jnp.int32)
    for part in range(1, LANES // channels):
        source = source + jnp.where(lane >= part * channels, 1, 0)
    source = jnp.concatenate([source] * (value.shape[0] // 8), axis=0)
    return jnp.take_along_axis(value, source, axis=1, mode="promise_in_bounds")


def join_kernel(keys_ref, values_ref, out_ref):
    width = keys_ref.shape[1]
    out_ref[:, :width] = keys_ref[...]
    out_ref[:, width:] = values_ref[...]


def pack_kernel(state_ref, keys_ref, values_ref, out_ref):
    rows = state_ref.shape[0]
    state = state_ref[...].astype(BF16)
    parts = []
    for ref in (keys_ref, values_ref):
        wide = ref[...].astype(F32)
        for head in range(wide.shape[1] // HD):
            parts.append(wide[:, head * HD : (head + 1) * HD])
    parts = jnp.concatenate(parts, axis=0).astype(BF16)
    for copy in range(out_ref.shape[0]):
        out_ref[copy, :rows, :] = state
        out_ref[copy, rows:, :] = parts


def level_part(lengths_ref, raw_ref, rate_ref, level_ref, column_ref, start_ref, weight_ref, tail_ref):
    heads, tokens = raw_ref.shape
    base = (lax.axis_index("reader") * tokens).astype(F32)
    lengths = lengths_ref[...].astype(F32)
    answers = lengths.shape[1]
    square = (answers, answers)
    ends = jnp.sum(
        jnp.where(iota(square, 1) <= iota(square, 0), lengths, 0.0), axis=1, keepdims=True
    )
    place = base + iota((1, tokens), 1).astype(F32)
    start = jnp.max(jnp.where(ends <= place, ends, 0.0), axis=0, keepdims=True) - base
    start = jnp.broadcast_to(start, (LANES, tokens)).T
    start_ref[...] = start
    wide = jnp.concatenate([start] * (tokens // LANES), axis=1)
    square = (tokens, tokens)
    source = iota(square, 1)
    mask = (source.astype(F32) >= wide) & (source <= iota(square, 0))
    mask = jnp.where(mask, 1.0, 0.0).astype(BF16)
    raw = raw_ref[...]
    rate = jnp.broadcast_to(rate_ref[...], (heads, heads))
    diagonal = iota((heads, heads), 0) == iota((heads, heads), 1)
    rate = jnp.sum(jnp.where(diagonal, rate, 0.0), axis=1, keepdims=True)
    step = jnp.maximum(raw, 0.0) + jnp.log1p(jnp.exp(-jnp.abs(raw)))
    falling = -rate * step
    first = falling.astype(BF16)
    rest = falling - first.astype(F32)
    second = rest.astype(BF16)
    third = (rest - second.astype(F32)).astype(BF16)
    level = dot(first, mask, 1, 1) + (dot(second, mask, 1, 1) + dot(third, mask, 1, 1))
    column_ref[...] = level * LOG2E - jnp.log(step) * LOG2E
    last = level[:, tokens - 1 :]
    decay = jnp.exp(jnp.broadcast_to(last, (heads, tail_ref.shape[1])))
    high = decay.astype(BF16)
    low = (decay - high.astype(F32)).astype(BF16)
    tail_ref[tail_ref.shape[0] - 2 * heads :, :] = jnp.concatenate([high, low], axis=0)
    own = iota((heads, tokens), 1).astype(F32) >= start[tokens - 1 :, :1]
    weight = jnp.where(own, jnp.exp(last - level) * step, 0.0)
    weight_ref[...] = jnp.concatenate([weight, weight], axis=0).T
    level_ref[...] = jnp.concatenate([level, level], axis=0).T


def tail_part(group, weight_ref, x_ref, write_ref, tail_ref, per_group, channels):
    width = per_group * channels
    begin = pl.multiple_of(group * width, width)
    weight = to_front(weight_ref[...], group * per_group)
    weighted = []
    for tile in range(width // LANES):
        scale = spread(weight, tile * LANES // channels, channels)
        x = x_ref[:, tile * LANES : (tile + 1) * LANES].astype(F32)
        weighted.append((x * scale).astype(BF16))
    state = dot(jnp.concatenate(weighted, axis=1), write_ref[...], 0, 0)
    tail_ref[pl.ds(begin, width), :] = state.astype(BF16)


def tail_kernel(
    lengths_ref,
    raw_ref,
    rate_ref,
    x_ref,
    write_ref,
    tail_ref,
    level_ref,
    column_ref,
    start_ref,
    weight_ref,
    *,
    per_group,
    channels,
):
    group = pl.program_id(0)

    @pl.when(group == 0)
    def _():
        level_part(
            lengths_ref, raw_ref, rate_ref, level_ref, column_ref, start_ref, weight_ref, tail_ref
        )

    tail_part(group, weight_ref, x_ref, write_ref, tail_ref, per_group, channels)


def inner_kernel(
    start_ref,
    level_ref,
    column_ref,
    skip_ref,
    x_ref,
    write_ref,
    read_ref,
    out_ref,
    *,
    heads,
    per_group,
    channels,
):
    group = pl.program_id(0)
    tokens = x_ref.shape[0]
    size = read_ref.shape[1] // (heads // per_group)
    own = pl.ds(pl.multiple_of(group * size, size), size)
    both = dot(read_ref[:, own], write_ref[:, own], 1, 1)
    square = (tokens, tokens)
    source = iota(square, 1)
    wide = jnp.concatenate([start_ref[...]] * (tokens // LANES), axis=1)
    both = jnp.where((source.astype(F32) >= wide) & (source <= iota(square, 0)), both, 0.0)
    lanes = level_ref.shape[1]
    level = pltpu.roll(level_ref[...] * LOG2E, lanes - group * per_group, 1)
    column = column_ref[pl.ds(pl.multiple_of(group * per_group, per_group), per_group), :]
    begin = pl.multiple_of(group * per_group * channels, per_group * channels)
    skip = jnp.concatenate([skip_ref[...]] * 2, axis=1)
    skip = two_parts(jnp.broadcast_to(skip, (16, 2 * heads)), heads).astype(BF16)
    skip = dot(skip, expander(heads, group, per_group, channels))[:1, :]
    per_tile = LANES // channels
    lane = iota((tokens, LANES), 1)
    for tile in range(per_group // per_tile):
        at = slice(tile * LANES, (tile + 1) * LANES)
        x = x_ref[:, pl.ds(begin + at.start, LANES)].astype(F32)
        owned = []
        for part in range(per_tile):
            mine = (lane >= part * channels) & (lane < (part + 1) * channels)
            owned.append(jnp.where(mine, x, 0.0).astype(BF16))
        for block in range(tokens // LANES):
            rows = slice(block * LANES, (block + 1) * LANES)
            reach = (block + 1) * LANES
            mixing = []
            for part in range(per_tile):
                head = tile * per_tile + part
                gap = level[rows, head : head + 1] - column[head : head + 1, :reach]
                mixing.append(
                    (jnp.exp2(jnp.minimum(gap, 64.0)) * both[rows, :reach]).astype(BF16)
                )
            total = dot(
                jnp.concatenate(mixing, axis=1),
                jnp.concatenate([value[:reach, :] for value in owned], axis=0),
            )
            out_ref[rows, pl.ds(begin + at.start, LANES)] = (
                total + skip[:, at] * x[rows, :]
            ).astype(BF16)


def attend_kernel(
    start_ref,
    query_ref,
    key_ref,
    value_ref,
    prior_ref,
    *rest,
    state_rows,
    prompt_rows,
    kv_count,
):
    gathered, (out_ref, bias_ref) = rest[:-2], rest[-2:]
    head = pl.program_id(0)
    tokens = query_ref.shape[0]
    own = pl.ds(pl.multiple_of(head * HD, HD), HD)
    prompt_count = len(gathered) * gathered[0].shape[0] * prompt_rows
    queries = query_ref.shape[1] // HD // kv_count
    scale = LOG2E / math.sqrt(HD)
    reach = tokens + LANES

    @pl.when(head == 0)
    def _():
        shape = (LANES, reach)
        wide = jnp.concatenate([start_ref[...]] * (reach // LANES), axis=1)
        for block in range(tokens // LANES):
            rows = slice(block * LANES, (block + 1) * LANES)
            place = iota(shape, 1) + (block * LANES - tokens)
            allowed = (place.astype(F32) >= wide[rows, :]) & (
                place <= iota(shape, 0) + block * LANES
            )
            bias_ref[rows, :] = jnp.where(allowed, 0.0, -jnp.inf)

    def prompt(which):
        at = pl.multiple_of(state_rows + (which * kv_count + head) // 2 * 2 * prompt_rows, 16)
        at = pl.ds(at, 2 * prompt_rows)
        pair = jnp.concatenate([ref[:, at, :] for ref in gathered], axis=0).astype(F32)
        odd = lax.rem(head, 2) == 1
        part = jnp.where(odd, pair[:, prompt_rows:, :], pair[:, :prompt_rows, :])
        return part.reshape(prompt_count, HD).astype(BF16)

    prompt_keys, prompt_values = prompt(0), prompt(1)
    prior = [
        prior_ref[:, pl.ds(pl.multiple_of((which * kv_count + head) * HD, HD), HD)]
        for which in range(2)
    ]
    near_keys = jnp.concatenate([prior[0], key_ref[:, own]], axis=0)
    near_values = jnp.concatenate([prior[1], value_ref[:, own]], axis=0)
    ones = jnp.ones((prompt_count + reach, LANES), BF16)
    for block in range(tokens // LANES):
        rows = slice(block * LANES, (block + 1) * LANES)
        window = slice(block * LANES, block * LANES + reach)
        keys = jnp.concatenate([prompt_keys, near_keys[window, :]], axis=0)
        values = jnp.concatenate([prompt_values, near_values[window, :]], axis=0)
        values = jnp.concatenate([values, ones], axis=1)
        begin = pl.multiple_of(head * queries * HD, queries * HD)
        stacked = [query_ref[rows, pl.ds(begin + query * HD, HD)] for query in range(queries)]
        scores = dot(jnp.concatenate(stacked, axis=0), keys, 1, 1)
        weights = []
        for query in range(queries):
            own = scores[query * LANES : (query + 1) * LANES, :]
            far, near = own[:, :prompt_count], own[:, prompt_count:] + bias_ref[rows, :]
            own = jnp.concatenate([far, near], axis=1)
            top = jnp.max(own, axis=1, keepdims=True)
            weights.append(jnp.exp2((own - top) * scale).astype(BF16))
        summed = dot(jnp.concatenate(weights, axis=0), values)
        for query in range(queries):
            own = summed[query * LANES : (query + 1) * LANES, :]
            out_ref[rows, query * HD : (query + 1) * HD] = (own[:, :HD] / own[:, HD:]).astype(BF16)


def final_kernel(
    start_ref,
    level_ref,
    tail_ref,
    decay_ref,
    read_ref,
    inner_ref,
    gate_ref,
    gain_ref,
    *rest,
    state_rows,
    heads,
    per_group,
    channels,
):
    gathered, (out_ref, value_ref) = rest[:NEAR], rest[-2:]
    group = pl.program_id(0)
    tokens = read_ref.shape[0]
    width, state = per_group * channels, tail_ref.shape[1]

    scale = to_front(jnp.exp(level_ref[...]), group * per_group)
    carried = start_ref[:, :state] < 0
    read = read_ref[:, pl.ds(pl.multiple_of(group * state, state), state)].astype(F32)
    read = jnp.concatenate([jnp.where(carried, 0.0, read), jnp.where(carried, read, 0.0)], axis=1)
    read = read.astype(BF16)
    falls_at = pl.multiple_of(group * per_group, per_group)
    decay = decay_ref[pl.ds(falls_at, per_group), :].astype(F32)
    decay = decay + decay_ref[pl.ds(falls_at + heads, per_group), :].astype(F32)
    begin = pl.multiple_of(group * width, width)
    own = lax.rem(lax.axis_index("reader"), NEAR)
    seeds = []
    runs = width // (NEAR * state_rows)
    for run in range(runs):
        parts = [ref[group * runs + run, :state_rows, :] for ref in gathered]
        bit = 1
        while bit < NEAR:
            swap = lax.rem(own // bit, 2) == 1
            parts = [jnp.where(swap, parts[i ^ bit], parts[i]) for i in range(NEAR)]
            bit *= 2
        seeds += parts
    seeds = jnp.concatenate(seeds, axis=0)
    squares = [None] * (tokens // LANES)
    for tile in range(width // WIDE):
        at = slice(tile * WIDE, (tile + 1) * WIDE)
        tile_heads = range(at.start // channels, at.stop // channels)
        falls = [jnp.broadcast_to(decay[h : h + 1, :], (channels, state)) for h in tile_heads]
        seed = seeds[at, :]
        entering = seed.astype(F32) * jnp.concatenate(falls, axis=0)
        entering = entering + tail_ref[at, :].astype(F32)
        states = jnp.concatenate([seed, entering.astype(BF16)], axis=1)
        for block in range(tokens // LANES):
            rows = slice(block * LANES, (block + 1) * LANES)
            inflow = dot(read[rows, :], states, 1, 1)
            falls = [
                spread(scale[rows, :], (at.start + offset) // channels, channels)
                for offset in range(0, WIDE, LANES)
            ]
            inflow = inflow * jnp.concatenate(falls, axis=1)
            half = 0.5 * gate_ref[rows, pl.ds(begin + at.start, WIDE)].astype(F32)
            gated = inner_ref[rows, pl.ds(begin + at.start, WIDE)].astype(F32) + inflow
            gated = gated * (half + half * jnp.tanh(half))
            value_ref[rows, at] = gated
            square = gated * gated
            for part in range(WIDE // LANES):
                piece = square[:, part * LANES : (part + 1) * LANES]
                squares[block] = piece if squares[block] is None else squares[block] + piece
    for block in range(tokens // LANES):
        rows = slice(block * LANES, (block + 1) * LANES)
        mean = jnp.sum(squares[block], axis=1, keepdims=True) * (1.0 / width)
        norm = lax.rsqrt(mean + 1e-05)
        for tile in range(width // WIDE):
            at = slice(tile * WIDE, (tile + 1) * WIDE)
            out_ref[rows, at] = (value_ref[rows, at] * norm * gain_ref[:, at]).astype(BF16)


def shifted(value, axis, by):
    length = lax.axis_size(axis)
    return lax.ppermute(value, axis, [(i, i + by) for i in range(length - by)])


def params(limit=32):
    return pltpu.CompilerParams(vmem_limit_bytes=limit * MIB)


def whole(shape):
    return pl.BlockSpec(shape, lambda g: (0,) * len(shape))


def local(
    answer_lengths,
    mixer_input,
    gate_input,
    state_write,
    state_read,
    step_raw,
    decay_rate,
    skip_gain,
    norm_gain,
    prompt_state,
    queries,
    answer_keys,
    answer_values,
    prompt_keys,
    prompt_values,
):
    tokens, columns = mixer_input.shape
    heads = decay_rate.shape[0]
    state_rows, state = prompt_state.shape
    groups = state_write.shape[1] // state
    per_group = heads // groups
    channels = columns // heads
    width = per_group * channels
    prompt_rows, kv_width = prompt_keys.shape
    kv_count = kv_width // HD
    devices = lax.axis_size("reader")
    in_hbm = lambda value: pltpu.with_memory_space_constraint(value, pltpu.MemorySpace.HBM)
    prompt_state, prompt_keys, prompt_values = map(
        in_hbm, (prompt_state, prompt_keys, prompt_values)
    )
    lengths, rate, skip, gain = map(
        lambda value: in_hbm(value.reshape(1, -1)),
        (answer_lengths, decay_rate, skip_gain, norm_gain),
    )
    at_hand = pl.BlockSpec(memory_space=pltpu.VMEM)
    sizes = dict(heads=heads, per_group=per_group, channels=channels)
    packed_rows = state_rows + 2 * prompt_rows * kv_count

    packed = pl.pallas_call(
        pack_kernel,
        out_shape=jax.ShapeDtypeStruct((devices // NEAR, packed_rows, HD), BF16),
        out_specs=at_hand,
        compiler_params=params(),
        name="pack",
    )(prompt_state, prompt_keys, prompt_values)
    packed, near_keys = lax.optimization_barrier((packed, answer_keys))
    near = pl.pallas_call(
        join_kernel,
        out_shape=jax.ShapeDtypeStruct((tokens, 2 * kv_width), BF16),
        out_specs=at_hand,
        compiler_params=params(),
        name="join",
    )(in_hbm(near_keys), in_hbm(answer_values))
    packed, raw = lax.optimization_barrier((packed, step_raw.T))
    lines = [list(range(first, devices, NEAR)) for first in range(NEAR)]
    line = lax.all_to_all(packed, "reader", 0, 0, axis_index_groups=lines, tiled=True)
    prior = shifted(near, "reader", 1)
    raw = in_hbm(raw)

    small = pl.CostEstimate(flops=0, bytes_accessed=0, transcendentals=0)
    wide = pl.BlockSpec((tokens, width), lambda g: (0, g))
    tail, level, column, start = pl.pallas_call(
        functools.partial(tail_kernel, per_group=per_group, channels=channels),
        grid=(groups,),
        in_specs=[
            whole(lengths.shape),
            whole(raw.shape),
            whole((1, heads)),
            wide,
            pl.BlockSpec((tokens, state), lambda g: (0, g)),
        ],
        out_specs=(at_hand, at_hand, at_hand, at_hand),
        out_shape=(
            jax.ShapeDtypeStruct((columns + 2 * heads, state), BF16),
            jax.ShapeDtypeStruct((tokens, 2 * heads), F32),
            jax.ShapeDtypeStruct((heads, tokens), F32),
            jax.ShapeDtypeStruct((tokens, LANES), F32),
        ),
        scratch_shapes=[pltpu.VMEM((tokens, 2 * heads), F32)],
        compiler_params=params(),
        cost_estimate=small,
        name="tail",
    )(lengths, raw, rate, in_hbm(mixer_input), in_hbm(state_write))
    tail = shifted(tail, "reader", 1)
    inner = pl.pallas_call(
        functools.partial(inner_kernel, **sizes),
        grid=(groups,),
        in_specs=[
            at_hand,
            at_hand,
            at_hand,
            whole((1, heads)),
            at_hand,
            at_hand,
            at_hand,
        ],
        out_specs=at_hand,
        out_shape=jax.ShapeDtypeStruct((tokens, columns), BF16),
        compiler_params=params(),
        cost_estimate=small,
        name="inner",
    )(start, level, column, skip, mixer_input, state_write, state_read)
    prior, line, inner = lax.optimization_barrier((prior, line, inner))
    gathered = (line, lax.ppermute(line, "reader", [(i, i ^ 1) for i in range(devices)]))

    group_size = queries.shape[1] // kv_width
    attention_out = pl.pallas_call(
        functools.partial(
            attend_kernel,
            state_rows=state_rows,
            prompt_rows=prompt_rows,
            kv_count=kv_count,
        ),
        grid=(kv_count,),
        in_specs=[at_hand] * 5
        + [at_hand] * NEAR,
        out_specs=pl.BlockSpec((tokens, group_size * HD), lambda k: (0, k)),
        out_shape=jax.ShapeDtypeStruct(queries.shape, BF16),
        scratch_shapes=[pltpu.VMEM((tokens, tokens + LANES), F32)],
        compiler_params=params(),
        cost_estimate=small,
        name="attend",
    )(start, queries, answer_keys, answer_values, prior, *gathered)

    inner, attention_out = lax.optimization_barrier((inner, attention_out))
    mixer_out = pl.pallas_call(
        functools.partial(final_kernel, state_rows=state_rows, **sizes),
        grid=(groups,),
        in_specs=[
            at_hand,
            at_hand,
            pl.BlockSpec((width, state), lambda g: (g, 0)),
            pl.BlockSpec((2 * heads, state), lambda g: (columns // (2 * heads), 0)),
            at_hand,
            at_hand,
            at_hand,
            pl.BlockSpec((1, width), lambda g: (0, g)),
        ]
        + [at_hand] * NEAR,
        out_specs=wide,
        out_shape=jax.ShapeDtypeStruct((tokens, columns), BF16),
        scratch_shapes=[pltpu.VMEM((tokens, width), F32)],
        compiler_params=params(),
        cost_estimate=small,
        name="final",
    )(start, level, tail, tail, state_read, inner, gate_input, gain, *gathered)
    return (mixer_out, attention_out)


def solution(mesh):
    rows = P(("group", "reader"), None)
    in_specs = (P("group"),) + (rows,) * 5 + (P(),) * 3 + (rows,) * 6
    return jax.shard_map(
        local, mesh=mesh, in_specs=in_specs, out_specs=(rows, rows), check_vma=False
    )
```

```python
import functools
import math

import jax
import jax.numpy as jnp
from jax import lax
from jax.experimental import pallas as pl
from jax.experimental.pallas import tpu as pltpu
from jax.sharding import PartitionSpec as P

HD = 128
LANES = 128
WIDE = 256
NEAR = 2
LOG2E = 1.4426950408889634
F32 = jnp.float32
BF16 = jnp.bfloat16
MIB = 1 << 20


def iota(shape, dim):
    return lax.broadcasted_iota(jnp.int32, shape, dim)


def dot(a, b, ca=1, cb=0):
    return lax.dot_general(a, b, (((ca,), (cb,)), ((), ())), preferred_element_type=F32)


def expander(heads, group, per_group, channels):
    shape = (2 * heads, per_group * channels)
    row = iota(shape, 0)
    head = jnp.where(row >= heads, row - heads, row) - group * per_group
    column = iota(shape, 1)
    first = head * channels
    return jnp.where((column >= first) & (column < first + channels), 1.0, 0.0).astype(BF16)


def two_parts(value, heads):
    high = value.astype(BF16).astype(F32)
    return jnp.where(iota(value.shape, 1) < heads, high, value - high)


def to_front(value, head):
    return pltpu.roll(value, value.shape[1] - head, 1)


def spread(value, first, channels):
    lane = iota((8, LANES), 1)
    source = jnp.full((8, LANES), first, jnp.int32)
    for part in range(1, LANES // channels):
        source = source + jnp.where(lane >= part * channels, 1, 0)
    source = jnp.concatenate([source] * (value.shape[0] // 8), axis=0)
    return jnp.take_along_axis(value, source, axis=1, mode="promise_in_bounds")


def join_kernel(keys_ref, values_ref, out_ref):
    width = keys_ref.shape[1]
    out_ref[:, :width] = keys_ref[...]
    out_ref[:, width:] = values_ref[...]


def pack_kernel(state_ref, keys_ref, values_ref, out_ref):
    rows = state_ref.shape[0]
    state = state_ref[...].astype(BF16)
    parts = []
    for ref in (keys_ref, values_ref):
        wide = ref[...].astype(F32)
        for head in range(wide.shape[1] // HD):
            parts.append(wide[:, head * HD : (head + 1) * HD])
    parts = jnp.concatenate(parts, axis=0).astype(BF16)
    for copy in range(out_ref.shape[0]):
        out_ref[copy, :rows, :] = state
        out_ref[copy, rows:, :] = parts


def level_part(lengths_ref, raw_ref, rate_ref, level_ref, column_ref, start_ref, weight_ref, tail_ref):
    heads, tokens = raw_ref.shape
    base = (lax.axis_index("reader") * tokens).astype(F32)
    lengths = lengths_ref[...].astype(F32)
    answers = lengths.shape[1]
    square = (answers, answers)
    ends = jnp.sum(
        jnp.where(iota(square, 1) <= iota(square, 0), lengths, 0.0), axis=1, keepdims=True
    )
    place = base + iota((1, tokens), 1).astype(F32)
    start = jnp.max(jnp.where(ends <= place, ends, 0.0), axis=0, keepdims=True) - base
    start = jnp.broadcast_to(start, (LANES, tokens)).T
    start_ref[...] = start
    wide = jnp.concatenate([start] * (tokens // LANES), axis=1)
    square = (tokens, tokens)
    source = iota(square, 1)
    mask = (source.astype(F32) >= wide) & (source <= iota(square, 0))
    mask = jnp.where(mask, 1.0, 0.0).astype(BF16)
    raw = raw_ref[...]
    rate = jnp.broadcast_to(rate_ref[...], (heads, heads))
    diagonal = iota((heads, heads), 0) == iota((heads, heads), 1)
    rate = jnp.sum(jnp.where(diagonal, rate, 0.0), axis=1, keepdims=True)
    step = jnp.maximum(raw, 0.0) + jnp.log1p(jnp.exp(-jnp.abs(raw)))
    falling = -rate * step
    first = falling.astype(BF16)
    rest = falling - first.astype(F32)
    second = rest.astype(BF16)
    third = (rest - second.astype(F32)).astype(BF16)
    level = dot(first, mask, 1, 1) + (dot(second, mask, 1, 1) + dot(third, mask, 1, 1))
    column_ref[...] = level * LOG2E - jnp.log(step) * LOG2E
    last = level[:, tokens - 1 :]
    decay = jnp.exp(jnp.broadcast_to(last, (heads, tail_ref.shape[1])))
    high = decay.astype(BF16)
    low = (decay - high.astype(F32)).astype(BF16)
    tail_ref[tail_ref.shape[0] - 2 * heads :, :] = jnp.concatenate([high, low], axis=0)
    own = iota((heads, tokens), 1).astype(F32) >= start[tokens - 1 :, :1]
    weight = jnp.where(own, jnp.exp(last - level) * step, 0.0)
    weight_ref[...] = jnp.concatenate([weight, weight], axis=0).T
    level_ref[...] = jnp.concatenate([level, level], axis=0).T


def tail_part(group, weight_ref, x_ref, write_ref, tail_ref, per_group, channels):
    width = per_group * channels
    begin = pl.multiple_of(group * width, width)
    weight = to_front(weight_ref[...], group * per_group)
    weighted = []
    for tile in range(width // LANES):
        scale = spread(weight, tile * LANES // channels, channels)
        x = x_ref[:, tile * LANES : (tile + 1) * LANES].astype(F32)
        weighted.append((x * scale).astype(BF16))
    state = dot(jnp.concatenate(weighted, axis=1), write_ref[...], 0, 0)
    tail_ref[pl.ds(begin, width), :] = state.astype(BF16)


def tail_kernel(
    lengths_ref,
    raw_ref,
    rate_ref,
    x_ref,
    write_ref,
    tail_ref,
    level_ref,
    column_ref,
    start_ref,
    weight_ref,
    *,
    per_group,
    channels,
):
    group = pl.program_id(0)

    @pl.when(group == 0)
    def _():
        level_part(
            lengths_ref, raw_ref, rate_ref, level_ref, column_ref, start_ref, weight_ref, tail_ref
        )

    tail_part(group, weight_ref, x_ref, write_ref, tail_ref, per_group, channels)


def inner_kernel(
    start_ref,
    level_ref,
    column_ref,
    skip_ref,
    x_ref,
    write_ref,
    read_ref,
    out_ref,
    *,
    heads,
    per_group,
    channels,
):
    group = pl.program_id(0)
    tokens = x_ref.shape[0]
    size = read_ref.shape[1] // (heads // per_group)
    own = pl.ds(pl.multiple_of(group * size, size), size)
    both = dot(read_ref[:, own], write_ref[:, own], 1, 1)
    square = (tokens, tokens)
    source = iota(square, 1)
    wide = jnp.concatenate([start_ref[...]] * (tokens // LANES), axis=1)
    both = jnp.where((source.astype(F32) >= wide) & (source <= iota(square, 0)), both, 0.0)
    lanes = level_ref.shape[1]
    level = pltpu.roll(level_ref[...] * LOG2E, lanes - group * per_group, 1)
    column = column_ref[pl.ds(pl.multiple_of(group * per_group, per_group), per_group), :]
    begin = pl.multiple_of(group * per_group * channels, per_group * channels)
    skip = jnp.concatenate([skip_ref[...]] * 2, axis=1)
    skip = two_parts(jnp.broadcast_to(skip, (16, 2 * heads)), heads).astype(BF16)
    skip = dot(skip, expander(heads, group, per_group, channels))[:1, :]
    per_tile = LANES // channels
    lane = iota((tokens, LANES), 1)
    for tile in range(per_group // per_tile):
        at = slice(tile * LANES, (tile + 1) * LANES)
        x = x_ref[:, pl.ds(begin + at.start, LANES)].astype(F32)
        owned = []
        for part in range(per_tile):
            mine = (lane >= part * channels) & (lane < (part + 1) * channels)
            owned.append(jnp.where(mine, x, 0.0).astype(BF16))
        for block in range(tokens // LANES):
            rows = slice(block * LANES, (block + 1) * LANES)
            reach = (block + 1) * LANES
            mixing = []
            for part in range(per_tile):
                head = tile * per_tile + part
                gap = level[rows, head : head + 1] - column[head : head + 1, :reach]
                mixing.append(
                    (jnp.exp2(jnp.minimum(gap, 64.0)) * both[rows, :reach]).astype(BF16)
                )
            total = dot(
                jnp.concatenate(mixing, axis=1),
                jnp.concatenate([value[:reach, :] for value in owned], axis=0),
            )
            out_ref[rows, pl.ds(begin + at.start, LANES)] = (
                total + skip[:, at] * x[rows, :]
            ).astype(BF16)


def attend_kernel(
    start_ref,
    query_ref,
    key_ref,
    value_ref,
    prior_ref,
    *rest,
    state_rows,
    prompt_rows,
    kv_count,
):
    gathered, (out_ref, bias_ref) = rest[:-2], rest[-2:]
    head = pl.program_id(0)
    tokens = query_ref.shape[0]
    own = pl.ds(pl.multiple_of(head * HD, HD), HD)
    prompt_count = len(gathered) * gathered[0].shape[0] * prompt_rows
    queries = query_ref.shape[1] // HD // kv_count
    scale = LOG2E / math.sqrt(HD)
    reach = tokens + LANES

    @pl.when(head == 0)
    def _():
        shape = (LANES, reach)
        wide = jnp.concatenate([start_ref[...]] * (reach // LANES), axis=1)
        for block in range(tokens // LANES):
            rows = slice(block * LANES, (block + 1) * LANES)
            place = iota(shape, 1) + (block * LANES - tokens)
            allowed = (place.astype(F32) >= wide[rows, :]) & (
                place <= iota(shape, 0) + block * LANES
            )
            bias_ref[rows, :] = jnp.where(allowed, 0.0, -jnp.inf)

    def prompt(which):
        at = pl.multiple_of(state_rows + (which * kv_count + head) // 2 * 2 * prompt_rows, 16)
        at = pl.ds(at, 2 * prompt_rows)
        pair = jnp.concatenate([ref[:, at, :] for ref in gathered], axis=0).astype(F32)
        odd = lax.rem(head, 2) == 1
        part = jnp.where(odd, pair[:, prompt_rows:, :], pair[:, :prompt_rows, :])
        return part.reshape(prompt_count, HD).astype(BF16)

    prompt_keys, prompt_values = prompt(0), prompt(1)
    prior = [
        prior_ref[:, pl.ds(pl.multiple_of((which * kv_count + head) * HD, HD), HD)]
        for which in range(2)
    ]
    near_keys = jnp.concatenate([prior[0], key_ref[:, own]], axis=0)
    near_values = jnp.concatenate([prior[1], value_ref[:, own]], axis=0)
    ones = jnp.ones((prompt_count + reach, LANES), BF16)
    for block in range(tokens // LANES):
        rows = slice(block * LANES, (block + 1) * LANES)
        window = slice(block * LANES, block * LANES + reach)
        keys = jnp.concatenate([prompt_keys, near_keys[window, :]], axis=0)
        values = jnp.concatenate([prompt_values, near_values[window, :]], axis=0)
        values = jnp.concatenate([values, ones], axis=1)
        begin = pl.multiple_of(head * queries * HD, queries * HD)
        stacked = [query_ref[rows, pl.ds(begin + query * HD, HD)] for query in range(queries)]
        scores = dot(jnp.concatenate(stacked, axis=0), keys, 1, 1)
        weights = []
        for query in range(queries):
            own = scores[query * LANES : (query + 1) * LANES, :]
            far, near = own[:, :prompt_count], own[:, prompt_count:] + bias_ref[rows, :]
            own = jnp.concatenate([far, near], axis=1)
            top = jnp.max(own, axis=1, keepdims=True)
            weights.append(jnp.exp2((own - top) * scale).astype(BF16))
        summed = dot(jnp.concatenate(weights, axis=0), values)
        for query in range(queries):
            own = summed[query * LANES : (query + 1) * LANES, :]
            out_ref[rows, query * HD : (query + 1) * HD] = (own[:, :HD] / own[:, HD:]).astype(BF16)


def final_kernel(
    start_ref,
    level_ref,
    tail_ref,
    decay_ref,
    read_ref,
    inner_ref,
    gate_ref,
    gain_ref,
    *rest,
    state_rows,
    heads,
    per_group,
    channels,
):
    gathered, (out_ref, value_ref) = rest[:NEAR], rest[-2:]
    group = pl.program_id(0)
    tokens = read_ref.shape[0]
    width, state = per_group * channels, tail_ref.shape[1]

    scale = to_front(jnp.exp(level_ref[...]), group * per_group)
    carried = start_ref[:, :state] < 0
    read = read_ref[:, pl.ds(pl.multiple_of(group * state, state), state)].astype(F32)
    fresh = jnp.where(carried, 0.0, read).astype(BF16)
    kept = jnp.where(carried, read, 0.0).astype(BF16)
    read = jnp.concatenate([fresh, kept, kept], axis=1)
    falls_at = pl.multiple_of(group * per_group, per_group)
    decay = decay_ref[pl.ds(falls_at, per_group), :].astype(F32)
    decay = decay + decay_ref[pl.ds(falls_at + heads, per_group), :].astype(F32)
    begin = pl.multiple_of(group * width, width)
    runs = width // (NEAR * state_rows)

    def finish(in_order):
        seeds = [
            ref[group * runs + run, :state_rows, :] for run in range(runs) for ref in in_order
        ]
        seeds = jnp.concatenate(seeds, axis=0)
        squares = [None] * (tokens // LANES)
        for tile in range(width // WIDE):
            at = slice(tile * WIDE, (tile + 1) * WIDE)
            tile_heads = range(at.start // channels, at.stop // channels)
            falls = [jnp.broadcast_to(decay[h : h + 1, :], (channels, state)) for h in tile_heads]
            seed = seeds[at, :]
            faded = (seed.astype(F32) * jnp.concatenate(falls, axis=0)).astype(BF16)
            states = jnp.concatenate([seed, faded, tail_ref[at, :]], axis=1)
            for block in range(tokens // LANES):
                rows = slice(block * LANES, (block + 1) * LANES)
                inflow = dot(read[rows, :], states, 1, 1)
                falls = [
                    spread(scale[rows, :], (at.start + offset) // channels, channels)
                    for offset in range(0, WIDE, LANES)
                ]
                inflow = inflow * jnp.concatenate(falls, axis=1)
                own = pl.ds(begin + at.start, WIDE)
                half = 0.5 * gate_ref[rows, own].astype(F32)
                gated = inner_ref[rows, own].astype(F32) + inflow
                gated = gated * (half + half * jnp.tanh(half))
                value_ref[rows, at] = gated
                square = gated * gated
                for part in range(WIDE // LANES):
                    piece = square[:, part * LANES : (part + 1) * LANES]
                    squares[block] = piece if squares[block] is None else squares[block] + piece
        for block in range(tokens // LANES):
            rows = slice(block * LANES, (block + 1) * LANES)
            mean = jnp.sum(squares[block], axis=1, keepdims=True) * (1.0 / width)
            norm = lax.rsqrt(mean + 1e-05)
            for tile in range(width // WIDE):
                at = slice(tile * WIDE, (tile + 1) * WIDE)
                out_ref[rows, at] = (value_ref[rows, at] * norm * gain_ref[:, at]).astype(BF16)

    place = lax.rem(lax.axis_index("reader"), NEAR)

    @pl.when(place == 0)
    def _():
        finish(gathered)

    @pl.when(place == 1)
    def _():
        finish(gathered[::-1])


def shifted(value, axis, by):
    length = lax.axis_size(axis)
    return lax.ppermute(value, axis, [(i, i + by) for i in range(length - by)])


def params(limit=32):
    return pltpu.CompilerParams(vmem_limit_bytes=limit * MIB)


def whole(shape):
    return pl.BlockSpec(shape, lambda g: (0,) * len(shape))


def local(
    answer_lengths,
    mixer_input,
    gate_input,
    state_write,
    state_read,
    step_raw,
    decay_rate,
    skip_gain,
    norm_gain,
    prompt_state,
    queries,
    answer_keys,
    answer_values,
    prompt_keys,
    prompt_values,
):
    tokens, columns = mixer_input.shape
    heads = decay_rate.shape[0]
    state_rows, state = prompt_state.shape
    groups = state_write.shape[1] // state
    per_group = heads // groups
    channels = columns // heads
    width = per_group * channels
    prompt_rows, kv_width = prompt_keys.shape
    kv_count = kv_width // HD
    devices = lax.axis_size("reader")
    in_hbm = lambda value: pltpu.with_memory_space_constraint(value, pltpu.MemorySpace.HBM)
    prompt_state, prompt_keys, prompt_values = map(
        in_hbm, (prompt_state, prompt_keys, prompt_values)
    )
    lengths, rate, skip, gain = map(
        lambda value: in_hbm(value.reshape(1, -1)),
        (answer_lengths, decay_rate, skip_gain, norm_gain),
    )
    at_hand = pl.BlockSpec(memory_space=pltpu.VMEM)
    sizes = dict(heads=heads, per_group=per_group, channels=channels)
    packed_rows = state_rows + 2 * prompt_rows * kv_count

    packed = pl.pallas_call(
        pack_kernel,
        out_shape=jax.ShapeDtypeStruct((devices // NEAR, packed_rows, HD), BF16),
        out_specs=at_hand,
        compiler_params=params(),
        name="pack",
    )(prompt_state, prompt_keys, prompt_values)
    packed, near_keys = lax.optimization_barrier((packed, answer_keys))
    near = pl.pallas_call(
        join_kernel,
        out_shape=jax.ShapeDtypeStruct((tokens, 2 * kv_width), BF16),
        out_specs=at_hand,
        compiler_params=params(),
        name="join",
    )(in_hbm(near_keys), in_hbm(answer_values))
    packed, raw = lax.optimization_barrier((packed, step_raw.T))
    lines = [list(range(first, devices, NEAR)) for first in range(NEAR)]
    line = lax.all_to_all(packed, "reader", 0, 0, axis_index_groups=lines, tiled=True)
    prior = shifted(near, "reader", 1)
    raw = in_hbm(raw)

    small = pl.CostEstimate(flops=0, bytes_accessed=0, transcendentals=0)
    wide = pl.BlockSpec((tokens, width), lambda g: (0, g))
    tail, level, column, start = pl.pallas_call(
        functools.partial(tail_kernel, per_group=per_group, channels=channels),
        grid=(groups,),
        in_specs=[
            whole(lengths.shape),
            whole(raw.shape),
            whole((1, heads)),
            wide,
            pl.BlockSpec((tokens, state), lambda g: (0, g)),
        ],
        out_specs=(at_hand, at_hand, at_hand, at_hand),
        out_shape=(
            jax.ShapeDtypeStruct((columns + 2 * heads, state), BF16),
            jax.ShapeDtypeStruct((tokens, 2 * heads), F32),
            jax.ShapeDtypeStruct((heads, tokens), F32),
            jax.ShapeDtypeStruct((tokens, LANES), F32),
        ),
        scratch_shapes=[pltpu.VMEM((tokens, 2 * heads), F32)],
        compiler_params=params(),
        cost_estimate=small,
        name="tail",
    )(lengths, raw, rate, in_hbm(mixer_input), in_hbm(state_write))
    tail = shifted(tail, "reader", 1)
    inner = pl.pallas_call(
        functools.partial(inner_kernel, **sizes),
        grid=(groups,),
        in_specs=[
            at_hand,
            at_hand,
            at_hand,
            whole((1, heads)),
            at_hand,
            at_hand,
            at_hand,
        ],
        out_specs=at_hand,
        out_shape=jax.ShapeDtypeStruct((tokens, columns), BF16),
        compiler_params=params(),
        cost_estimate=small,
        name="inner",
    )(start, level, column, skip, mixer_input, state_write, state_read)
    prior, line, inner = lax.optimization_barrier((prior, line, inner))
    gathered = (line, lax.ppermute(line, "reader", [(i, i ^ 1) for i in range(devices)]))

    group_size = queries.shape[1] // kv_width
    attention_out = pl.pallas_call(
        functools.partial(
            attend_kernel,
            state_rows=state_rows,
            prompt_rows=prompt_rows,
            kv_count=kv_count,
        ),
        grid=(kv_count,),
        in_specs=[at_hand] * 5
        + [at_hand] * NEAR,
        out_specs=pl.BlockSpec((tokens, group_size * HD), lambda k: (0, k)),
        out_shape=jax.ShapeDtypeStruct(queries.shape, BF16),
        scratch_shapes=[pltpu.VMEM((tokens, tokens + LANES), F32)],
        compiler_params=params(),
        cost_estimate=small,
        name="attend",
    )(start, queries, answer_keys, answer_values, prior, *gathered)

    inner, attention_out = lax.optimization_barrier((inner, attention_out))
    mixer_out = pl.pallas_call(
        functools.partial(final_kernel, state_rows=state_rows, **sizes),
        grid=(groups,),
        in_specs=[
            at_hand,
            at_hand,
            pl.BlockSpec((width, state), lambda g: (g, 0)),
            pl.BlockSpec((2 * heads, state), lambda g: (columns // (2 * heads), 0)),
            at_hand,
            at_hand,
            at_hand,
            pl.BlockSpec((1, width), lambda g: (0, g)),
        ]
        + [at_hand] * NEAR,
        out_specs=wide,
        out_shape=jax.ShapeDtypeStruct((tokens, columns), BF16),
        scratch_shapes=[pltpu.VMEM((tokens, width), F32)],
        compiler_params=params(),
        cost_estimate=small,
        name="final",
    )(start, level, tail, tail, state_read, inner, gate_input, gain, *gathered)
    return (mixer_out, attention_out)


def solution(mesh):
    rows = P(("group", "reader"), None)
    in_specs = (P("group"),) + (rows,) * 5 + (P(),) * 3 + (rows,) * 6
    return jax.shard_map(
        local, mesh=mesh, in_specs=in_specs, out_specs=(rows, rows), check_vma=False
    )
```

```python
import functools
import math

import jax
import jax.numpy as jnp
from jax import lax
from jax.experimental import pallas as pl
from jax.experimental.pallas import tpu as pltpu
from jax.sharding import PartitionSpec as P

HD = 128
LANES = 128
WIDE = 256
NEAR = 2
LOG2E = 1.4426950408889634
F32 = jnp.float32
BF16 = jnp.bfloat16
MIB = 1 << 20


def iota(shape, dim):
    return lax.broadcasted_iota(jnp.int32, shape, dim)


def dot(a, b, ca=1, cb=0):
    return lax.dot_general(a, b, (((ca,), (cb,)), ((), ())), preferred_element_type=F32)


def expander(heads, group, per_group, channels):
    shape = (2 * heads, per_group * channels)
    row = iota(shape, 0)
    head = jnp.where(row >= heads, row - heads, row) - group * per_group
    column = iota(shape, 1)
    first = head * channels
    return jnp.where((column >= first) & (column < first + channels), 1.0, 0.0).astype(BF16)


def two_parts(value, heads):
    high = value.astype(BF16).astype(F32)
    return jnp.where(iota(value.shape, 1) < heads, high, value - high)


def to_front(value, head):
    return pltpu.roll(value, value.shape[1] - head, 1)


def spread(value, first, channels):
    lane = iota((8, LANES), 1)
    source = jnp.full((8, LANES), first, jnp.int32)
    for part in range(1, LANES // channels):
        source = source + jnp.where(lane >= part * channels, 1, 0)
    source = jnp.concatenate([source] * (value.shape[0] // 8), axis=0)
    return jnp.take_along_axis(value, source, axis=1, mode="promise_in_bounds")


def join_kernel(keys_ref, values_ref, out_ref):
    width = keys_ref.shape[1]
    out_ref[:, :width] = keys_ref[...]
    out_ref[:, width:] = values_ref[...]


def pack_kernel(state_ref, keys_ref, values_ref, out_ref):
    rows = state_ref.shape[0]
    state = state_ref[...].astype(BF16)
    parts = []
    for ref in (keys_ref, values_ref):
        wide = ref[...].astype(F32)
        for head in range(wide.shape[1] // HD):
            parts.append(wide[:, head * HD : (head + 1) * HD])
    parts = jnp.concatenate(parts, axis=0).astype(BF16)
    for copy in range(out_ref.shape[0]):
        out_ref[copy, :rows, :] = state
        out_ref[copy, rows:, :] = parts


def level_part(lengths_ref, raw_ref, rate_ref, level_ref, column_ref, start_ref, weight_ref, tail_ref):
    heads, tokens = raw_ref.shape
    base = (lax.axis_index("reader") * tokens).astype(F32)
    lengths = lengths_ref[...].astype(F32)
    answers = lengths.shape[1]
    square = (answers, answers)
    ends = jnp.sum(
        jnp.where(iota(square, 1) <= iota(square, 0), lengths, 0.0), axis=1, keepdims=True
    )
    place = base + iota((1, tokens), 1).astype(F32)
    start = jnp.max(jnp.where(ends <= place, ends, 0.0), axis=0, keepdims=True) - base
    start = jnp.broadcast_to(start, (LANES, tokens)).T
    start_ref[...] = start
    wide = jnp.concatenate([start] * (tokens // LANES), axis=1)
    square = (tokens, tokens)
    source = iota(square, 1)
    mask = (source.astype(F32) >= wide) & (source <= iota(square, 0))
    mask = jnp.where(mask, 1.0, 0.0).astype(BF16)
    raw = raw_ref[...]
    rate = jnp.broadcast_to(rate_ref[...], (heads, heads))
    diagonal = iota((heads, heads), 0) == iota((heads, heads), 1)
    rate = jnp.sum(jnp.where(diagonal, rate, 0.0), axis=1, keepdims=True)
    step = jnp.maximum(raw, 0.0) + jnp.log1p(jnp.exp(-jnp.abs(raw)))
    falling = -rate * step
    first = falling.astype(BF16)
    rest = falling - first.astype(F32)
    second = rest.astype(BF16)
    third = (rest - second.astype(F32)).astype(BF16)
    level = dot(first, mask, 1, 1) + (dot(second, mask, 1, 1) + dot(third, mask, 1, 1))
    column_ref[...] = level * LOG2E - jnp.log(step) * LOG2E
    last = level[:, tokens - 1 :]
    decay = jnp.exp(jnp.broadcast_to(last, (heads, tail_ref.shape[1])))
    high = decay.astype(BF16)
    low = (decay - high.astype(F32)).astype(BF16)
    tail_ref[tail_ref.shape[0] - 2 * heads :, :] = jnp.concatenate([high, low], axis=0)
    own = iota((heads, tokens), 1).astype(F32) >= start[tokens - 1 :, :1]
    weight = jnp.where(own, jnp.exp(last - level) * step, 0.0)
    weight_ref[...] = jnp.concatenate([weight, weight], axis=0).T
    level_ref[...] = jnp.concatenate([level, level], axis=0).T


def tail_part(group, weight_ref, x_ref, write_ref, tail_ref, per_group, channels):
    width = per_group * channels
    begin = pl.multiple_of(group * width, width)
    weight = to_front(weight_ref[...], group * per_group)
    weighted = []
    for tile in range(width // LANES):
        scale = spread(weight, tile * LANES // channels, channels)
        x = x_ref[:, tile * LANES : (tile + 1) * LANES].astype(F32)
        weighted.append((x * scale).astype(BF16))
    state = dot(jnp.concatenate(weighted, axis=1), write_ref[...], 0, 0)
    tail_ref[pl.ds(begin, width), :] = state.astype(BF16)


def tail_kernel(
    lengths_ref,
    raw_ref,
    rate_ref,
    x_ref,
    write_ref,
    tail_ref,
    level_ref,
    column_ref,
    start_ref,
    weight_ref,
    *,
    per_group,
    channels,
):
    group = pl.program_id(0)

    @pl.when(group == 0)
    def _():
        level_part(
            lengths_ref, raw_ref, rate_ref, level_ref, column_ref, start_ref, weight_ref, tail_ref
        )

    tail_part(group, weight_ref, x_ref, write_ref, tail_ref, per_group, channels)


def inner_kernel(
    start_ref,
    level_ref,
    column_ref,
    skip_ref,
    x_ref,
    write_ref,
    read_ref,
    out_ref,
    *,
    heads,
    per_group,
    channels,
):
    group = pl.program_id(0)
    tokens = x_ref.shape[0]
    size = read_ref.shape[1] // (heads // per_group)
    own = pl.ds(pl.multiple_of(group * size, size), size)
    both = dot(read_ref[:, own], write_ref[:, own], 1, 1)
    square = (tokens, tokens)
    source = iota(square, 1)
    wide = jnp.concatenate([start_ref[...]] * (tokens // LANES), axis=1)
    both = jnp.where((source.astype(F32) >= wide) & (source <= iota(square, 0)), both, 0.0)
    lanes = level_ref.shape[1]
    level = pltpu.roll(level_ref[...] * LOG2E, lanes - group * per_group, 1)
    column = column_ref[pl.ds(pl.multiple_of(group * per_group, per_group), per_group), :]
    begin = pl.multiple_of(group * per_group * channels, per_group * channels)
    skip = jnp.concatenate([skip_ref[...]] * 2, axis=1)
    skip = two_parts(jnp.broadcast_to(skip, (16, 2 * heads)), heads).astype(BF16)
    skip = dot(skip, expander(heads, group, per_group, channels))[:1, :]
    per_tile = LANES // channels
    lane = iota((tokens, LANES), 1)
    for tile in range(per_group // per_tile):
        at = slice(tile * LANES, (tile + 1) * LANES)
        x = x_ref[:, pl.ds(begin + at.start, LANES)].astype(F32)
        owned = []
        for part in range(per_tile):
            mine = (lane >= part * channels) & (lane < (part + 1) * channels)
            owned.append(jnp.where(mine, x, 0.0).astype(BF16))
        for block in range(tokens // LANES):
            rows = slice(block * LANES, (block + 1) * LANES)
            reach = (block + 1) * LANES
            mixing = []
            for part in range(per_tile):
                head = tile * per_tile + part
                gap = level[rows, head : head + 1] - column[head : head + 1, :reach]
                mixing.append(
                    (jnp.exp2(jnp.minimum(gap, 64.0)) * both[rows, :reach]).astype(BF16)
                )
            total = dot(
                jnp.concatenate(mixing, axis=1),
                jnp.concatenate([value[:reach, :] for value in owned], axis=0),
            )
            out_ref[rows, pl.ds(begin + at.start, LANES)] = (
                total + skip[:, at] * x[rows, :]
            ).astype(BF16)


def attend_kernel(
    start_ref,
    query_ref,
    key_ref,
    value_ref,
    prior_ref,
    *rest,
    state_rows,
    prompt_rows,
    kv_count,
):
    gathered, (out_ref, bias_ref) = rest[:-2], rest[-2:]
    head = pl.program_id(0)
    tokens = query_ref.shape[0]
    own = pl.ds(pl.multiple_of(head * HD, HD), HD)
    prompt_count = len(gathered) * gathered[0].shape[0] * prompt_rows
    queries = query_ref.shape[1] // HD // kv_count
    scale = LOG2E / math.sqrt(HD)
    reach = tokens + LANES

    @pl.when(head == 0)
    def _():
        shape = (LANES, reach)
        wide = jnp.concatenate([start_ref[...]] * (reach // LANES), axis=1)
        for block in range(tokens // LANES):
            rows = slice(block * LANES, (block + 1) * LANES)
            place = iota(shape, 1) + (block * LANES - tokens)
            allowed = (place.astype(F32) >= wide[rows, :]) & (
                place <= iota(shape, 0) + block * LANES
            )
            bias_ref[rows, :] = jnp.where(allowed, 0.0, -jnp.inf)

    def prompt(which):
        at = pl.multiple_of(state_rows + (which * kv_count + head) // 2 * 2 * prompt_rows, 16)
        at = pl.ds(at, 2 * prompt_rows)
        pair = jnp.concatenate([ref[:, at, :] for ref in gathered], axis=0).astype(F32)
        odd = lax.rem(head, 2) == 1
        part = jnp.where(odd, pair[:, prompt_rows:, :], pair[:, :prompt_rows, :])
        return part.reshape(prompt_count, HD).astype(BF16)

    prompt_keys, prompt_values = prompt(0), prompt(1)
    prior = [
        prior_ref[:, pl.ds(pl.multiple_of((which * kv_count + head) * HD, HD), HD)]
        for which in range(2)
    ]
    near_keys = jnp.concatenate([prior[0], key_ref[:, own]], axis=0)
    near_values = jnp.concatenate([prior[1], value_ref[:, own]], axis=0)
    ones = jnp.ones((prompt_count + reach, LANES), BF16)
    for block in range(tokens // LANES):
        rows = slice(block * LANES, (block + 1) * LANES)
        window = slice(block * LANES, block * LANES + reach)
        keys = jnp.concatenate([prompt_keys, near_keys[window, :]], axis=0)
        values = jnp.concatenate([prompt_values, near_values[window, :]], axis=0)
        values = jnp.concatenate([values, ones], axis=1)
        begin = pl.multiple_of(head * queries * HD, queries * HD)
        stacked = [query_ref[rows, pl.ds(begin + query * HD, HD)] for query in range(queries)]
        scores = dot(jnp.concatenate(stacked, axis=0), keys, 1, 1)
        weights = []
        for query in range(queries):
            own = scores[query * LANES : (query + 1) * LANES, :]
            far, near = own[:, :prompt_count], own[:, prompt_count:] + bias_ref[rows, :]
            own = jnp.concatenate([far, near], axis=1)
            top = jnp.max(own, axis=1, keepdims=True)
            weights.append(jnp.exp2((own - top) * scale).astype(BF16))
        summed = dot(jnp.concatenate(weights, axis=0), values)
        for query in range(queries):
            own = summed[query * LANES : (query + 1) * LANES, :]
            out_ref[rows, query * HD : (query + 1) * HD] = (own[:, :HD] / own[:, HD:]).astype(BF16)


def final_kernel(
    start_ref,
    level_ref,
    tail_ref,
    decay_ref,
    read_ref,
    inner_ref,
    gate_ref,
    gain_ref,
    *rest,
    state_rows,
    heads,
    per_group,
    channels,
):
    gathered, (out_ref, value_ref) = rest[:NEAR], rest[-2:]
    group = pl.program_id(0)
    tokens = read_ref.shape[0]
    width, state = per_group * channels, tail_ref.shape[1]

    scale = to_front(jnp.exp(level_ref[...]), group * per_group)
    carried = start_ref[:, :state] < 0
    read = read_ref[:, pl.ds(pl.multiple_of(group * state, state), state)].astype(F32)
    fresh = jnp.where(carried, 0.0, read).astype(BF16)
    kept = jnp.where(carried, read, 0.0).astype(BF16)
    read = jnp.concatenate([fresh, kept, kept], axis=1)
    falls_at = pl.multiple_of(group * per_group, per_group)
    decay = decay_ref[pl.ds(falls_at, per_group), :].astype(F32)
    decay = decay + decay_ref[pl.ds(falls_at + heads, per_group), :].astype(F32)
    begin = pl.multiple_of(group * width, width)
    runs = width // (NEAR * state_rows)

    def finish(in_order):
        seeds = [
            ref[group * runs + run, :state_rows, :] for run in range(runs) for ref in in_order
        ]
        seeds = jnp.concatenate(seeds, axis=0)
        squares = [None] * (tokens // LANES)
        for tile in range(width // WIDE):
            at = slice(tile * WIDE, (tile + 1) * WIDE)
            tile_heads = range(at.start // channels, at.stop // channels)
            falls = [jnp.broadcast_to(decay[h : h + 1, :], (channels, state)) for h in tile_heads]
            seed = seeds[at, :]
            faded = (seed.astype(F32) * jnp.concatenate(falls, axis=0)).astype(BF16)
            states = jnp.concatenate([seed, faded, tail_ref[at, :]], axis=1)
            inflows = dot(read, states, 1, 1)
            for block in range(tokens // LANES):
                rows = slice(block * LANES, (block + 1) * LANES)
                falls = [
                    spread(scale[rows, :], (at.start + offset) // channels, channels)
                    for offset in range(0, WIDE, LANES)
                ]
                inflow = inflows[rows, :] * jnp.concatenate(falls, axis=1)
                own = pl.ds(begin + at.start, WIDE)
                half = 0.5 * gate_ref[rows, own].astype(F32)
                gated = inner_ref[rows, own].astype(F32) + inflow
                gated = gated * (half + half * jnp.tanh(half))
                value_ref[rows, at] = gated
                square = gated * gated
                for part in range(WIDE // LANES):
                    piece = square[:, part * LANES : (part + 1) * LANES]
                    squares[block] = piece if squares[block] is None else squares[block] + piece
        for block in range(tokens // LANES):
            rows = slice(block * LANES, (block + 1) * LANES)
            mean = jnp.sum(squares[block], axis=1, keepdims=True) * (1.0 / width)
            norm = lax.rsqrt(mean + 1e-05)
            for tile in range(width // WIDE):
                at = slice(tile * WIDE, (tile + 1) * WIDE)
                out_ref[rows, at] = (value_ref[rows, at] * norm * gain_ref[:, at]).astype(BF16)

    place = lax.rem(lax.axis_index("reader"), NEAR)

    @pl.when(place == 0)
    def _():
        finish(gathered)

    @pl.when(place == 1)
    def _():
        finish(gathered[::-1])


def shifted(value, axis, by):
    length = lax.axis_size(axis)
    return lax.ppermute(value, axis, [(i, i + by) for i in range(length - by)])


def params(limit=32):
    return pltpu.CompilerParams(vmem_limit_bytes=limit * MIB)


def whole(shape):
    return pl.BlockSpec(shape, lambda g: (0,) * len(shape))


def local(
    answer_lengths,
    mixer_input,
    gate_input,
    state_write,
    state_read,
    step_raw,
    decay_rate,
    skip_gain,
    norm_gain,
    prompt_state,
    queries,
    answer_keys,
    answer_values,
    prompt_keys,
    prompt_values,
):
    tokens, columns = mixer_input.shape
    heads = decay_rate.shape[0]
    state_rows, state = prompt_state.shape
    groups = state_write.shape[1] // state
    per_group = heads // groups
    channels = columns // heads
    width = per_group * channels
    prompt_rows, kv_width = prompt_keys.shape
    kv_count = kv_width // HD
    devices = lax.axis_size("reader")
    in_hbm = lambda value: pltpu.with_memory_space_constraint(value, pltpu.MemorySpace.HBM)
    prompt_state, prompt_keys, prompt_values = map(
        in_hbm, (prompt_state, prompt_keys, prompt_values)
    )
    lengths, rate, skip, gain = map(
        lambda value: in_hbm(value.reshape(1, -1)),
        (answer_lengths, decay_rate, skip_gain, norm_gain),
    )
    at_hand = pl.BlockSpec(memory_space=pltpu.VMEM)
    sizes = dict(heads=heads, per_group=per_group, channels=channels)
    packed_rows = state_rows + 2 * prompt_rows * kv_count

    packed = pl.pallas_call(
        pack_kernel,
        out_shape=jax.ShapeDtypeStruct((devices // NEAR, packed_rows, HD), BF16),
        out_specs=at_hand,
        compiler_params=params(),
        name="pack",
    )(prompt_state, prompt_keys, prompt_values)
    packed, near_keys = lax.optimization_barrier((packed, answer_keys))
    near = pl.pallas_call(
        join_kernel,
        out_shape=jax.ShapeDtypeStruct((tokens, 2 * kv_width), BF16),
        out_specs=at_hand,
        compiler_params=params(),
        name="join",
    )(in_hbm(near_keys), in_hbm(answer_values))
    packed, raw = lax.optimization_barrier((packed, step_raw.T))
    lines = [list(range(first, devices, NEAR)) for first in range(NEAR)]
    line = lax.all_to_all(packed, "reader", 0, 0, axis_index_groups=lines, tiled=True)
    prior = shifted(near, "reader", 1)
    raw = in_hbm(raw)

    small = pl.CostEstimate(flops=0, bytes_accessed=0, transcendentals=0)
    wide = pl.BlockSpec((tokens, width), lambda g: (0, g))
    tail, level, column, start = pl.pallas_call(
        functools.partial(tail_kernel, per_group=per_group, channels=channels),
        grid=(groups,),
        in_specs=[
            whole(lengths.shape),
            whole(raw.shape),
            whole((1, heads)),
            wide,
            pl.BlockSpec((tokens, state), lambda g: (0, g)),
        ],
        out_specs=(at_hand, at_hand, at_hand, at_hand),
        out_shape=(
            jax.ShapeDtypeStruct((columns + 2 * heads, state), BF16),
            jax.ShapeDtypeStruct((tokens, 2 * heads), F32),
            jax.ShapeDtypeStruct((heads, tokens), F32),
            jax.ShapeDtypeStruct((tokens, LANES), F32),
        ),
        scratch_shapes=[pltpu.VMEM((tokens, 2 * heads), F32)],
        compiler_params=params(),
        cost_estimate=small,
        name="tail",
    )(lengths, raw, rate, in_hbm(mixer_input), in_hbm(state_write))
    tail = shifted(tail, "reader", 1)
    inner = pl.pallas_call(
        functools.partial(inner_kernel, **sizes),
        grid=(groups,),
        in_specs=[
            at_hand,
            at_hand,
            at_hand,
            whole((1, heads)),
            at_hand,
            at_hand,
            at_hand,
        ],
        out_specs=at_hand,
        out_shape=jax.ShapeDtypeStruct((tokens, columns), BF16),
        compiler_params=params(),
        cost_estimate=small,
        name="inner",
    )(start, level, column, skip, mixer_input, state_write, state_read)
    prior, line, inner = lax.optimization_barrier((prior, line, inner))
    gathered = (line, lax.ppermute(line, "reader", [(i, i ^ 1) for i in range(devices)]))

    group_size = queries.shape[1] // kv_width
    attention_out = pl.pallas_call(
        functools.partial(
            attend_kernel,
            state_rows=state_rows,
            prompt_rows=prompt_rows,
            kv_count=kv_count,
        ),
        grid=(kv_count,),
        in_specs=[at_hand] * 5
        + [at_hand] * NEAR,
        out_specs=pl.BlockSpec((tokens, group_size * HD), lambda k: (0, k)),
        out_shape=jax.ShapeDtypeStruct(queries.shape, BF16),
        scratch_shapes=[pltpu.VMEM((tokens, tokens + LANES), F32)],
        compiler_params=params(),
        cost_estimate=small,
        name="attend",
    )(start, queries, answer_keys, answer_values, prior, *gathered)

    inner, attention_out = lax.optimization_barrier((inner, attention_out))
    mixer_out = pl.pallas_call(
        functools.partial(final_kernel, state_rows=state_rows, **sizes),
        grid=(groups,),
        in_specs=[
            at_hand,
            at_hand,
            pl.BlockSpec((width, state), lambda g: (g, 0)),
            pl.BlockSpec((2 * heads, state), lambda g: (columns // (2 * heads), 0)),
            at_hand,
            at_hand,
            at_hand,
            pl.BlockSpec((1, width), lambda g: (0, g)),
        ]
        + [at_hand] * NEAR,
        out_specs=wide,
        out_shape=jax.ShapeDtypeStruct((tokens, columns), BF16),
        scratch_shapes=[pltpu.VMEM((tokens, width), F32)],
        compiler_params=params(),
        cost_estimate=small,
        name="final",
    )(start, level, tail, tail, state_read, inner, gate_input, gain, *gathered)
    return (mixer_out, attention_out)


def solution(mesh):
    rows = P(("group", "reader"), None)
    in_specs = (P("group"),) + (rows,) * 5 + (P(),) * 3 + (rows,) * 6
    return jax.shard_map(
        local, mesh=mesh, in_specs=in_specs, out_specs=(rows, rows), check_vma=False
    )
```

```python
import functools
import math

import jax
import jax.numpy as jnp
from jax import lax
from jax.experimental import pallas as pl
from jax.experimental.pallas import tpu as pltpu
from jax.sharding import PartitionSpec as P

HD = 128
LANES = 128
WIDE = 256
NEAR = 2
LOG2E = 1.4426950408889634
F32 = jnp.float32
BF16 = jnp.bfloat16
MIB = 1 << 20


def iota(shape, dim):
    return lax.broadcasted_iota(jnp.int32, shape, dim)


def dot(a, b, ca=1, cb=0):
    return lax.dot_general(a, b, (((ca,), (cb,)), ((), ())), preferred_element_type=F32)


def expander(heads, group, per_group, channels):
    shape = (2 * heads, per_group * channels)
    row = iota(shape, 0)
    head = jnp.where(row >= heads, row - heads, row) - group * per_group
    column = iota(shape, 1)
    first = head * channels
    return jnp.where((column >= first) & (column < first + channels), 1.0, 0.0).astype(BF16)


def two_parts(value, heads):
    high = value.astype(BF16).astype(F32)
    return jnp.where(iota(value.shape, 1) < heads, high, value - high)


def to_front(value, head):
    return pltpu.roll(value, value.shape[1] - head, 1)


def spread(value, first, channels):
    lane = iota((8, LANES), 1)
    source = jnp.full((8, LANES), first, jnp.int32)
    for part in range(1, LANES // channels):
        source = source + jnp.where(lane >= part * channels, 1, 0)
    source = jnp.concatenate([source] * (value.shape[0] // 8), axis=0)
    return jnp.take_along_axis(value, source, axis=1, mode="promise_in_bounds")


def join_kernel(keys_ref, values_ref, out_ref):
    width = keys_ref.shape[1]
    out_ref[:, :width] = keys_ref[...]
    out_ref[:, width:] = values_ref[...]


def pack_kernel(state_ref, keys_ref, values_ref, out_ref, held_ref, sems):
    rows = state_ref.shape[0]
    held_ref[:rows, :] = state_ref[...].astype(BF16)
    parts = []
    for ref in (keys_ref, values_ref):
        wide = ref[...].astype(F32)
        for head in range(wide.shape[1] // HD):
            parts.append(wide[:, head * HD : (head + 1) * HD])
    held_ref[rows:, :] = jnp.concatenate(parts, axis=0).astype(BF16)
    copies = [
        pltpu.make_async_copy(held_ref, out_ref.at[place], sems.at[place])
        for place in range(out_ref.shape[0])
    ]
    for copy in copies:
        copy.start()
    for copy in copies:
        copy.wait()


def level_part(lengths_ref, raw_ref, rate_ref, level_ref, column_ref, start_ref, weight_ref, tail_ref):
    heads, tokens = raw_ref.shape
    base = (lax.axis_index("reader") * tokens).astype(F32)
    lengths = lengths_ref[...].astype(F32)
    answers = lengths.shape[1]
    square = (answers, answers)
    ends = jnp.sum(
        jnp.where(iota(square, 1) <= iota(square, 0), lengths, 0.0), axis=1, keepdims=True
    )
    place = base + iota((1, tokens), 1).astype(F32)
    start = jnp.max(jnp.where(ends <= place, ends, 0.0), axis=0, keepdims=True) - base
    start = jnp.broadcast_to(start, (LANES, tokens)).T
    start_ref[...] = start
    wide = jnp.concatenate([start] * (tokens // LANES), axis=1)
    square = (tokens, tokens)
    source = iota(square, 1)
    mask = (source.astype(F32) >= wide) & (source <= iota(square, 0))
    mask = jnp.where(mask, 1.0, 0.0).astype(BF16)
    raw = raw_ref[...]
    rate = jnp.broadcast_to(rate_ref[...], (heads, heads))
    diagonal = iota((heads, heads), 0) == iota((heads, heads), 1)
    rate = jnp.sum(jnp.where(diagonal, rate, 0.0), axis=1, keepdims=True)
    step = jnp.maximum(raw, 0.0) + jnp.log1p(jnp.exp(-jnp.abs(raw)))
    falling = -rate * step
    first = falling.astype(BF16)
    rest = falling - first.astype(F32)
    second = rest.astype(BF16)
    third = (rest - second.astype(F32)).astype(BF16)
    level = dot(first, mask, 1, 1) + (dot(second, mask, 1, 1) + dot(third, mask, 1, 1))
    column_ref[...] = level * LOG2E - jnp.log(step) * LOG2E
    last = level[:, tokens - 1 :]
    decay = jnp.exp(jnp.broadcast_to(last, (heads, tail_ref.shape[1])))
    high = decay.astype(BF16)
    low = (decay - high.astype(F32)).astype(BF16)
    tail_ref[tail_ref.shape[0] - 2 * heads :, :] = jnp.concatenate([high, low], axis=0)
    own = iota((heads, tokens), 1).astype(F32) >= start[tokens - 1 :, :1]
    weight = jnp.where(own, jnp.exp(last - level) * step, 0.0)
    weight_ref[...] = jnp.concatenate([weight, weight], axis=0).T
    level_ref[...] = jnp.concatenate([level, level], axis=0).T


def tail_part(group, weight_ref, x_ref, write_ref, tail_ref, per_group, channels):
    width = per_group * channels
    begin = pl.multiple_of(group * width, width)
    weight = to_front(weight_ref[...], group * per_group)
    weighted = []
    for tile in range(width // LANES):
        scale = spread(weight, tile * LANES // channels, channels)
        x = x_ref[:, tile * LANES : (tile + 1) * LANES].astype(F32)
        weighted.append((x * scale).astype(BF16))
    state = dot(jnp.concatenate(weighted, axis=1), write_ref[...], 0, 0)
    tail_ref[pl.ds(begin, width), :] = state.astype(BF16)


def tail_kernel(
    lengths_ref,
    raw_ref,
    rate_ref,
    x_ref,
    write_ref,
    tail_ref,
    level_ref,
    column_ref,
    start_ref,
    weight_ref,
    *,
    per_group,
    channels,
):
    group = pl.program_id(0)

    @pl.when(group == 0)
    def _():
        level_part(
            lengths_ref, raw_ref, rate_ref, level_ref, column_ref, start_ref, weight_ref, tail_ref
        )

    tail_part(group, weight_ref, x_ref, write_ref, tail_ref, per_group, channels)


def inner_kernel(
    start_ref,
    level_ref,
    column_ref,
    skip_ref,
    x_ref,
    write_ref,
    read_ref,
    out_ref,
    *,
    heads,
    per_group,
    channels,
):
    group = pl.program_id(0)
    tokens = x_ref.shape[0]
    size = read_ref.shape[1] // (heads // per_group)
    own = pl.ds(pl.multiple_of(group * size, size), size)
    both = dot(read_ref[:, own], write_ref[:, own], 1, 1)
    square = (tokens, tokens)
    source = iota(square, 1)
    wide = jnp.concatenate([start_ref[...]] * (tokens // LANES), axis=1)
    both = jnp.where((source.astype(F32) >= wide) & (source <= iota(square, 0)), both, 0.0)
    lanes = level_ref.shape[1]
    level = pltpu.roll(level_ref[...] * LOG2E, lanes - group * per_group, 1)
    column = column_ref[pl.ds(pl.multiple_of(group * per_group, per_group), per_group), :]
    begin = pl.multiple_of(group * per_group * channels, per_group * channels)
    skip = jnp.concatenate([skip_ref[...]] * 2, axis=1)
    skip = two_parts(jnp.broadcast_to(skip, (16, 2 * heads)), heads).astype(BF16)
    skip = dot(skip, expander(heads, group, per_group, channels))[:1, :]
    per_tile = LANES // channels
    lane = iota((tokens, LANES), 1)
    for tile in range(per_group // per_tile):
        at = slice(tile * LANES, (tile + 1) * LANES)
        x = x_ref[:, pl.ds(begin + at.start, LANES)].astype(F32)
        owned = []
        for part in range(per_tile):
            mine = (lane >= part * channels) & (lane < (part + 1) * channels)
            owned.append(jnp.where(mine, x, 0.0).astype(BF16))
        for block in range(tokens // LANES):
            rows = slice(block * LANES, (block + 1) * LANES)
            reach = (block + 1) * LANES
            mixing = []
            for part in range(per_tile):
                head = tile * per_tile + part
                gap = level[rows, head : head + 1] - column[head : head + 1, :reach]
                mixing.append(
                    (jnp.exp2(jnp.minimum(gap, 64.0)) * both[rows, :reach]).astype(BF16)
                )
            total = dot(
                jnp.concatenate(mixing, axis=1),
                jnp.concatenate([value[:reach, :] for value in owned], axis=0),
            )
            out_ref[rows, pl.ds(begin + at.start, LANES)] = (
                total + skip[:, at] * x[rows, :]
            ).astype(BF16)


def attend_kernel(
    start_ref,
    query_ref,
    key_ref,
    value_ref,
    prior_ref,
    *rest,
    state_rows,
    prompt_rows,
    kv_count,
):
    gathered, (out_ref, bias_ref) = rest[:-2], rest[-2:]
    head = pl.program_id(0)
    tokens = query_ref.shape[0]
    own = pl.ds(pl.multiple_of(head * HD, HD), HD)
    prompt_count = len(gathered) * gathered[0].shape[0] * prompt_rows
    queries = query_ref.shape[1] // HD // kv_count
    scale = LOG2E / math.sqrt(HD)
    reach = tokens + LANES

    @pl.when(head == 0)
    def _():
        shape = (LANES, reach)
        wide = jnp.concatenate([start_ref[...]] * (reach // LANES), axis=1)
        for block in range(tokens // LANES):
            rows = slice(block * LANES, (block + 1) * LANES)
            place = iota(shape, 1) + (block * LANES - tokens)
            allowed = (place.astype(F32) >= wide[rows, :]) & (
                place <= iota(shape, 0) + block * LANES
            )
            bias_ref[rows, :] = jnp.where(allowed, 0.0, -jnp.inf)

    def prompt(which):
        at = pl.multiple_of(state_rows + (which * kv_count + head) // 2 * 2 * prompt_rows, 16)
        at = pl.ds(at, 2 * prompt_rows)
        pair = jnp.concatenate([ref[:, at, :] for ref in gathered], axis=0).astype(F32)
        odd = lax.rem(head, 2) == 1
        part = jnp.where(odd, pair[:, prompt_rows:, :], pair[:, :prompt_rows, :])
        return part.reshape(prompt_count, HD).astype(BF16)

    prompt_keys, prompt_values = prompt(0), prompt(1)
    prior = [
        prior_ref[:, pl.ds(pl.multiple_of((which * kv_count + head) * HD, HD), HD)]
        for which in range(2)
    ]
    near_keys = jnp.concatenate([prior[0], key_ref[:, own]], axis=0)
    near_values = jnp.concatenate([prior[1], value_ref[:, own]], axis=0)
    ones = jnp.ones((prompt_count + reach, LANES), BF16)
    for block in range(tokens // LANES):
        rows = slice(block * LANES, (block + 1) * LANES)
        window = slice(block * LANES, block * LANES + reach)
        keys = jnp.concatenate([prompt_keys, near_keys[window, :]], axis=0)
        values = jnp.concatenate([prompt_values, near_values[window, :]], axis=0)
        values = jnp.concatenate([values, ones], axis=1)
        begin = pl.multiple_of(head * queries * HD, queries * HD)
        stacked = [query_ref[rows, pl.ds(begin + query * HD, HD)] for query in range(queries)]
        scores = dot(jnp.concatenate(stacked, axis=0), keys, 1, 1)
        weights = []
        for query in range(queries):
            own = scores[query * LANES : (query + 1) * LANES, :]
            far, near = own[:, :prompt_count], own[:, prompt_count:] + bias_ref[rows, :]
            own = jnp.concatenate([far, near], axis=1)
            top = jnp.max(own, axis=1, keepdims=True)
            weights.append(jnp.exp2((own - top) * scale).astype(BF16))
        summed = dot(jnp.concatenate(weights, axis=0), values)
        for query in range(queries):
            own = summed[query * LANES : (query + 1) * LANES, :]
            out_ref[rows, query * HD : (query + 1) * HD] = (own[:, :HD] / own[:, HD:]).astype(BF16)


def final_kernel(
    start_ref,
    level_ref,
    tail_ref,
    decay_ref,
    read_ref,
    inner_ref,
    gate_ref,
    gain_ref,
    *rest,
    state_rows,
    heads,
    per_group,
    channels,
):
    gathered, (out_ref, value_ref) = rest[:NEAR], rest[-2:]
    group = pl.program_id(0)
    tokens = read_ref.shape[0]
    width, state = per_group * channels, tail_ref.shape[1]

    scale = to_front(jnp.exp(level_ref[...]), group * per_group)
    carried = start_ref[:, :state] < 0
    read = read_ref[:, pl.ds(pl.multiple_of(group * state, state), state)].astype(F32)
    fresh = jnp.where(carried, 0.0, read).astype(BF16)
    kept = jnp.where(carried, read, 0.0).astype(BF16)
    read = jnp.concatenate([fresh, kept, kept], axis=1)
    falls_at = pl.multiple_of(group * per_group, per_group)
    decay = decay_ref[pl.ds(falls_at, per_group), :].astype(F32)
    decay = decay + decay_ref[pl.ds(falls_at + heads, per_group), :].astype(F32)
    begin = pl.multiple_of(group * width, width)
    runs = width // (NEAR * state_rows)

    def finish(in_order):
        seeds = [
            ref[group * runs + run, :state_rows, :] for run in range(runs) for ref in in_order
        ]
        seeds = jnp.concatenate(seeds, axis=0)
        squares = [None] * (tokens // LANES)
        for tile in range(width // WIDE):
            at = slice(tile * WIDE, (tile + 1) * WIDE)
            tile_heads = range(at.start // channels, at.stop // channels)
            falls = [jnp.broadcast_to(decay[h : h + 1, :], (channels, state)) for h in tile_heads]
            seed = seeds[at, :]
            faded = (seed.astype(F32) * jnp.concatenate(falls, axis=0)).astype(BF16)
            states = jnp.concatenate([seed, faded, tail_ref[at, :]], axis=1)
            inflows = dot(read, states, 1, 1)
            for block in range(tokens // LANES):
                rows = slice(block * LANES, (block + 1) * LANES)
                falls = [
                    spread(scale[rows, :], (at.start + offset) // channels, channels)
                    for offset in range(0, WIDE, LANES)
                ]
                inflow = inflows[rows, :] * jnp.concatenate(falls, axis=1)
                own = pl.ds(begin + at.start, WIDE)
                half = 0.5 * gate_ref[rows, own].astype(F32)
                gated = inner_ref[rows, own].astype(F32) + inflow
                gated = gated * (half + half * jnp.tanh(half))
                value_ref[rows, at] = gated
                square = gated * gated
                for part in range(WIDE // LANES):
                    piece = square[:, part * LANES : (part + 1) * LANES]
                    squares[block] = piece if squares[block] is None else squares[block] + piece
        for block in range(tokens // LANES):
            rows = slice(block * LANES, (block + 1) * LANES)
            mean = jnp.sum(squares[block], axis=1, keepdims=True) * (1.0 / width)
            norm = lax.rsqrt(mean + 1e-05)
            for tile in range(width // WIDE):
                at = slice(tile * WIDE, (tile + 1) * WIDE)
                out_ref[rows, at] = (value_ref[rows, at] * norm * gain_ref[:, at]).astype(BF16)

    place = lax.rem(lax.axis_index("reader"), NEAR)

    @pl.when(place == 0)
    def _():
        finish(gathered)

    @pl.when(place == 1)
    def _():
        finish(gathered[::-1])


def shifted(value, axis, by):
    length = lax.axis_size(axis)
    return lax.ppermute(value, axis, [(i, i + by) for i in range(length - by)])


def params(limit=32):
    return pltpu.CompilerParams(vmem_limit_bytes=limit * MIB)


def whole(shape):
    return pl.BlockSpec(shape, lambda g: (0,) * len(shape))


def local(
    answer_lengths,
    mixer_input,
    gate_input,
    state_write,
    state_read,
    step_raw,
    decay_rate,
    skip_gain,
    norm_gain,
    prompt_state,
    queries,
    answer_keys,
    answer_values,
    prompt_keys,
    prompt_values,
):
    tokens, columns = mixer_input.shape
    heads = decay_rate.shape[0]
    state_rows, state = prompt_state.shape
    groups = state_write.shape[1] // state
    per_group = heads // groups
    channels = columns // heads
    width = per_group * channels
    prompt_rows, kv_width = prompt_keys.shape
    kv_count = kv_width // HD
    devices = lax.axis_size("reader")
    in_hbm = lambda value: pltpu.with_memory_space_constraint(value, pltpu.MemorySpace.HBM)
    prompt_state, prompt_keys, prompt_values = map(
        in_hbm, (prompt_state, prompt_keys, prompt_values)
    )
    lengths, rate, skip, gain = map(
        lambda value: in_hbm(value.reshape(1, -1)),
        (answer_lengths, decay_rate, skip_gain, norm_gain),
    )
    at_hand = pl.BlockSpec(memory_space=pltpu.VMEM)
    sizes = dict(heads=heads, per_group=per_group, channels=channels)
    packed_rows = state_rows + 2 * prompt_rows * kv_count

    packed = pl.pallas_call(
        pack_kernel,
        out_shape=jax.ShapeDtypeStruct((devices // NEAR, packed_rows, HD), BF16),
        out_specs=pl.BlockSpec(memory_space=pl.ANY),
        scratch_shapes=[
            pltpu.VMEM((packed_rows, HD), BF16),
            pltpu.SemaphoreType.DMA((devices // NEAR,)),
        ],
        compiler_params=params(),
        name="pack",
    )(prompt_state, prompt_keys, prompt_values)
    packed, near_keys = lax.optimization_barrier((packed, answer_keys))
    near = pl.pallas_call(
        join_kernel,
        out_shape=jax.ShapeDtypeStruct((tokens, 2 * kv_width), BF16),
        out_specs=at_hand,
        compiler_params=params(),
        name="join",
    )(in_hbm(near_keys), in_hbm(answer_values))
    packed, raw = lax.optimization_barrier((packed, step_raw.T))
    lines = [list(range(first, devices, NEAR)) for first in range(NEAR)]
    line = lax.all_to_all(packed, "reader", 0, 0, axis_index_groups=lines, tiled=True)
    prior = shifted(near, "reader", 1)
    raw = in_hbm(raw)

    small = pl.CostEstimate(flops=0, bytes_accessed=0, transcendentals=0)
    wide = pl.BlockSpec((tokens, width), lambda g: (0, g))
    tail, level, column, start = pl.pallas_call(
        functools.partial(tail_kernel, per_group=per_group, channels=channels),
        grid=(groups,),
        in_specs=[
            whole(lengths.shape),
            whole(raw.shape),
            whole((1, heads)),
            wide,
            pl.BlockSpec((tokens, state), lambda g: (0, g)),
        ],
        out_specs=(at_hand, at_hand, at_hand, at_hand),
        out_shape=(
            jax.ShapeDtypeStruct((columns + 2 * heads, state), BF16),
            jax.ShapeDtypeStruct((tokens, 2 * heads), F32),
            jax.ShapeDtypeStruct((heads, tokens), F32),
            jax.ShapeDtypeStruct((tokens, LANES), F32),
        ),
        scratch_shapes=[pltpu.VMEM((tokens, 2 * heads), F32)],
        compiler_params=params(),
        cost_estimate=small,
        name="tail",
    )(lengths, raw, rate, in_hbm(mixer_input), in_hbm(state_write))
    tail = shifted(tail, "reader", 1)
    inner = pl.pallas_call(
        functools.partial(inner_kernel, **sizes),
        grid=(groups,),
        in_specs=[
            at_hand,
            at_hand,
            at_hand,
            whole((1, heads)),
            at_hand,
            at_hand,
            at_hand,
        ],
        out_specs=at_hand,
        out_shape=jax.ShapeDtypeStruct((tokens, columns), BF16),
        compiler_params=params(),
        cost_estimate=small,
        name="inner",
    )(start, level, column, skip, mixer_input, state_write, state_read)
    prior, line, inner = lax.optimization_barrier((prior, line, inner))
    gathered = (line, lax.ppermute(line, "reader", [(i, i ^ 1) for i in range(devices)]))

    group_size = queries.shape[1] // kv_width
    attention_out = pl.pallas_call(
        functools.partial(
            attend_kernel,
            state_rows=state_rows,
            prompt_rows=prompt_rows,
            kv_count=kv_count,
        ),
        grid=(kv_count,),
        in_specs=[at_hand] * 5
        + [at_hand] * NEAR,
        out_specs=pl.BlockSpec((tokens, group_size * HD), lambda k: (0, k)),
        out_shape=jax.ShapeDtypeStruct(queries.shape, BF16),
        scratch_shapes=[pltpu.VMEM((tokens, tokens + LANES), F32)],
        compiler_params=params(),
        cost_estimate=small,
        name="attend",
    )(start, queries, answer_keys, answer_values, prior, *gathered)

    inner, attention_out = lax.optimization_barrier((inner, attention_out))
    mixer_out = pl.pallas_call(
        functools.partial(final_kernel, state_rows=state_rows, **sizes),
        grid=(groups,),
        in_specs=[
            at_hand,
            at_hand,
            pl.BlockSpec((width, state), lambda g: (g, 0)),
            pl.BlockSpec((2 * heads, state), lambda g: (columns // (2 * heads), 0)),
            at_hand,
            at_hand,
            at_hand,
            pl.BlockSpec((1, width), lambda g: (0, g)),
        ]
        + [at_hand] * NEAR,
        out_specs=wide,
        out_shape=jax.ShapeDtypeStruct((tokens, columns), BF16),
        scratch_shapes=[pltpu.VMEM((tokens, width), F32)],
        compiler_params=params(),
        cost_estimate=small,
        name="final",
    )(start, level, tail, tail, state_read, inner, gate_input, gain, *gathered)
    return (mixer_out, attention_out)


def solution(mesh):
    rows = P(("group", "reader"), None)
    in_specs = (P("group"),) + (rows,) * 5 + (P(),) * 3 + (rows,) * 6
    return jax.shard_map(
        local, mesh=mesh, in_specs=in_specs, out_specs=(rows, rows), check_vma=False
    )
```

```python
import functools
import math

import jax
import jax.numpy as jnp
from jax import lax
from jax.experimental import pallas as pl
from jax.experimental.pallas import tpu as pltpu
from jax.sharding import PartitionSpec as P

HD = 128
LANES = 128
WIDE = 512
NEAR = 2
LOG2E = 1.4426950408889634
F32 = jnp.float32
BF16 = jnp.bfloat16
MIB = 1 << 20


def iota(shape, dim):
    return lax.broadcasted_iota(jnp.int32, shape, dim)


def dot(a, b, ca=1, cb=0):
    return lax.dot_general(a, b, (((ca,), (cb,)), ((), ())), preferred_element_type=F32)


def expander(heads, group, per_group, channels):
    shape = (2 * heads, per_group * channels)
    row = iota(shape, 0)
    head = jnp.where(row >= heads, row - heads, row) - group * per_group
    column = iota(shape, 1)
    first = head * channels
    return jnp.where((column >= first) & (column < first + channels), 1.0, 0.0).astype(BF16)


def two_parts(value, heads):
    high = value.astype(BF16).astype(F32)
    return jnp.where(iota(value.shape, 1) < heads, high, value - high)


def to_front(value, head):
    return pltpu.roll(value, value.shape[1] - head, 1)


def spread(value, first, channels):
    lane = iota((8, LANES), 1)
    source = jnp.full((8, LANES), first, jnp.int32)
    for part in range(1, LANES // channels):
        source = source + jnp.where(lane >= part * channels, 1, 0)
    source = jnp.concatenate([source] * (value.shape[0] // 8), axis=0)
    return jnp.take_along_axis(value, source, axis=1, mode="promise_in_bounds")


def join_kernel(keys_ref, values_ref, out_ref):
    width = keys_ref.shape[1]
    out_ref[:, :width] = keys_ref[...]
    out_ref[:, width:] = values_ref[...]


def pack_kernel(state_ref, keys_ref, values_ref, out_ref, held_ref, sems):
    rows = state_ref.shape[0]
    held_ref[:rows, :] = state_ref[...].astype(BF16)
    parts = []
    for ref in (keys_ref, values_ref):
        wide = ref[...].astype(F32)
        for head in range(wide.shape[1] // HD):
            parts.append(wide[:, head * HD : (head + 1) * HD])
    held_ref[rows:, :] = jnp.concatenate(parts, axis=0).astype(BF16)
    copies = [
        pltpu.make_async_copy(held_ref, out_ref.at[place], sems.at[place])
        for place in range(out_ref.shape[0])
    ]
    for copy in copies:
        copy.start()
    for copy in copies:
        copy.wait()


def level_part(lengths_ref, raw_ref, rate_ref, level_ref, column_ref, start_ref, weight_ref, tail_ref):
    heads, tokens = raw_ref.shape
    base = (lax.axis_index("reader") * tokens).astype(F32)
    lengths = lengths_ref[...].astype(F32)
    answers = lengths.shape[1]
    square = (answers, answers)
    ends = jnp.sum(
        jnp.where(iota(square, 1) <= iota(square, 0), lengths, 0.0), axis=1, keepdims=True
    )
    place = base + iota((1, tokens), 1).astype(F32)
    start = jnp.max(jnp.where(ends <= place, ends, 0.0), axis=0, keepdims=True) - base
    start = jnp.broadcast_to(start, (LANES, tokens)).T
    start_ref[...] = start
    wide = jnp.concatenate([start] * (tokens // LANES), axis=1)
    square = (tokens, tokens)
    source = iota(square, 1)
    mask = (source.astype(F32) >= wide) & (source <= iota(square, 0))
    mask = jnp.where(mask, 1.0, 0.0).astype(BF16)
    raw = raw_ref[...]
    rate = jnp.broadcast_to(rate_ref[...], (heads, heads))
    diagonal = iota((heads, heads), 0) == iota((heads, heads), 1)
    rate = jnp.sum(jnp.where(diagonal, rate, 0.0), axis=1, keepdims=True)
    step = jnp.maximum(raw, 0.0) + jnp.log1p(jnp.exp(-jnp.abs(raw)))
    falling = -rate * step
    first = falling.astype(BF16)
    rest = falling - first.astype(F32)
    second = rest.astype(BF16)
    third = (rest - second.astype(F32)).astype(BF16)
    level = dot(first, mask, 1, 1) + (dot(second, mask, 1, 1) + dot(third, mask, 1, 1))
    column_ref[...] = level * LOG2E - jnp.log(step) * LOG2E
    last = level[:, tokens - 1 :]
    decay = jnp.exp(jnp.broadcast_to(last, (heads, tail_ref.shape[1])))
    high = decay.astype(BF16)
    low = (decay - high.astype(F32)).astype(BF16)
    tail_ref[tail_ref.shape[0] - 2 * heads :, :] = jnp.concatenate([high, low], axis=0)
    own = iota((heads, tokens), 1).astype(F32) >= start[tokens - 1 :, :1]
    weight = jnp.where(own, jnp.exp(last - level) * step, 0.0)
    weight_ref[...] = jnp.concatenate([weight, weight], axis=0).T
    level_ref[...] = jnp.concatenate([level, level], axis=0).T


def tail_part(group, weight_ref, x_ref, write_ref, tail_ref, per_group, channels):
    width = per_group * channels
    begin = pl.multiple_of(group * width, width)
    weight = to_front(weight_ref[...], group * per_group)
    weighted = []
    for tile in range(width // LANES):
        scale = spread(weight, tile * LANES // channels, channels)
        x = x_ref[:, tile * LANES : (tile + 1) * LANES].astype(F32)
        weighted.append((x * scale).astype(BF16))
    state = dot(jnp.concatenate(weighted, axis=1), write_ref[...], 0, 0)
    tail_ref[pl.ds(begin, width), :] = state.astype(BF16)


def tail_kernel(
    lengths_ref,
    raw_ref,
    rate_ref,
    x_ref,
    write_ref,
    tail_ref,
    level_ref,
    column_ref,
    start_ref,
    weight_ref,
    *,
    per_group,
    channels,
):
    group = pl.program_id(0)

    @pl.when(group == 0)
    def _():
        level_part(
            lengths_ref, raw_ref, rate_ref, level_ref, column_ref, start_ref, weight_ref, tail_ref
        )

    tail_part(group, weight_ref, x_ref, write_ref, tail_ref, per_group, channels)


def inner_kernel(
    start_ref,
    level_ref,
    column_ref,
    skip_ref,
    x_ref,
    write_ref,
    read_ref,
    out_ref,
    *,
    heads,
    per_group,
    channels,
):
    group = pl.program_id(0)
    tokens = x_ref.shape[0]
    size = read_ref.shape[1] // (heads // per_group)
    own = pl.ds(pl.multiple_of(group * size, size), size)
    both = dot(read_ref[:, own], write_ref[:, own], 1, 1)
    square = (tokens, tokens)
    source = iota(square, 1)
    wide = jnp.concatenate([start_ref[...]] * (tokens // LANES), axis=1)
    both = jnp.where((source.astype(F32) >= wide) & (source <= iota(square, 0)), both, 0.0)
    lanes = level_ref.shape[1]
    level = pltpu.roll(level_ref[...] * LOG2E, lanes - group * per_group, 1)
    column = column_ref[pl.ds(pl.multiple_of(group * per_group, per_group), per_group), :]
    begin = pl.multiple_of(group * per_group * channels, per_group * channels)
    skip = jnp.concatenate([skip_ref[...]] * 2, axis=1)
    skip = two_parts(jnp.broadcast_to(skip, (16, 2 * heads)), heads).astype(BF16)
    skip = dot(skip, expander(heads, group, per_group, channels))[:1, :]
    per_tile = LANES // channels
    lane = iota((tokens, LANES), 1)
    for tile in range(per_group // per_tile):
        at = slice(tile * LANES, (tile + 1) * LANES)
        x = x_ref[:, pl.ds(begin + at.start, LANES)].astype(F32)
        owned = []
        for part in range(per_tile):
            mine = (lane >= part * channels) & (lane < (part + 1) * channels)
            owned.append(jnp.where(mine, x, 0.0).astype(BF16))
        for block in range(tokens // LANES):
            rows = slice(block * LANES, (block + 1) * LANES)
            reach = (block + 1) * LANES
            mixing = []
            for part in range(per_tile):
                head = tile * per_tile + part
                gap = level[rows, head : head + 1] - column[head : head + 1, :reach]
                mixing.append(
                    (jnp.exp2(jnp.minimum(gap, 64.0)) * both[rows, :reach]).astype(BF16)
                )
            total = dot(
                jnp.concatenate(mixing, axis=1),
                jnp.concatenate([value[:reach, :] for value in owned], axis=0),
            )
            out_ref[rows, pl.ds(begin + at.start, LANES)] = (
                total + skip[:, at] * x[rows, :]
            ).astype(BF16)


def attend_kernel(
    start_ref,
    query_ref,
    key_ref,
    value_ref,
    prior_ref,
    *rest,
    state_rows,
    prompt_rows,
    kv_count,
):
    gathered, (out_ref, bias_ref) = rest[:-2], rest[-2:]
    head = pl.program_id(0)
    tokens = query_ref.shape[0]
    own = pl.ds(pl.multiple_of(head * HD, HD), HD)
    prompt_count = len(gathered) * gathered[0].shape[0] * prompt_rows
    queries = query_ref.shape[1] // HD // kv_count
    scale = LOG2E / math.sqrt(HD)
    reach = tokens + LANES

    @pl.when(head == 0)
    def _():
        shape = (LANES, reach)
        wide = jnp.concatenate([start_ref[...]] * (reach // LANES), axis=1)
        for block in range(tokens // LANES):
            rows = slice(block * LANES, (block + 1) * LANES)
            place = iota(shape, 1) + (block * LANES - tokens)
            allowed = (place.astype(F32) >= wide[rows, :]) & (
                place <= iota(shape, 0) + block * LANES
            )
            bias_ref[rows, :] = jnp.where(allowed, 0.0, -jnp.inf)

    def prompt(which):
        at = pl.multiple_of(state_rows + (which * kv_count + head) // 2 * 2 * prompt_rows, 16)
        at = pl.ds(at, 2 * prompt_rows)
        pair = jnp.concatenate([ref[:, at, :] for ref in gathered], axis=0).astype(F32)
        odd = lax.rem(head, 2) == 1
        part = jnp.where(odd, pair[:, prompt_rows:, :], pair[:, :prompt_rows, :])
        return part.reshape(prompt_count, HD).astype(BF16)

    prompt_keys, prompt_values = prompt(0), prompt(1)
    prior = [
        prior_ref[:, pl.ds(pl.multiple_of((which * kv_count + head) * HD, HD), HD)]
        for which in range(2)
    ]
    near_keys = jnp.concatenate([prior[0], key_ref[:, own]], axis=0)
    near_values = jnp.concatenate([prior[1], value_ref[:, own]], axis=0)
    ones = jnp.ones((prompt_count + reach, LANES), BF16)
    for block in range(tokens // LANES):
        rows = slice(block * LANES, (block + 1) * LANES)
        window = slice(block * LANES, block * LANES + reach)
        keys = jnp.concatenate([prompt_keys, near_keys[window, :]], axis=0)
        values = jnp.concatenate([prompt_values, near_values[window, :]], axis=0)
        values = jnp.concatenate([values, ones], axis=1)
        begin = pl.multiple_of(head * queries * HD, queries * HD)
        stacked = [query_ref[rows, pl.ds(begin + query * HD, HD)] for query in range(queries)]
        scores = dot(jnp.concatenate(stacked, axis=0), keys, 1, 1)
        weights = []
        for query in range(queries):
            own = scores[query * LANES : (query + 1) * LANES, :]
            far, near = own[:, :prompt_count], own[:, prompt_count:] + bias_ref[rows, :]
            own = jnp.concatenate([far, near], axis=1)
            top = jnp.max(own, axis=1, keepdims=True)
            weights.append(jnp.exp2((own - top) * scale).astype(BF16))
        summed = dot(jnp.concatenate(weights, axis=0), values)
        for query in range(queries):
            own = summed[query * LANES : (query + 1) * LANES, :]
            out_ref[rows, query * HD : (query + 1) * HD] = (own[:, :HD] / own[:, HD:]).astype(BF16)


def final_kernel(
    start_ref,
    level_ref,
    tail_ref,
    decay_ref,
    read_ref,
    inner_ref,
    gate_ref,
    gain_ref,
    *rest,
    state_rows,
    heads,
    per_group,
    channels,
):
    gathered, (out_ref, value_ref) = rest[:NEAR], rest[-2:]
    group = pl.program_id(0)
    tokens = read_ref.shape[0]
    width, state = per_group * channels, tail_ref.shape[1]

    scale = to_front(jnp.exp(level_ref[...]), group * per_group)
    carried = start_ref[:, :state] < 0
    read = read_ref[:, pl.ds(pl.multiple_of(group * state, state), state)].astype(F32)
    fresh = jnp.where(carried, 0.0, read).astype(BF16)
    kept = jnp.where(carried, read, 0.0).astype(BF16)
    read = jnp.concatenate([fresh, kept, kept], axis=1)
    falls_at = pl.multiple_of(group * per_group, per_group)
    decay = decay_ref[pl.ds(falls_at, per_group), :].astype(F32)
    decay = decay + decay_ref[pl.ds(falls_at + heads, per_group), :].astype(F32)
    begin = pl.multiple_of(group * width, width)
    runs = width // (NEAR * state_rows)

    def finish(in_order):
        seeds = [
            ref[group * runs + run, :state_rows, :] for run in range(runs) for ref in in_order
        ]
        seeds = jnp.concatenate(seeds, axis=0)
        squares = [None] * (tokens // LANES)
        for tile in range(width // WIDE):
            at = slice(tile * WIDE, (tile + 1) * WIDE)
            tile_heads = range(at.start // channels, at.stop // channels)
            falls = [jnp.broadcast_to(decay[h : h + 1, :], (channels, state)) for h in tile_heads]
            seed = seeds[at, :]
            faded = (seed.astype(F32) * jnp.concatenate(falls, axis=0)).astype(BF16)
            states = jnp.concatenate([seed, faded, tail_ref[at, :]], axis=1)
            inflows = dot(read, states, 1, 1)
            for block in range(tokens // LANES):
                rows = slice(block * LANES, (block + 1) * LANES)
                falls = [
                    spread(scale[rows, :], (at.start + offset) // channels, channels)
                    for offset in range(0, WIDE, LANES)
                ]
                inflow = inflows[rows, :] * jnp.concatenate(falls, axis=1)
                own = pl.ds(begin + at.start, WIDE)
                half = 0.5 * gate_ref[rows, own].astype(F32)
                gated = inner_ref[rows, own].astype(F32) + inflow
                gated = gated * (half + half * jnp.tanh(half))
                value_ref[rows, at] = gated
                square = gated * gated
                for part in range(WIDE // LANES):
                    piece = square[:, part * LANES : (part + 1) * LANES]
                    squares[block] = piece if squares[block] is None else squares[block] + piece
        for block in range(tokens // LANES):
            rows = slice(block * LANES, (block + 1) * LANES)
            mean = jnp.sum(squares[block], axis=1, keepdims=True) * (1.0 / width)
            norm = lax.rsqrt(mean + 1e-05)
            for tile in range(width // WIDE):
                at = slice(tile * WIDE, (tile + 1) * WIDE)
                out_ref[rows, at] = (value_ref[rows, at] * norm * gain_ref[:, at]).astype(BF16)

    place = lax.rem(lax.axis_index("reader"), NEAR)

    @pl.when(place == 0)
    def _():
        finish(gathered)

    @pl.when(place == 1)
    def _():
        finish(gathered[::-1])


def shifted(value, axis, by):
    length = lax.axis_size(axis)
    return lax.ppermute(value, axis, [(i, i + by) for i in range(length - by)])


def params(limit=32):
    return pltpu.CompilerParams(vmem_limit_bytes=limit * MIB)


def whole(shape):
    return pl.BlockSpec(shape, lambda g: (0,) * len(shape))


def local(
    answer_lengths,
    mixer_input,
    gate_input,
    state_write,
    state_read,
    step_raw,
    decay_rate,
    skip_gain,
    norm_gain,
    prompt_state,
    queries,
    answer_keys,
    answer_values,
    prompt_keys,
    prompt_values,
):
    tokens, columns = mixer_input.shape
    heads = decay_rate.shape[0]
    state_rows, state = prompt_state.shape
    groups = state_write.shape[1] // state
    per_group = heads // groups
    channels = columns // heads
    width = per_group * channels
    prompt_rows, kv_width = prompt_keys.shape
    kv_count = kv_width // HD
    devices = lax.axis_size("reader")
    in_hbm = lambda value: pltpu.with_memory_space_constraint(value, pltpu.MemorySpace.HBM)
    prompt_state, prompt_keys, prompt_values = map(
        in_hbm, (prompt_state, prompt_keys, prompt_values)
    )
    lengths, rate, skip, gain = map(
        lambda value: in_hbm(value.reshape(1, -1)),
        (answer_lengths, decay_rate, skip_gain, norm_gain),
    )
    at_hand = pl.BlockSpec(memory_space=pltpu.VMEM)
    sizes = dict(heads=heads, per_group=per_group, channels=channels)
    packed_rows = state_rows + 2 * prompt_rows * kv_count

    packed = pl.pallas_call(
        pack_kernel,
        out_shape=jax.ShapeDtypeStruct((devices // NEAR, packed_rows, HD), BF16),
        out_specs=pl.BlockSpec(memory_space=pl.ANY),
        scratch_shapes=[
            pltpu.VMEM((packed_rows, HD), BF16),
            pltpu.SemaphoreType.DMA((devices // NEAR,)),
        ],
        compiler_params=params(),
        name="pack",
    )(prompt_state, prompt_keys, prompt_values)
    packed, near_keys = lax.optimization_barrier((packed, answer_keys))
    near = pl.pallas_call(
        join_kernel,
        out_shape=jax.ShapeDtypeStruct((tokens, 2 * kv_width), BF16),
        out_specs=at_hand,
        compiler_params=params(),
        name="join",
    )(in_hbm(near_keys), in_hbm(answer_values))
    packed, raw = lax.optimization_barrier((packed, step_raw.T))
    lines = [list(range(first, devices, NEAR)) for first in range(NEAR)]
    line = lax.all_to_all(packed, "reader", 0, 0, axis_index_groups=lines, tiled=True)
    prior = shifted(near, "reader", 1)
    raw = in_hbm(raw)

    small = pl.CostEstimate(flops=0, bytes_accessed=0, transcendentals=0)
    wide = pl.BlockSpec((tokens, width), lambda g: (0, g))
    tail, level, column, start = pl.pallas_call(
        functools.partial(tail_kernel, per_group=per_group, channels=channels),
        grid=(groups,),
        in_specs=[
            whole(lengths.shape),
            whole(raw.shape),
            whole((1, heads)),
            wide,
            pl.BlockSpec((tokens, state), lambda g: (0, g)),
        ],
        out_specs=(at_hand, at_hand, at_hand, at_hand),
        out_shape=(
            jax.ShapeDtypeStruct((columns + 2 * heads, state), BF16),
            jax.ShapeDtypeStruct((tokens, 2 * heads), F32),
            jax.ShapeDtypeStruct((heads, tokens), F32),
            jax.ShapeDtypeStruct((tokens, LANES), F32),
        ),
        scratch_shapes=[pltpu.VMEM((tokens, 2 * heads), F32)],
        compiler_params=params(),
        cost_estimate=small,
        name="tail",
    )(lengths, raw, rate, in_hbm(mixer_input), in_hbm(state_write))
    tail = shifted(tail, "reader", 1)
    inner = pl.pallas_call(
        functools.partial(inner_kernel, **sizes),
        grid=(groups,),
        in_specs=[
            at_hand,
            at_hand,
            at_hand,
            whole((1, heads)),
            at_hand,
            at_hand,
            at_hand,
        ],
        out_specs=at_hand,
        out_shape=jax.ShapeDtypeStruct((tokens, columns), BF16),
        compiler_params=params(),
        cost_estimate=small,
        name="inner",
    )(start, level, column, skip, mixer_input, state_write, state_read)
    prior, line, inner = lax.optimization_barrier((prior, line, inner))
    gathered = (line, lax.ppermute(line, "reader", [(i, i ^ 1) for i in range(devices)]))

    group_size = queries.shape[1] // kv_width
    attention_out = pl.pallas_call(
        functools.partial(
            attend_kernel,
            state_rows=state_rows,
            prompt_rows=prompt_rows,
            kv_count=kv_count,
        ),
        grid=(kv_count,),
        in_specs=[at_hand] * 5
        + [at_hand] * NEAR,
        out_specs=pl.BlockSpec((tokens, group_size * HD), lambda k: (0, k)),
        out_shape=jax.ShapeDtypeStruct(queries.shape, BF16),
        scratch_shapes=[pltpu.VMEM((tokens, tokens + LANES), F32)],
        compiler_params=params(),
        cost_estimate=small,
        name="attend",
    )(start, queries, answer_keys, answer_values, prior, *gathered)

    inner, attention_out = lax.optimization_barrier((inner, attention_out))
    mixer_out = pl.pallas_call(
        functools.partial(final_kernel, state_rows=state_rows, **sizes),
        grid=(groups,),
        in_specs=[
            at_hand,
            at_hand,
            pl.BlockSpec((width, state), lambda g: (g, 0)),
            pl.BlockSpec((2 * heads, state), lambda g: (columns // (2 * heads), 0)),
            at_hand,
            at_hand,
            at_hand,
            pl.BlockSpec((1, width), lambda g: (0, g)),
        ]
        + [at_hand] * NEAR,
        out_specs=wide,
        out_shape=jax.ShapeDtypeStruct((tokens, columns), BF16),
        scratch_shapes=[pltpu.VMEM((tokens, width), F32)],
        compiler_params=params(),
        cost_estimate=small,
        name="final",
    )(start, level, tail, tail, state_read, inner, gate_input, gain, *gathered)
    return (mixer_out, attention_out)


def solution(mesh):
    rows = P(("group", "reader"), None)
    in_specs = (P("group"),) + (rows,) * 5 + (P(),) * 3 + (rows,) * 6
    return jax.shard_map(
        local, mesh=mesh, in_specs=in_specs, out_specs=(rows, rows), check_vma=False
    )
```
